32 devices in a mesh: batch: 16 (over z, y, core), blk: 2 (over x).
Axes of the slice: x: 2, y: 2, z: 4, core: 2. Of those that a mesh axis runs over, the one named last changes fastest.
Arguments:
- tokens: bfloat16 [16, 2, 1024, 768], P('batch', None, 'blk'), may hold values from -6 to 6
- cotangent: bfloat16 [16, 2, 1024, 768], P('batch', None, 'blk'), may hold values from -6 to 6
- counts: int32 [16], P('batch'), may hold values from 2 to 3
- perms: int32 [2, 12, 3], replicated, may hold values from 0 to 2, as said below
- key_mask: int32 [16, 2, 1024], P('batch', None, 'blk'), may hold values from 0 to 1, as said below
- w_qkv: bfloat16 [768, 2304], replicated, may hold values from -0.21875 to 0.21875
- bias_q: float32 [768], replicated, may hold values from -3 to 3
- bias_v: float32 [768], replicated, may hold values from -3 to 3
- w_out: bfloat16 [768, 768], replicated, may hold values from -0.875 to 0.875
- bias_out: float32 [768], replicated, may hold values from -3 to 3
- gain_one: float32 [768], replicated, may hold values from 0.5 to 1.5
- shift_one: float32 [768], replicated, may hold values from -3 to 3
- w_in: bfloat16 [768, 3072], replicated, may hold values from -0.21875 to 0.21875
- bias_in: float32 [3072], replicated, may hold values from -3 to 3
- w_back: bfloat16 [3072, 768], replicated, may hold values from -0.109375 to 0.109375
- bias_back: float32 [768], replicated, may hold values from -3 to 3
- gain_two: float32 [768], replicated, may hold values from 0.5 to 1.5
- shift_two: float32 [768], replicated, may hold values from -3 to 3
Outputs:
- mixed_out: bfloat16 [16, 2, 1024, 768], P('batch', None, 'blk')
- tokens_grad: bfloat16 [16, 2, 1024, 768], P('batch', None, 'blk')
- w_qkv_grad: float32 [768, 2304], P('batch')
- bias_q_grad: float32 [768], P('batch')
- bias_v_grad: float32 [768], P('batch')
- w_out_grad: float32 [768, 768], P('batch')
- bias_out_grad: float32 [768], P('batch')
- gain_one_grad: float32 [768], P('batch')
- shift_one_grad: float32 [768], P('batch')
- w_in_grad: float32 [768, 3072], P('batch')
- bias_in_grad: float32 [3072], P('batch')
- w_back_grad: float32 [3072, 768], P('batch')
- bias_back_grad: float32 [768], P('batch')
- gain_two_grad: float32 [768], P('batch')
- shift_two_grad: float32 [768], P('batch')
The draws below stay inside these ranges and needn't reach their ends.
Inputs may be any that keep to these rules, and one draw needn't show every extreme that they name: `perms`: row 0 holds for each head a permutation of 0 and 1 followed by 2; row 1 holds for each head a permutation of 0, 1, 2. `key_mask`: the first token of every block of 512 tokens is 1.
All inputs are finite; a program needn't handle non-finite values.
Results may differ from the reference program's by a relative error of at most 0.014.
Values may be sent and summed in bfloat16 or wider, within the bound.
No kernel may reach another device: no remote copies, remote signals or barrier semaphores. Data moves between devices by JAX's collectives and lax.ppermute only.
A program may use at most 192 MiB of HBM per device.

```python
import jax
import jax.numpy as jnp
from jax import lax

D = 768
HEADS = 12
HEAD_DIM = 64
FF = 3072
BLOCK = 512
SEQS = 16


def draw_perms(key, part):
    key = jax.random.fold_in(key, 11)
    flip_key, order_key = jax.random.split(key)
    flip_bits = jax.random.randint(flip_key, (HEADS,), 0, 2).astype(jnp.int32)
    pair_rows = jnp.stack([flip_bits, 1 - flip_bits, jnp.full((HEADS,), 2, jnp.int32)], axis=1)
    order_keys = jax.random.split(order_key, HEADS)
    triple_rows = jax.vmap(lambda one_key: jax.random.permutation(one_key, 3))(order_keys).astype(jnp.int32)
    return jnp.stack([pair_rows, triple_rows], axis=0).astype(jnp.int32)


def draw_key_mask(key, part):
    key = jax.random.fold_in(key, 23)
    chances = jax.random.randint(key, (SEQS, 2, 2 * BLOCK), 0, 20)
    position = jnp.arange(2 * BLOCK, dtype=jnp.int32) % BLOCK
    return jnp.where((chances < 17) | (position[None, None, :] == 0), 1, 0).astype(jnp.int32)


def set_ends(values, own_key, smallest, high):
    shape = values.shape
    index_at = [jax.random.randint(jax.random.fold_in(own_key, axis), (), 0, shape[axis]) for axis in range(len(shape))]
    values = values.at[tuple(index_at)].set(smallest)
    longest = shape.index(max(shape))
    index_at[longest] = (index_at[longest] + 1) % shape[longest]
    return values.at[tuple(index_at)].set(high)


def levels(own_key, extent, cuts, smallest, largest):
    def one(axis_at, blocks):
        steps = jax.random.uniform(jax.random.fold_in(jax.random.fold_in(own_key, 6), axis_at), (blocks,), jnp.float32, smallest / len(cuts), largest / len(cuts))
        return jnp.repeat(jnp.exp(steps), extent[axis_at] // blocks).reshape((-1,) + (1,) * (len(extent) - axis_at - 1))

    factor_of = one(*cuts[0])
    for cut in cuts[1:]:
        factor_of = factor_of * one(*cut)
    return factor_of


def scatter_about(key, dims, scale, reach, cuts=(), kind=jnp.bfloat16):
    factor_of = levels(key, dims, cuts, -0.22, 0.18) if cuts else 1.0
    drawn = jax.random.normal(key, dims, jnp.float32) * scale * factor_of
    return jnp.minimum(jnp.maximum(drawn, -reach), reach).astype(kind)


def setup_inputs(seed: int = 0) -> dict:
    key_list = jax.random.split(jax.random.key(seed), 19)
    tokens = scatter_about(key_list[0], (SEQS, 2, 2 * BLOCK, D), 1.0, 6.0, ((0, 16), (2, 2)))
    cotangent = scatter_about(key_list[1], (SEQS, 2, 2 * BLOCK, D), 1.0, 6.0, ((0, 16), (2, 2)))
    counts = set_ends(jax.random.randint(key_list[2], (SEQS,), 2, 4), jax.random.fold_in(key_list[2], 1), 2, 3).astype(jnp.int32)
    perms = draw_perms(jax.random.fold_in(key_list[18], 71), 0)
    key_mask = draw_key_mask(jax.random.fold_in(key_list[18], 71), 0)
    w_qkv = scatter_about(key_list[5], (D, 3 * D), D ** -0.5, 0.21875)
    bias_q = scatter_about(key_list[6], (D,), 0.5, 3.0, (), jnp.float32)
    bias_v = scatter_about(key_list[7], (D,), 0.5, 3.0, (), jnp.float32)
    w_out = scatter_about(key_list[8], (D, D), (D // 16) ** -0.5, 0.875)
    bias_out = scatter_about(key_list[9], (D,), 0.5, 3.0, (), jnp.float32)
    gain_one = jnp.clip(1.0 + 0.1 * jax.random.normal(key_list[10], (D,), jnp.float32), 0.5, 1.5)
    shift_one = scatter_about(key_list[11], (D,), 0.5, 3.0, (), jnp.float32)
    w_in = scatter_about(key_list[12], (D, FF), D ** -0.5, 0.21875)
    bias_in = scatter_about(key_list[13], (FF,), 0.5, 3.0, (), jnp.float32)
    w_back = scatter_about(key_list[14], (FF, D), FF ** -0.5, 0.109375)
    bias_back = scatter_about(key_list[15], (D,), 0.5, 3.0, (), jnp.float32)
    gain_two = jnp.clip(1.0 + 0.1 * jax.random.normal(key_list[16], (D,), jnp.float32), 0.5, 1.5)
    shift_two = scatter_about(key_list[17], (D,), 0.5, 3.0, (), jnp.float32)
    return dict(tokens=tokens, cotangent=cotangent, counts=counts, perms=perms, key_mask=key_mask, w_qkv=w_qkv, bias_q=bias_q, bias_v=bias_v, w_out=w_out, bias_out=bias_out, gain_one=gain_one, shift_one=shift_one, w_in=w_in, bias_in=bias_in, w_back=w_back, bias_back=bias_back, gain_two=gain_two, shift_two=shift_two)


@jax.custom_vjp
def low(v):
    return lax.optimization_barrier(v.astype(jnp.bfloat16)).astype(jnp.float32)

@jax.custom_vjp
def low_back(v):
    return v

def low_keep(v):
    return (low(v), None)

def low_pass(kept, grad):
    return (grad,)

def back_keep(v):
    return (v, None)

def back_low(kept, grad):
    return (low(grad),)
low.defvjp(low_keep, low_pass)
low_back.defvjp(back_keep, back_low)
HIGHEST = lax.Precision.HIGHEST
EPSILON = 1e-05

def layer_norm(hidden, norm_gain, norm_shift):
    centre = lax.optimization_barrier(jnp.mean(hidden, axis=-1, keepdims=True))
    centred = hidden - centre
    spread = lax.optimization_barrier(jnp.mean(centred * centred, axis=-1, keepdims=True))
    return centred * lax.rsqrt(spread + EPSILON) * norm_gain + norm_shift

def sources_of(block_count, perms):
    lookup = jnp.where(block_count == 2, perms[0], perms[1])
    extended = jnp.concatenate([lookup, jnp.full((HEADS, 1), 3, jnp.int32)], axis=1)
    blocks = jnp.arange(4, dtype=jnp.int32)
    return jnp.where(blocks[None, :] < block_count, extended, blocks[None, :])

def item_forward(token_rows, params, choose, mask_rows, live_rows):
    w_qkv, bias_q, bias_v, w_out, bias_out, gain_one, shift_one, w_in, bias_in, w_back, bias_back, gain_two, shift_two = params
    projected = low_back(jnp.dot(token_rows, w_qkv, precision=HIGHEST))
    queries = low(projected[:, :D] + bias_q).reshape(4, BLOCK, HEADS, HEAD_DIM)
    keys_all = low(projected[:, D:2 * D]).reshape(4, BLOCK, HEADS, HEAD_DIM)
    values_all = low(projected[:, 2 * D:] + bias_v).reshape(4, BLOCK, HEADS, HEAD_DIM)
    keys_used = jnp.einsum('hjc,cthe->jthe', choose, keys_all, precision=HIGHEST)
    values_used = jnp.einsum('hjc,cthe->jthe', choose, values_all, precision=HIGHEST)
    mask_used = jnp.einsum('hjc,ct->jht', choose, mask_rows, precision=HIGHEST)
    scores = low_back(jnp.einsum('jqhe,jkhe->jhqk', queries, keys_used, precision=HIGHEST) * 0.125)
    scores = jnp.where(mask_used[:, :, None, :] > 0.5, scores, -1e+30)
    probs = low(jax.nn.softmax(scores, axis=-1))
    attended = jnp.einsum('jhqk,jkhe->jqhe', probs, values_used, precision=HIGHEST)
    attended = low(low_back(attended.reshape(4 * BLOCK, D)))
    first_sum = token_rows + low_back(jnp.dot(attended, w_out, precision=HIGHEST)) + bias_out
    normed = layer_norm(first_sum, gain_one, shift_one)
    hidden_pre = low_back(jnp.dot(low(normed), w_in, precision=HIGHEST)) + bias_in
    active = low(jax.nn.gelu(hidden_pre, approximate=False))
    second = normed + low_back(jnp.dot(active, w_back, precision=HIGHEST)) + bias_back
    return layer_norm(second, gain_two, shift_two) * live_rows[:, None]

def reference(tokens, cotangent, counts, perms, key_mask, w_qkv, bias_q, bias_v, w_out, bias_out, gain_one, shift_one, w_in, bias_in, w_back, bias_back, gain_two, shift_two):
    weights = tuple((weight.astype(jnp.float32) for weight in (w_qkv, bias_q, bias_v, w_out, bias_out, gain_one, shift_one, w_in, bias_in, w_back, bias_back, gain_two, shift_two)))

    def one_item(totals, pieces):
        token_item, cot_item, block_count, mask_item = pieces
        token_rows = token_item.astype(jnp.float32).reshape(4 * BLOCK, D)
        sources = sources_of(block_count, perms)
        choose = (sources[:, :, None] == jnp.arange(4, dtype=jnp.int32)[None, None, :]).astype(jnp.float32)
        live_blocks = (jnp.arange(4, dtype=jnp.int32) < block_count).astype(jnp.float32)
        live_rows = jnp.repeat(live_blocks, BLOCK)
        mask_rows = mask_item.reshape(4, BLOCK).astype(jnp.float32)
        result, pullback = jax.vjp(lambda inputs, params: item_forward(inputs, params, choose, mask_rows, live_rows), token_rows, weights)
        row_grads, weight_grads = pullback(cot_item.astype(jnp.float32).reshape(4 * BLOCK, D))
        totals = tuple((older + newer for older, newer in zip(totals, weight_grads)))
        outputs = (result.astype(jnp.bfloat16).reshape(2, 2 * BLOCK, D), row_grads.astype(jnp.bfloat16).reshape(2, 2 * BLOCK, D))
        return (totals, outputs)
    zero_grads = tuple((jnp.zeros_like(weight) for weight in weights))
    totals, stacked = lax.scan(one_item, zero_grads, (tokens, cotangent, counts, key_mask))
    mixed_out, tokens_grad = stacked
    return (mixed_out, tokens_grad, totals[0], totals[1], totals[2], totals[3], totals[4], totals[5], totals[6], totals[7], totals[8], totals[9], totals[10], totals[11], totals[12])
```

```python
import functools
import math

import jax
import jax.numpy as jnp
from jax import lax
from jax.experimental import pallas as pl
from jax.experimental.pallas import tpu as pltpu
from jax.sharding import PartitionSpec as P

EPSILON = 1e-05
BF = jnp.bfloat16
F32 = jnp.float32
VMEM_BYTES = 60 * 1024 * 1024
NEGATIVE = -1e30

SIDE, CORE, LIVE, OWNER, SOURCE = 0, 1, 2, 4, 5


def dot(a, b, ca=1, cb=0):
    return lax.dot_general(a, b, (((ca,), (cb,)), ((), ())), preferred_element_type=F32)


def params(**more):
    return pltpu.CompilerParams(vmem_limit_bytes=VMEM_BYTES, **more)


def cost(flops, read):
    return pl.CostEstimate(flops=int(flops), bytes_accessed=int(read), transcendentals=0)


def once(shape, index):
    return pl.BlockSpec(shape, index, pipeline_mode=pl.Buffered(1))


def mask_columns(mask_row):
    penalty = jnp.where(mask_row == 0, NEGATIVE, 0.0).astype(F32)
    return jnp.broadcast_to(penalty, (128, penalty.shape[1])).T


def project(with_queries, half_rows, meta, tok, mask, w_q, w_k, w_v, vec, *refs):
    q_t, k, k_t, v, v_t, mb = refs[-6:]
    rows = tok[...]
    keys = dot(rows, w_k[...]).astype(BF)
    k[...] = keys
    k_t[...] = keys.T
    values = (dot(rows, w_v[...]) + vec[1:2, :]).astype(BF)
    v[...] = values
    v_t[...] = values.T
    if with_queries:
        if half_rows:
            rows = tok[pl.ds(pl.multiple_of(meta[SIDE] * half_rows, half_rows), half_rows), :]
        queries = (dot(rows, w_q[...]) + vec[0:1, :]).astype(BF)
        q_t[...] = (queries * 0.125).T
    mb[...] = mask_columns(mask[...])


def pad_pair(part, half):
    zeros = jnp.zeros_like(part)
    return jnp.concatenate([part, zeros] if half == 0 else [zeros, part], axis=0)


def units(heads, size, total, meta):
    pair = pl.program_id(0)
    out = []
    for half in range(2):
        for slot, queries in enumerate((slice(0, size), slice(size, total))):
            source = meta[SOURCE + slot * heads + 2 * pair + half]
            out.append((half, slice(64 * half, 64 * half + 64), queries, source))
    return out


def attention_forward(heads, meta, q_t, k, v_t, mb, probs, att, att_t, inv):
    size, total = k.shape[1], q_t.shape[1]
    todo = units(heads, size, total, meta)

    def score(unit):
        half, span, queries, source = unit
        return dot(k[source], pad_pair(q_t[span, queries], half))

    def soften(unit, scores):
        half, span, queries, source = unit
        scores = scores + jnp.concatenate([mb[source]] * (scores.shape[1] // 128), axis=1)
        weights = jnp.exp(scores - jnp.max(scores, axis=0, keepdims=True))
        inverse = 1.0 / jnp.sum(weights, axis=0, keepdims=True)
        low = weights.astype(BF)
        probs[half, :, queries] = low
        inv[0, half : half + 1, queries] = inverse
        return low, inverse

    def attend(unit, soft):
        half, span, queries, source = unit
        att_t[span, queries] = (dot(v_t[source, span, :], soft[0]) * soft[1]).astype(BF)

    scores = {0: score(todo[0])}
    soft = {}
    for at in range(len(todo) + 1):
        if at + 1 < len(todo):
            scores[at + 1] = score(todo[at + 1])
        if at < len(todo):
            soft[at] = soften(todo[at], scores.pop(at))
        if at > 0:
            attend(todo[at - 1], soft.pop(at - 1))
    att[...] = att_t[...].T


def lane_sums(block):
    width = block.shape[1]
    part = block[:, :128]
    for at in range(128, width, 128):
        part = part + block[:, at : at + 128]
    return jnp.sum(part.T, axis=0, keepdims=True)


def attention_backward(
    heads, meta, probs, k_t, v, q_t, do_t, att_t, inv, gq_t, gk_t, gv_t, bq, bv, sum_k, sum_v, sum_q
):
    size, total = v.shape[1], q_t.shape[1]
    todo = units(heads, size, total, meta)
    sum_k[...] = jnp.zeros_like(sum_k)
    sum_v[...] = jnp.zeros_like(sum_v)

    def begin(unit):
        half, span, queries, source = unit
        scaled = do_t[span, queries].astype(F32) * inv[0, half : half + 1, queries]
        delta = jnp.sum(scaled * att_t[span, queries].astype(F32), axis=0, keepdims=True)
        scaled = scaled.astype(BF)
        return scaled, delta, dot(v[source], pad_pair(scaled, half))

    def middle(unit, begun):
        half, span, queries, source = unit
        scaled, delta, grad_probs = begun
        low = probs[half, :, queries]
        sum_v[source, span, :] += dot(scaled, low, 1, 1)
        return (low.astype(F32) * (grad_probs - delta)).astype(BF)

    def end(unit, grad_scores):
        half, span, queries, source = unit
        sum_k[source, span, :] += dot(q_t[span, queries], grad_scores, 1, 1)
        grad_q = dot(k_t[source, span, :], grad_scores) * 0.125
        sum_q[span, queries] = grad_q
        gq_t[span, queries] = grad_q.astype(BF)

    begun = {0: begin(todo[0])}
    grads = {}
    for at in range(len(todo) + 1):
        if at + 1 < len(todo):
            begun[at + 1] = begin(todo[at + 1])
        if at < len(todo):
            grads[at] = middle(todo[at], begun.pop(at))
        if at > 0:
            end(todo[at - 1], grads.pop(at - 1))
    gk_t[...] = sum_k[...].astype(BF)
    gv_t[...] = sum_v[...].astype(BF)
    bq[...] = lane_sums(sum_q[...])
    bv[...] = lane_sums(sum_v[0] + sum_v[1] + sum_v[2])


def normalise(rows):
    centred = rows - jnp.mean(rows, axis=-1, keepdims=True)
    scale = lax.rsqrt(jnp.mean(centred * centred, axis=-1, keepdims=True) + EPSILON)
    return centred * scale, scale


def norm_backward(grad, norm, scale, gain):
    scaled = grad * gain
    mean = jnp.mean(scaled, axis=-1, keepdims=True)
    along = jnp.mean(scaled * norm, axis=-1, keepdims=True)
    return scale * (scaled - mean - norm * along)


def gelu_pair(u):
    t = 1.0 / (1.0 + (0.3275911 * math.sqrt(0.5)) * jnp.abs(u))
    bell = jnp.exp(-0.5 * (u * u))
    poly = 0.5 * 1.061405429
    for factor in (-1.453152027, 1.421413741, -0.284496736, 0.254829592):
        poly = poly * t + 0.5 * factor
    tail = poly * t * bell
    below = jnp.where(u < 0, tail, 1.0 - tail)
    return u * below, below + u * (bell * (1.0 / math.sqrt(2.0 * math.pi)))


B_OUT, GAIN_ONE, SHIFT_ONE, B_BACK, GAIN_TWO, SHIFT_TWO = 2, 3, 4, 5, 6, 7


def tiles_of(total, tile):
    return [slice(at, at + tile) for at in range(0, total, tile)]


def split_cores(meta, block, keep, send, groups, rows):
    mine = meta[CORE]
    for at in range(groups):
        low = block[2 * at * rows : (2 * at + 1) * rows]
        high = block[(2 * at + 1) * rows : (2 * at + 2) * rows]
        keep[at] = jnp.where(mine == 0, low, high).astype(BF)
        send[at] = jnp.where(mine == 0, high, low).astype(BF)


def rows_forward(
    steps, meta, tok, tok_half, att, cot, cot_half, w_out, vec, w_in, b_in, w_back,
    slope, keep, send, sums, first_out, normed_out, mixed_out, second_out, back_out,
    first, normed_low, mixed, second, back_low, active, sems,
):
    step = pl.program_id(0)
    total = att.shape[0]
    tile = tok_half.shape[0]
    chunk = w_in.shape[1]
    tiles = tiles_of(total, tile)
    copies = [
        pltpu.make_async_copy(source, target, sems.at[at])
        for at, (source, target) in enumerate(
            ((first, first_out), (normed_low, normed_out), (mixed, mixed_out), (second, second_out), (back_low, back_out))
        )
    ]

    @pl.when(step == 0)
    def _():
        for at, span in enumerate(tiles):
            rows = (tok[span, :] if at + 1 < len(tiles) else tok_half[...]).astype(F32)
            rows = rows + dot(att[span, :], w_out[...]) + vec[B_OUT : B_OUT + 1, :]
            first[span, :] = rows
            result = normalise(rows)[0] * vec[GAIN_ONE : GAIN_ONE + 1, :] + vec[SHIFT_ONE : SHIFT_ONE + 1, :]
            normed_low[span, :] = result.astype(BF)
            second[span, :] = result + vec[B_BACK : B_BACK + 1, :]
        copies[0].start()
        copies[1].start()

    @pl.when(step < steps)
    def _():
        hidden = dot(normed_low[...], w_in[...]) + b_in[...]
        value, grad = gelu_pair(hidden)
        value = value.astype(BF)
        active[:, pl.ds(pl.multiple_of(step * chunk, chunk), chunk)] = value
        slope[...] = grad.astype(BF)
        second[...] += dot(value, w_back[...])

    @pl.when(step == steps - 1)
    def _():
        sums[...] = jnp.zeros_like(sums)
        gain, shift = vec[GAIN_TWO : GAIN_TWO + 1, :], vec[SHIFT_TWO : SHIFT_TWO + 1, :]
        for at, span in enumerate(tiles):
            last = at + 1 == len(tiles)
            live = meta[LIVE + last].astype(F32)
            norm, scale = normalise(second[span, :])
            mixed[span, :] = ((norm * gain + shift) * live).astype(BF)
            grad = (cot_half[...] if last else cot[span, :]).astype(F32) * live
            sums[0:1, :] += jnp.sum(grad * norm, axis=0, keepdims=True)
            sums[1:2, :] += jnp.sum(grad, axis=0, keepdims=True)
            grad = norm_backward(grad, norm, scale, gain)
            sums[2:3, :] += jnp.sum(grad, axis=0, keepdims=True)
            second[span, :] = grad
            back_low[span, :] = grad.astype(BF)
        for copy in copies[2:]:
            copy.start()

    @pl.when(step >= steps)
    def _():
        rows = keep.shape[1]
        columns = 2 * rows * keep.shape[0]
        part = active[:, pl.ds(pl.multiple_of((step - steps) * columns, columns), columns)]
        split_cores(meta, dot(part, back_low[...], 0, 0), keep, send, keep.shape[0], rows)

    @pl.when(step == pl.num_programs(0) - 1)
    def _():
        for copy in copies:
            copy.wait()


def rows_backward(
    meta, back_low, normed_low, slope, w_in, w_back, w_out, vec, first_in, second_in,
    keep, send, g_first, first_low, do_t, b_in, sums, first, g_normed, g_second, sems,
):
    step = pl.program_id(0)
    total = back_low.shape[0]
    tiles = tiles_of(total, total // 3)
    copies = [
        pltpu.make_async_copy(first_in, first, sems.at[0]),
        pltpu.make_async_copy(second_in, g_second, sems.at[1]),
    ]

    @pl.when(step == 0)
    def _():
        for copy in copies:
            copy.start()
        g_normed[...] = jnp.zeros_like(g_normed)

    grad = dot(back_low[...], w_back[...], 1, 1) * slope[...].astype(F32)
    b_in[...] = jnp.sum(grad, axis=0, keepdims=True)
    low = grad.astype(BF)
    g_normed[...] += dot(low, w_in[...], 1, 1)
    split_cores(meta, dot(normed_low[...], low, 0, 0), keep, send, keep.shape[0], keep.shape[1])

    @pl.when(step == pl.num_programs(0) - 1)
    def _():
        for copy in copies:
            copy.wait()
        sums[...] = jnp.zeros_like(sums)
        for span in tiles:
            norm, scale = normalise(first[span, :])
            grad = g_normed[span, :] + g_second[span, :]
            sums[0:1, :] += jnp.sum(grad * norm, axis=0, keepdims=True)
            sums[1:2, :] += jnp.sum(grad, axis=0, keepdims=True)
            grad = norm_backward(grad, norm, scale, vec[GAIN_ONE : GAIN_ONE + 1, :])
            sums[2:3, :] += jnp.sum(grad, axis=0, keepdims=True)
            g_first[span, :] = grad
            first_low[span, :] = grad.astype(BF)
        do_t[...] = dot(w_out[...], first_low[...], 1, 1).astype(BF)


def weight_gradients(per, meta, tok, tok_two, tok_two_half, tok_other, gq_t, gk_t, gv_t, att_t, first_low, rows, keep, send):
    step = pl.program_id(0)
    size = tok.shape[0]
    cut = keep.shape[2]

    def finish(block):
        split_cores(meta, block, keep, send, keep.shape[0], keep.shape[1])

    @pl.when(step < per)
    def _():
        finish(dot(tok[...], gq_t[:, :size], 0, 1) + dot(tok_two_half[...], gq_t[:, size:], 0, 1))

    for which, ref in ((1, gk_t), (2, gv_t)):

        @pl.when((step >= which * per) & (step < (which + 1) * per))
        def _():
            finish(
                dot(tok[...], ref[0], 0, 1) + dot(tok_two[...], ref[1], 0, 1) + dot(tok_other[...], ref[2], 0, 1)
            )

    @pl.when((step >= 3 * per) & (step < 4 * per))
    def _():
        finish(dot(att_t[...], first_low[...]))

    @pl.when(step == 4 * per)
    def _():
        vectors = rows[...]
        vectors = jnp.concatenate([vectors, jnp.zeros((cut - vectors.shape[0], vectors.shape[1]), F32)], axis=0)
        finish(vectors.T)


def tokens_sent(meta, w, gq_t, gk_t, gv_t, g_half, other, two, two_low):
    width = w.shape[0]
    half_rows = g_half.shape[0]
    total = dot(w[:, width : 2 * width], gk_t[1]) + dot(w[:, 2 * width :], gv_t[1])
    other[...] = total.T.astype(BF)
    total = dot(w[:, width : 2 * width], gk_t[0]) + dot(w[:, 2 * width :], gv_t[0])
    two[...] = total.T
    span = pl.ds(pl.multiple_of(meta[SIDE] * half_rows, half_rows), half_rows)
    two[span, :] += dot(w[:, :width], gq_t[...]).T + g_half[...]
    two_low[...] = two[...].astype(BF)


def tokens_kept(meta, w, gq_t, gk_t, gv_t, g_first, out):
    width = w.shape[0]
    total = dot(w[:, :width], gq_t[...]) + dot(w[:, width : 2 * width], gk_t[...]) + dot(w[:, 2 * width :], gv_t[...])
    out[...] = total.T + g_first[...]


def flip(value, axis, bit):
    count = lax.axis_size(axis)
    return lax.ppermute(value, axis, [(at, at ^ bit) for at in range(count)])


def after(value, *others):
    return lax.optimization_barrier((value,) + others)[0]


def add_halves(parts, meta, *refs):
    ins, outs = refs[: 4 * parts], refs[4 * parts :]
    for at in range(parts):
        kept, came, kept_other, came_other = ins[4 * at : 4 * at + 4]
        outs[2 * at][...] = (kept[...].astype(F32) + came[...].astype(F32)).astype(BF)
        outs[2 * at + 1][...] = (kept_other[...].astype(F32) + came_other[...].astype(F32)).astype(BF)


def combine(meta, arrays, splits):
    in_specs, operands, out_specs, shapes = [], [], [], []
    for (kept, came), (start, columns, bit, place) in zip(arrays, splits):
        count, rows, _ = kept.shape
        block = start // columns

        def index(flipped, i, m, bit=bit, place=place, block=block):
            mine = (m[OWNER] >> bit) & 1
            mine = 1 - mine if flipped else mine
            return ((((i >> place) << 1) | mine) << place) | (i & ((1 << place) - 1)), 0, block

        for flipped in (False, True):
            for array in (kept, came):
                in_specs.append(pl.BlockSpec((1, rows, columns), functools.partial(index, flipped)))
                operands.append(array)
        out_specs += [pl.BlockSpec((1, rows, columns), lambda i, m: (i, 0, 0))] * 2
        shapes += [jax.ShapeDtypeStruct((count // 2, rows, columns), BF)] * 2
    steps = arrays[0][0].shape[0] // 2
    out = pl.pallas_call(
        functools.partial(add_halves, len(splits)),
        grid_spec=pltpu.PrefetchScalarGridSpec(
            num_scalar_prefetch=1, grid=(steps,), in_specs=in_specs, out_specs=out_specs
        ),
        out_shape=shapes,
        compiler_params=params(),
        cost_estimate=cost(1e6, 3 * sum(2 * s.size for s in shapes)),
        name="combine",
    )(meta, *operands)
    return [(out[2 * at], out[2 * at + 1]) for at in range(len(splits))]


class Piece:
    def __init__(self, meta, keep, send, orders):
        self.meta, self.keep, self.orders = meta, keep, orders
        self.came = flip(send, "batch", 1)
        self.done = 0
        self.left = [sorted(order) for order in orders]

    def hop(self):
        if self.done == 0:
            columns = self.keep.shape[2] // len(self.orders)
            arrays = [(self.keep, self.came)] * len(self.orders)
            starts = [columns * at for at in range(len(self.orders))]
        else:
            arrays = list(zip(self.keep, self.came))
            columns = arrays[0][0].shape[2]
            starts = [0] * len(self.orders)
        if self.done < len(self.orders[0]):
            bits = [order[self.done] for order in self.orders]
            splits = [
                (start, columns, bit, left.index(bit)) for start, bit, left in zip(starts, bits, self.left)
            ]
            out = combine(self.meta, arrays, splits)
            self.keep = [kept for kept, _ in out]
            self.came = [flip(sent, "batch", 1 << bit) for (_, sent), bit in zip(out, bits)]
            for bit, left in zip(bits, self.left):
                left.remove(bit)
        elif self.done == len(self.orders[0]):
            self.keep = [
                (kept[0].astype(F32) + came[0].astype(F32)).astype(BF) for kept, came in arrays
            ]
            self.came = [flip(kept, "blk", 1) for kept in self.keep]
        self.done += 1
        return tuple(self.keep)

    def finish(self):
        while self.done <= len(self.orders[0]):
            self.hop()
        return [kept.astype(F32) + came.astype(F32) for kept, came in zip(self.keep, self.came)]


def local(
    tokens, cotangent, counts, perms, key_mask, w_qkv, bias_q, bias_v, w_out, bias_out, gain_one, shift_one,
    w_in, bias_in, w_back, bias_back, gain_two, shift_two,
):
    _, _, size, width = tokens.shape
    heads = perms.shape[1]
    pairs = heads // 2
    hidden = w_in.shape[1]
    half_rows = size // 2
    total = size + half_rows
    owners = lax.axis_size("batch")
    side = lax.axis_index("blk").astype(jnp.int32)
    owner = lax.axis_index("batch").astype(jnp.int32)
    whole = lambda *shape: once(shape, lambda *_: (0,) * len(shape))
    sds = jax.ShapeDtypeStruct
    anywhere = pl.BlockSpec(memory_space=pl.ANY)

    other_first = flip(tokens[0, 0], "blk", 1)
    other_mask = flip(key_mask[0], "blk", 1)
    came_two = lax.ppermute(tokens[0, 1], "blk", [(0, 1)])
    came_cot = lax.ppermute(cotangent[0, 1, half_rows:], "blk", [(0, 1)])

    count = counts[0]
    lookup = jnp.where(count == 2, perms[0], perms[1])
    own = jnp.where(side == 0, lookup[:, 0], lookup[:, 1])
    two = jnp.where(count > 2, lookup[:, 2], 2)
    source = jnp.concatenate([own, two])
    place = jnp.where(source == 2, 1, jnp.where(source == side, 0, 2))
    live = jnp.stack([(side < count).astype(jnp.int32), (count > 2).astype(jnp.int32)])
    meta = jnp.concatenate([jnp.stack([side, owner & 1]), live, owner[None], place])
    vec = jnp.stack([bias_q, bias_v, bias_out, gain_one, shift_one, bias_back, gain_two, shift_two])
    own_mask = key_mask[0]
    masks = jnp.stack([own_mask[0], jnp.where(side == 0, own_mask[1], other_mask[1]), other_mask[0]])[:, None]

    def grid_spec(grid, in_specs, out_specs, scratch=()):
        return pltpu.PrefetchScalarGridSpec(
            num_scalar_prefetch=1, grid=grid, in_specs=in_specs, out_specs=out_specs, scratch_shapes=list(scratch)
        )

    cut = 256
    per = width // cut
    kv_shapes = [
        sds((width, total), BF), sds((3, size, width), BF), sds((3, width, size), BF), sds((3, size, width), BF),
        sds((3, width, size), BF), sds((3, size, 128), F32),
    ]

    def run_projection(position, rows, mask, before):
        w_at = lambda base: pl.BlockSpec((width, cut), lambda g, m: (0, base * per + g))
        wide = pl.BlockSpec((None, size, cut), lambda g, m: (position, 0, g))
        tall = pl.BlockSpec((None, cut, size), lambda g, m: (position, g, 0))
        queries = (
            pl.BlockSpec((cut, half_rows), lambda g, m: (g, size // half_rows))
            if position == 1
            else pl.BlockSpec((cut, size), lambda g, m: (g, 0))
        )
        return pl.pallas_call(
            functools.partial(project, position != 2, half_rows if position == 1 else 0),
            grid_spec=grid_spec(
                (per,),
                [
                    whole(size, width),
                    pl.BlockSpec((None, 1, size), lambda g, m: (position, 0, 0)),
                    w_at(0), w_at(1), w_at(2),
                    pl.BlockSpec((8, cut), lambda g, m: (0, g)),
                ]
                + [anywhere] * len(before),
                [
                    anywhere if position == 2 else queries, wide, tall, wide, tall,
                    pl.BlockSpec((None, size, 128), lambda g, m: (position, 0, 0)),
                ],
            ),
            out_shape=kv_shapes,
            input_output_aliases={7 + n: n for n in range(len(before))},
            compiler_params=params(),
            cost_estimate=cost(2 * size * width * 2 * width, 10e6),
            name=f"project_{position}",
        )(meta, rows, mask, w_qkv, w_qkv, w_qkv, vec, *before)

    state = run_projection(0, tokens[0, 0], masks, [])
    state = run_projection(2, other_first, masks, state)
    tok_two = jnp.where(side == 0, tokens[0, 1], came_two)
    q_t, k, k_t, v, v_t, mb = run_projection(1, tok_two, masks, state)

    pair_q = pl.BlockSpec((128, total), lambda p, m: (p, 0))
    pair_rows = pl.BlockSpec((3, size, 128), lambda p, m: (0, 0, p))
    pair_cols = pl.BlockSpec((3, 128, size), lambda p, m: (0, p, 0))
    pair_probs = pl.BlockSpec((2, size, total), lambda p, m: (p, 0, 0))
    pair_inv = pl.BlockSpec((1, 2, total), lambda p, m: (p, 0, 0))
    probs, att, att_t, inv = pl.pallas_call(
        functools.partial(attention_forward, heads),
        grid_spec=grid_spec(
            (pairs,),
            [pair_q, pair_rows, pair_cols, whole(3, size, 128)],
            [pair_probs, pl.BlockSpec((total, 128), lambda p, m: (0, p)), pair_q, pair_inv],
        ),
        out_shape=[
            sds((heads, size, total), BF), sds((total, width), BF), sds((width, total), BF),
            sds((pairs, 2, total), F32),
        ],
        compiler_params=params(),
        cost_estimate=cost(8e9, 20e6),
        name="attention_forward",
    )(meta, q_t, k, v_t, mb)

    chunk = 512
    steps = hidden // chunk
    half = owners // 2
    back_rows = hidden // owners
    per_step = max(1, 192 // back_rows)
    flat = lambda dtype, columns=width: sds((total, columns), dtype)
    all_rows = whole(total, width)
    vectors = whole(8, width)
    side_rows = once((half_rows, width), lambda i, m: (m[SIDE], 0))
    early = lambda i: jnp.minimum(i, steps - 1)
    back_half = pl.BlockSpec((per_step, back_rows, width), lambda i, m: (jnp.maximum(i - steps, 0), 0, 0))
    cot_half = jnp.where(side == 0, cotangent[0, 1, :half_rows], came_cot)
    slope, back_keep, back_send, sums_two, first, normed_low, mixed, g_second, back_low = pl.pallas_call(
        functools.partial(rows_forward, steps),
        grid_spec=grid_spec(
            (steps + half // per_step,),
            [
                whole(size, width), side_rows, all_rows, whole(size, width), whole(half_rows, width),
                whole(width, width), vectors,
                pl.BlockSpec((width, chunk), lambda i, m: (0, early(i))),
                pl.BlockSpec((1, chunk), lambda i, m: (0, early(i))),
                pl.BlockSpec((chunk, width), lambda i, m: (early(i), 0)),
            ],
            [
                pl.BlockSpec((total, chunk), lambda i, m: (0, early(i))), back_half, back_half, whole(8, width),
            ] + [anywhere] * 5,
            [
                pltpu.VMEM((total, width), F32), pltpu.VMEM((total, width), BF), pltpu.VMEM((total, width), BF),
                pltpu.VMEM((total, width), F32), pltpu.VMEM((total, width), BF), pltpu.VMEM((total, hidden), BF),
                pltpu.SemaphoreType.DMA((5,)),
            ],
        ),
        out_shape=[
            flat(BF, hidden), sds((half, back_rows, width), BF), sds((half, back_rows, width), BF),
            sds((8, width), F32), flat(F32), flat(BF), flat(BF), flat(F32), flat(BF),
        ],
        compiler_params=params(),
        cost_estimate=cost(2 * total * width * (3 * hidden + width), 40e6),
        name="rows_forward",
    )(
        meta, tokens[0, 0], tok_two, att, cotangent[0, 0], cot_half, w_out, vec, w_in, bias_in.reshape(1, hidden),
        w_back,
    )

    bits = owners.bit_length() - 1
    turn = lambda first_bit: [1 + (first_bit + at) % (bits - 1) for at in range(bits - 1)]
    one_way = turn(0)
    other_way = [one_way[1], one_way[0]] + one_way[2:] if bits > 2 else one_way
    ways = [one_way, other_way]
    back = Piece(meta, back_keep, back_send, ways)
    mixed_came = lax.ppermute(mixed[size:], "blk", [(1, 0)])

    own_rows = width // owners
    in_half = lambda c: pl.BlockSpec((half, own_rows, c), lambda i, m: (0, 0, i))
    in_keep, in_send, g_first, first_low, do_t, g_b_in, sums_one = pl.pallas_call(
        rows_backward,
        grid_spec=grid_spec(
            (steps,),
            [
                all_rows, all_rows, pl.BlockSpec((total, chunk), lambda i, m: (0, i)),
                pl.BlockSpec((width, chunk), lambda i, m: (0, i)), pl.BlockSpec((chunk, width), lambda i, m: (i, 0)),
                whole(width, width), vectors, anywhere, anywhere,
            ],
            [
                in_half(chunk), in_half(chunk), all_rows, all_rows, whole(width, total),
                pl.BlockSpec((1, chunk), lambda i, m: (0, i)), whole(8, width),
            ],
            [
                pltpu.VMEM((total, width), F32), pltpu.VMEM((total, width), F32), pltpu.VMEM((total, width), F32),
                pltpu.SemaphoreType.DMA((2,)),
            ],
        ),
        out_shape=[
            sds((half, own_rows, hidden), BF), sds((half, own_rows, hidden), BF), flat(F32), flat(BF),
            sds((width, total), BF), sds((1, hidden), F32), sds((8, width), F32),
        ],
        compiler_params=params(),
        cost_estimate=cost(2 * total * width * (3 * hidden + width), 40e6),
        name="rows_backward",
    )(meta, back_low, normed_low, slope, w_in, w_back, w_out, vec, first, g_second)
    inner = Piece(meta, in_keep, in_send, ways)
    do_t = after(do_t, *back.hop())

    gq_t, gk_t, gv_t, g_bq, g_bv = pl.pallas_call(
        functools.partial(attention_backward, heads),
        grid_spec=grid_spec(
            (pairs,),
            [pair_probs, pair_cols, pair_rows, pair_q, pair_q, pair_q, pair_inv],
            [pair_q, pair_cols, pair_cols] + [pl.BlockSpec((1, 128), lambda p, m: (0, p))] * 2,
            [pltpu.VMEM((3, 128, size), F32), pltpu.VMEM((3, 128, size), F32), pltpu.VMEM((128, total), F32)],
        ),
        out_shape=[
            sds((width, total), BF), sds((3, width, size), BF), sds((3, width, size), BF), sds((1, width), F32),
            sds((1, width), F32),
        ],
        compiler_params=params(),
        cost_estimate=cost(14e9, 30e6),
        name="attention_backward",
    )(meta, probs, k_t, v, q_t, do_t, att_t, inv)
    gq_t = after(gq_t, *inner.hop())

    within = lambda base: (lambda i: jnp.clip(i - base * per, 0, per - 1))
    rows = jnp.concatenate(
        [sums_two[:3], sums_one[:3], g_bq, g_bv, g_b_in.reshape(width, -1).T, jnp.zeros((4, width), F32)], axis=0
    )
    at = lambda base: pl.BlockSpec((3, cut, size), lambda i, m: (0, within(base)(i), 0))
    qkv_keep, qkv_send = pl.pallas_call(
        functools.partial(weight_gradients, per),
        grid_spec=grid_spec(
            (4 * per + 1,),
            [
                whole(size, width), whole(size, width), side_rows, whole(size, width),
                pl.BlockSpec((cut, total), lambda i, m: (within(0)(i), 0)), at(1), at(2), whole(width, total),
                pl.BlockSpec((total, cut), lambda i, m: (0, within(3)(i))), whole(16, width),
            ],
            [in_half(cut), in_half(cut)],
        ),
        out_shape=[sds((half, own_rows, 4 * width + cut), BF)] * 2,
        compiler_params=params(),
        cost_estimate=cost(2 * size * width * width * 10, 25e6),
        name="weight_gradients",
    )(meta, tokens[0, 0], tok_two, tok_two, other_first, gq_t, gk_t, gv_t, att_t, first_low, rows)
    last = Piece(meta, qkv_keep, qkv_send, ways)
    gq_t = after(gq_t, qkv_keep, *back.hop())

    sent_shapes = [sds((size, width), BF), sds((size, width), F32), sds((size, width), BF)]
    last_two = lambda i, m: (0, 0, 0)
    sent_other, two_own, two_sent = pl.pallas_call(
        tokens_sent,
        grid_spec=grid_spec(
            (1,),
            [
                whole(width, 3 * width),
                pl.BlockSpec((width, half_rows), lambda i, m: (0, size // half_rows)),
                pl.BlockSpec((pl.Element(2), pl.Element(width), pl.Element(size)), lambda i, m: (1, 0, 0)),
                pl.BlockSpec((pl.Element(2), pl.Element(width), pl.Element(size)), lambda i, m: (1, 0, 0)),
                pl.BlockSpec((half_rows, width), lambda i, m: (size // half_rows, 0)),
            ],
            [whole(size, width)] * 3,
        ),
        out_shape=sent_shapes,
        compiler_params=params(),
        cost_estimate=cost(2 * size * width * width * 5, 12e6),
        name="tokens_sent",
    )(meta, w_qkv, gq_t, gk_t, gv_t, g_first)
    came_own = flip(sent_other, "blk", 1)
    came_two_grad = lax.ppermute(two_sent, "blk", [(1, 0)])
    own_grad = pl.pallas_call(
        tokens_kept,
        grid_spec=grid_spec(
            (1,),
            [
                whole(width, 3 * width), whole(width, size),
                pl.BlockSpec((None, width, size), lambda i, m: (0, 0, 0)),
                pl.BlockSpec((None, width, size), lambda i, m: (0, 0, 0)),
                whole(size, width),
            ],
            whole(size, width),
        ),
        out_shape=sds((size, width), F32),
        compiler_params=params(),
        cost_estimate=cost(2 * size * width * width * 3, 12e6),
        name="tokens_kept",
    )(meta, w_qkv, after(gq_t, *last.hop()), gk_t, gv_t, g_first)

    inner.hop()
    back.hop()
    last.hop()
    out_back = jnp.concatenate(back.finish(), axis=1)
    out_in = jnp.concatenate(inner.finish(), axis=1)
    out_last = jnp.concatenate(last.finish(), axis=1)

    tokens_grad = jnp.stack(
        [own_grad + came_own.astype(F32), jnp.where(side == 0, two_own + came_two_grad.astype(F32), 0.0)]
    ).astype(BF)[None]
    mixed_two = jnp.where(side == 0, jnp.concatenate([mixed[size:], mixed_came]), 0.0)
    mixed_all = jnp.stack([mixed[:size], mixed_two.astype(BF)])[None]
    pick = lambda at: out_last[:, 4 * width + at]
    return (
        mixed_all, tokens_grad,
        out_last[:, : 3 * width], pick(6), pick(7), out_last[:, 3 * width : 4 * width], pick(5), pick(3), pick(4),
        out_in, out_last[:, 4 * width + 8 : 4 * width + 8 + hidden // width].reshape(-1), out_back, pick(2), pick(0),
        pick(1),
    )


def solution(mesh):
    split = P("batch", None, "blk", None)
    in_specs = (split, split, P("batch"), P(), P("batch", None, "blk")) + (P(),) * 13
    matrix, vector = P("batch", None), P("batch")
    out_specs = (
        split, split, matrix, vector, vector, matrix, vector, vector, vector, matrix, vector, matrix, vector, vector,
        vector,
    )
    return jax.shard_map(local, mesh=mesh, in_specs=in_specs, out_specs=out_specs, check_vma=False)
```

```python
import functools
import math

import jax
import jax.numpy as jnp
from jax import lax
from jax.experimental import pallas as pl
from jax.experimental.pallas import tpu as pltpu
from jax.sharding import PartitionSpec as P

EPSILON = 1e-05
BF = jnp.bfloat16
F32 = jnp.float32
MIB = 1024 * 1024
NEGATIVE = -1e30

SIDE, CORE, LIVE, OWNER, SOURCE = 0, 1, 2, 4, 5


def dot(a, b, ca=1, cb=0):
    return lax.dot_general(a, b, (((ca,), (cb,)), ((), ())), preferred_element_type=F32)


def params(mebibytes):
    return pltpu.CompilerParams(vmem_limit_bytes=mebibytes * MIB)


def cost(flops, read):
    return pl.CostEstimate(flops=int(flops), bytes_accessed=int(read), transcendentals=0)


def once(shape, index):
    return pl.BlockSpec(shape, index, pipeline_mode=pl.Buffered(1))


def mask_columns(mask_row):
    penalty = jnp.where(mask_row == 0, NEGATIVE, 0.0).astype(F32)
    return jnp.broadcast_to(penalty, (128, penalty.shape[1])).T


def project_own(meta, tok, mask, w, vec, q_t, k, v_t, mb):
    step = pl.program_id(0)
    rows = tok[...]

    @pl.when(step == 0)
    def _():
        queries = (dot(rows, w[...]) + vec[0:1, :]).astype(BF)
        q_t[...] = (queries * 0.125).T
        mb[...] = mask_columns(mask[...])

    @pl.when(step == 1)
    def _():
        k[...] = dot(rows, w[...]).astype(BF)

    @pl.when(step == 2)
    def _():
        v_t[...] = (dot(rows, w[...]) + vec[1:2, :]).astype(BF).T


def pad_pair(part, half):
    zeros = jnp.zeros_like(part)
    return jnp.concatenate([part, zeros] if half == 0 else [zeros, part], axis=0)


def units(heads, size, total, meta):
    pair = pl.program_id(0)
    out = []
    for half in range(2):
        for slot, queries in enumerate((slice(0, size), slice(size, total))):
            source = meta[SOURCE + slot * heads + 2 * pair + half]
            out.append((half, slice(64 * half, 64 * half + 64), queries, source))
    return out


def project_others(meta, vec, masks, starts, ins, k, v_t, q_t, mb, w, two, came):
    size, width = two.shape
    half_rows = size // 2
    own_two, partner_two = starts
    later = ins
    for copy in later:
        copy.start()

    @pl.when(meta[SIDE] == 0)
    def _():
        own_two.start()

    @pl.when(meta[SIDE] == 1)
    def _():
        partner_two.start()

    mb[1] = mask_columns(masks[0:1, :])
    mb[2] = mask_columns(masks[1:2, :])
    own_two.wait()
    later[0].wait()
    k[1] = dot(two[...], w[:, width : 2 * width]).astype(BF)
    later[1].wait()
    k[2] = dot(came[...], w[:, width : 2 * width]).astype(BF)
    later[2].wait()
    v_t[1] = (dot(two[...], w[:, 2 * width :]) + vec[1:2, :]).astype(BF).T
    v_t[2] = (dot(came[...], w[:, 2 * width :]) + vec[1:2, :]).astype(BF).T
    later[3].wait()
    rows = two[pl.ds(pl.multiple_of(meta[SIDE] * half_rows, half_rows), half_rows), :]
    q_t[:, size:] = ((dot(rows, w[:, :width]) + vec[0:1, :]).astype(BF) * 0.125).T
    for copy in later[4:]:
        copy.wait()


def attention_forward(
    heads, meta, masks, vec, tok_in, came_in, w_in, q_own, k_own, v_own, mb_own,
    probs, att, att_t, inv, q_out, k_out, v_out, two_out,
    q_t, k, v_t, mb, w, two, came, sems, out_sems,
):
    size, total = k.shape[1], q_t.shape[1]
    width = k.shape[2]
    step = pl.program_id(0)
    copy = pltpu.make_async_copy
    outs = [
        copy(source, target, out_sems.at[at])
        for at, (source, target) in enumerate(((q_t, q_out), (k, k_out), (v_t, v_out), (two, two_out)))
    ]

    @pl.when(step == 0)
    def _():
        columns = [slice(width, 2 * width), slice(2 * width, 3 * width), slice(0, width)]
        starts = [copy(tok_in.at[1], two, sems.at[0]), copy(came_in.at[1], two, sems.at[0])]
        ins = [
            copy(w_in.at[:, columns[0]], w.at[:, columns[0]], sems.at[1]),
            copy(came_in.at[0], came, sems.at[2]),
            copy(w_in.at[:, columns[1]], w.at[:, columns[1]], sems.at[3]),
            copy(w_in.at[:, columns[2]], w.at[:, columns[2]], sems.at[4]),
            copy(q_own, q_t.at[:, pl.ds(0, size)], sems.at[5]),
            copy(k_own, k.at[0], sems.at[6]),
            copy(v_own, v_t.at[0], sems.at[7]),
            copy(mb_own, mb.at[0], sems.at[8]),
        ]
        project_others(meta, vec, masks, starts, ins, k, v_t, q_t, mb, w, two, came)
        for out in outs:
            out.start()

    todo = units(heads, size, total, meta)
    lanes = pl.ds(pl.multiple_of(step * 128, 128), 128)

    def rows_of(span):
        return pl.ds(pl.multiple_of(step * 128 + span.start, 64), 64)

    def score(unit):
        half, span, queries, source = unit
        return dot(k[source, :, lanes], pad_pair(q_t[rows_of(span), queries], half))

    def soften(unit, scores):
        half, span, queries, source = unit
        scores = scores + jnp.concatenate([mb[source]] * (scores.shape[1] // 128), axis=1)
        weights = jnp.exp(scores - jnp.max(scores, axis=0, keepdims=True))
        inverse = 1.0 / jnp.sum(weights, axis=0, keepdims=True)
        low = weights.astype(BF)
        probs[half, :, queries] = low
        inv[0, half : half + 1, queries] = inverse
        return low, inverse

    def attend(unit, soft):
        half, span, queries, source = unit
        att_t[span, queries] = (dot(v_t[source, rows_of(span), :], soft[0]) * soft[1]).astype(BF)

    scores = {0: score(todo[0])}
    soft = {}
    for at in range(len(todo) + 1):
        if at + 1 < len(todo):
            scores[at + 1] = score(todo[at + 1])
        if at < len(todo):
            soft[at] = soften(todo[at], scores.pop(at))
        if at > 0:
            attend(todo[at - 1], soft.pop(at - 1))
    att[...] = att_t[...].T

    @pl.when(step == pl.num_programs(0) - 1)
    def _():
        for out in outs:
            out.wait()


def lane_sums(block):
    width = block.shape[1]
    part = block[:, :128]
    for at in range(128, width, 128):
        part = part + block[:, at : at + 128]
    return jnp.sum(part.T, axis=0, keepdims=True)


def attention_backward(
    heads, meta, probs, k, v_t, q_t, do_t, att_t, inv, gq_t, gkv_t, bq, bv, sum_k, sum_v, sum_q, k_t, v
):
    size, total = k.shape[1], q_t.shape[1]
    for at in range(3):
        k_t[at] = k[at].T
        v[at] = v_t[at].T
    todo = units(heads, size, total, meta)
    sum_k[...] = jnp.zeros_like(sum_k)
    sum_v[...] = jnp.zeros_like(sum_v)

    def begin(unit):
        half, span, queries, source = unit
        scaled = do_t[span, queries].astype(F32) * inv[0, half : half + 1, queries]
        delta = jnp.sum(scaled * att_t[span, queries].astype(F32), axis=0, keepdims=True)
        scaled = scaled.astype(BF)
        return scaled, delta, dot(v[source], pad_pair(scaled, half))

    def middle(unit, begun):
        half, span, queries, source = unit
        scaled, delta, grad_probs = begun
        low = probs[half, :, queries]
        sum_v[source, span, :] += dot(scaled, low, 1, 1)
        return (low.astype(F32) * (grad_probs - delta)).astype(BF)

    def end(unit, grad_scores):
        half, span, queries, source = unit
        sum_k[source, span, :] += dot(q_t[span, queries], grad_scores, 1, 1)
        grad_q = dot(k_t[source, span, :], grad_scores) * 0.125
        sum_q[span, queries] = grad_q
        gq_t[span, queries] = grad_q.astype(BF)

    begun = {0: begin(todo[0])}
    grads = {}
    for at in range(len(todo) + 1):
        if at + 1 < len(todo):
            begun[at + 1] = begin(todo[at + 1])
        if at < len(todo):
            grads[at] = middle(todo[at], begun.pop(at))
        if at > 0:
            end(todo[at - 1], grads.pop(at - 1))
    gkv_t[:, 0] = sum_k[...].astype(BF)
    gkv_t[:, 1] = sum_v[...].astype(BF)
    bq[...] = lane_sums(sum_q[...])
    bv[...] = lane_sums(sum_v[0] + sum_v[1] + sum_v[2])


def normalise(rows):
    centred = rows - jnp.mean(rows, axis=-1, keepdims=True)
    scale = lax.rsqrt(jnp.mean(centred * centred, axis=-1, keepdims=True) + EPSILON)
    return centred * scale, scale


def norm_backward(grad, norm, scale, gain):
    scaled = grad * gain
    mean = jnp.mean(scaled, axis=-1, keepdims=True)
    along = jnp.mean(scaled * norm, axis=-1, keepdims=True)
    return scale * (scaled - mean - norm * along)


def gelu_pair(u):
    below = 0.5 + 0.5 * lax.erf(u * math.sqrt(0.5))
    bell = jnp.exp2((-0.5 * math.log2(math.e)) * (u * u)) * (1.0 / math.sqrt(2.0 * math.pi))
    return u * below, below + u * bell


B_OUT, GAIN_ONE, SHIFT_ONE, B_BACK, GAIN_TWO, SHIFT_TWO = 2, 3, 4, 5, 6, 7


def tiles_of(total, tile):
    return [slice(at, at + tile) for at in range(0, total, tile)]


def split_cores(meta, block, keep, send, groups, rows):
    mine = meta[CORE]
    for at in range(groups):
        low = block[2 * at * rows : (2 * at + 1) * rows]
        high = block[(2 * at + 1) * rows : (2 * at + 2) * rows]
        if keep is not None:
            keep[at] = jnp.where(mine == 0, low, high).astype(BF)
        if send is not None:
            send[at] = jnp.where(mine == 0, high, low).astype(BF)


def rows_forward(
    steps, meta, tok, two_half, att, cot, cot_half, cot_came, w_out, vec, w_in, b_in, w_back,
    slope, keep, send, sums, first_out, normed_out, mixed_out, mixed_two_out, second_out, back_out,
    first, normed_low, mixed, second, back_low, active, sems,
):
    step = pl.program_id(0)
    total = att.shape[0]
    tile = two_half.shape[0]
    size = total - tile
    chunk = w_in.shape[1]
    tiles = tiles_of(total, tile)
    copies = [
        pltpu.make_async_copy(source, target, sems.at[at])
        for at, (source, target) in enumerate(
            (
                (first, first_out), (normed_low, normed_out), (mixed.at[pl.ds(0, size)], mixed_out),
                (mixed.at[pl.ds(size, tile)], mixed_two_out), (second, second_out), (back_low, back_out),
            )
        )
    ]

    @pl.when(step == 0)
    def _():
        for at, span in enumerate(tiles):
            rows = (tok[span, :] if at + 1 < len(tiles) else two_half[...]).astype(F32)
            rows = rows + dot(att[span, :], w_out[...]) + vec[B_OUT : B_OUT + 1, :]
            first[span, :] = rows
            result = normalise(rows)[0] * vec[GAIN_ONE : GAIN_ONE + 1, :] + vec[SHIFT_ONE : SHIFT_ONE + 1, :]
            normed_low[span, :] = result.astype(BF)
            second[span, :] = result + vec[B_BACK : B_BACK + 1, :]
        copies[0].start()
        copies[1].start()

    @pl.when(step < steps)
    def _():
        hidden = dot(normed_low[...], w_in[...]) + b_in[...]
        value, grad = gelu_pair(hidden)
        value = value.astype(BF)
        active[:, pl.ds(pl.multiple_of(step * chunk, chunk), chunk)] = value
        slope[...] = grad.astype(BF)
        second[...] += dot(value, w_back[...])

    @pl.when(step == steps - 1)
    def _():
        sums[...] = jnp.zeros_like(sums)
        gain, shift = vec[GAIN_TWO : GAIN_TWO + 1, :], vec[SHIFT_TWO : SHIFT_TWO + 1, :]
        for at, span in enumerate(tiles):
            last = at + 1 == len(tiles)
            live = meta[LIVE + last].astype(F32)
            norm, scale = normalise(second[span, :])
            mixed[span, :] = ((norm * gain + shift) * live).astype(BF)
            cotangent = jnp.where(meta[SIDE] == 0, cot_half[...], cot_came[...]) if last else cot[span, :]
            grad = cotangent.astype(F32) * live
            sums[0:1, :] += jnp.sum(grad * norm, axis=0, keepdims=True)
            sums[1:2, :] += jnp.sum(grad, axis=0, keepdims=True)
            grad = norm_backward(grad, norm, scale, gain)
            sums[2:3, :] += jnp.sum(grad, axis=0, keepdims=True)
            second[span, :] = grad
            back_low[span, :] = grad.astype(BF)
        for copy in copies[2:]:
            copy.start()

    @pl.when(step >= steps)
    def _():
        groups, rows, _ = keep.shape
        columns = 2 * groups * rows
        part = active[:, pl.ds(pl.multiple_of((step - steps) * columns, columns), columns)]
        split_cores(meta, dot(part, back_low[...], 0, 0), keep, send, groups, rows)

    @pl.when(step == pl.num_programs(0) - 1)
    def _():
        for copy in copies:
            copy.wait()


def rows_backward(
    meta, back_low, normed_low, slope, w_in, w_back, w_out, vec, first_in, second_in, att_in,
    keep, *refs
):
    sends, (g_first, first_low, do_t, b_in, sums, first, g_normed, g_second, att_t, sems) = refs[:-10], refs[-10:]
    step = pl.program_id(0)
    last = pl.num_programs(0) - 1
    total = back_low.shape[0]
    tiles = tiles_of(total, total // 3)
    copies = [
        pltpu.make_async_copy(first_in, first, sems.at[0]),
        pltpu.make_async_copy(second_in, g_second, sems.at[1]),
        pltpu.make_async_copy(att_in, att_t, sems.at[2]),
    ]

    @pl.when(step == 0)
    def _():
        for copy in copies:
            copy.start()
        g_normed[...] = jnp.zeros_like(g_normed)

    @pl.when(step < last)
    def _():
        grad = dot(back_low[...], w_back[...], 1, 1) * slope[...].astype(F32)
        b_in[...] = jnp.sum(grad, axis=0, keepdims=True)
        low = grad.astype(BF)
        g_normed[...] += dot(low, w_in[...], 1, 1)
        block = dot(normed_low[...], low, 0, 0)
        for number, send in enumerate(sends[:-1]):

            @pl.when(step == number)
            def _():
                split_cores(meta, block, None, send, keep.shape[0], keep.shape[1])

        split_cores(meta, block, keep, None, keep.shape[0], keep.shape[1])

    @pl.when(step == last)
    def _():
        for copy in copies:
            copy.wait()
        sums[...] = jnp.zeros_like(sums)
        for span in tiles:
            norm, scale = normalise(first[span, :])
            grad = g_normed[span, :] + g_second[span, :]
            sums[0:1, :] += jnp.sum(grad * norm, axis=0, keepdims=True)
            sums[1:2, :] += jnp.sum(grad, axis=0, keepdims=True)
            grad = norm_backward(grad, norm, scale, vec[GAIN_ONE : GAIN_ONE + 1, :])
            sums[2:3, :] += jnp.sum(grad, axis=0, keepdims=True)
            g_first[span, :] = grad
            first_low[span, :] = grad.astype(BF)
        do_t[...] = dot(w_out[...], first_low[...], 1, 1).astype(BF)
        split_cores(meta, dot(att_t[...], first_low[...]), keep, sends[-1], keep.shape[0], keep.shape[1])


def weight_gradients(
    meta, tok_in, two_in, other_in, gq_in, gkv_in, sums_two, sums_one, g_bq, g_bv, g_b_in,
    keep_out, send_out,
    tok, gq_t, gkv_t, tok_t, keep, send, keep_last, send_last, sems, out_sems,
):
    _, size, width = tok.shape
    half_rows = size // 2
    ins = [
        pltpu.make_async_copy(source, target, sems.at[at])
        for at, (source, target) in enumerate(
            [
                (tok_in.at[0], tok.at[0]), (two_in, tok.at[1]), (gq_in, gq_t), (other_in.at[0], tok.at[2]),
                (gkv_in.at[0], gkv_t.at[0]), (gkv_in.at[1], gkv_t.at[1]), (gkv_in.at[2], gkv_t.at[2]),
            ]
        )
    ]
    for copy in ins:
        copy.start()
    groups, own_rows = keep.shape[1], keep.shape[2]

    def outs(section):
        slot = section % 2
        columns = pl.ds(section * width, width)
        return [
            pltpu.make_async_copy(keep.at[slot], keep_out.at[:, :, columns], out_sems.at[2 * slot]),
            pltpu.make_async_copy(send.at[slot], send_out.at[:, :, columns], out_sems.at[2 * slot + 1]),
        ]

    def finish(section, block):
        slot = section % 2
        if section >= 2:
            for copy in outs(section - 2):
                copy.wait()
        split_cores(meta, block, keep.at[slot], send.at[slot], groups, own_rows)
        for copy in outs(section):
            copy.start()

    def turn(at):
        tok_t[:, at * size : (at + 1) * size] = tok[at].T

    vectors = [sums_two[0:3, :], sums_one[0:3, :], g_bq[...], g_bv[...], jnp.zeros((120, width), F32)]
    vectors = jnp.concatenate(vectors, axis=0).T
    per_owner = g_b_in.shape[1] // (2 * groups)
    line = min(64, per_owner)
    bias_rows = []
    for at in range(2 * groups):
        lines = [
            jnp.concatenate(
                [
                    jnp.zeros((1, 64), F32),
                    g_b_in[:, at * per_owner + to : at * per_owner + to + line],
                    jnp.zeros((1, 64 - line), F32),
                ][: 2 + (line < 64)],
                axis=1,
            )
            for to in range(0, per_owner, line)
        ]
        bias_rows.append(jnp.concatenate(lines + [jnp.zeros((own_rows - len(lines), 128), F32)], axis=0))
    split_cores(meta, vectors + jnp.concatenate(bias_rows, axis=0), keep_last, send_last, groups, own_rows)
    last = [
        pltpu.make_async_copy(keep_last, keep_out.at[:, :, pl.ds(3 * width, 128)], out_sems.at[4]),
        pltpu.make_async_copy(send_last, send_out.at[:, :, pl.ds(3 * width, 128)], out_sems.at[5]),
    ]
    for copy in last:
        copy.start()
    for copy in ins[:3]:
        copy.wait()
    turn(0)
    turn(1)
    half = tok_t[:, pl.ds(pl.multiple_of(size + meta[SIDE] * half_rows, half_rows), half_rows)]
    finish(0, dot(tok_t[:, :size], gq_t[:, :size], 1, 1) + dot(half, gq_t[:, size:], 1, 1))
    for copy in ins[3:]:
        copy.wait()
    turn(2)
    for which in range(2):
        span = slice(which * width, (which + 1) * width)
        block = dot(tok_t[:, :size], gkv_t[0, span, :], 1, 1)
        block = block + dot(tok_t[:, size : 2 * size], gkv_t[1, span, :], 1, 1)
        finish(1 + which, block + dot(tok_t[:, 2 * size :], gkv_t[2, span, :], 1, 1))
    for copy in outs(1) + outs(2) + last:
        copy.wait()


def tokens_backward(meta, w, gq_t, gkv_t, g_first, sent, two, own, w_kv, w_q):
    step = pl.program_id(0)
    size, width = own.shape
    half_rows = size // 2

    @pl.when(step == 0)
    def _():
        w_kv[...] = w[:, width:]
        w_q[...] = w[:, :width]
        sent[0] = dot(w_kv[...], gkv_t[...]).T.astype(BF)

    @pl.when(step == 1)
    def _():
        two[...] = dot(w_kv[...], gkv_t[...]).T
        span = pl.ds(pl.multiple_of(meta[SIDE] * half_rows, half_rows), half_rows)
        two[span, :] += dot(w_q[...], gq_t[:, size:]).T + g_first[size:, :]
        sent[1] = two[...].astype(BF)

    @pl.when(step == 2)
    def _():
        total = dot(w_q[...], gq_t[:, :size]) + dot(w_kv[...], gkv_t[...])
        own[...] = total.T + g_first[:size, :]


def flip(value, axis, bit):
    count = lax.axis_size(axis)
    return lax.ppermute(value, axis, [(at, at ^ bit) for at in range(count)])


def after(value, *others):
    return lax.optimization_barrier((value,) + others)[0]


CORE_SUM, QUAD, PAIR = 0, 1, 2


def combine_kernel(plan, meta, *refs):
    refs = list(refs)
    ins = [[refs.pop(0) for _ in range(count)] for _, _, _, count, _ in plan]
    outs = [[refs.pop(0) for _ in range(count)] for _, _, _, _, count in plan]
    for (stage, over_x, bit, _, _), parts, targets in zip(plan, ins, outs):
        if stage == CORE_SUM:
            kept, pieces = parts[0], parts[1:]
            (out,) = targets
            columns = kept.shape[2]
            each = columns // len(pieces)
            for at in range(kept.shape[0]):
                for number, piece in enumerate(pieces):
                    if not over_x:
                        span = slice(each * number, each * (number + 1))
                        total = kept[at, :, span].astype(F32) + piece[at].astype(F32)
                        out[at % 4, at // 4, :, span] = total.astype(BF)
                        continue
                    for side in range(2):
                        low = max(each * number, side * columns // 2)
                        high = min(each * (number + 1), (side + 1) * columns // 2)
                        if low < high:
                            total = kept[at, :, low:high].astype(F32)
                            total = total + piece[at, :, low - each * number : high - each * number].astype(F32)
                            to = slice(low - side * columns // 2, high - side * columns // 2)
                            out[2 * (at % 2) + side, at // 2, :, to] = total.astype(BF)
            continue

        def total_at(index):
            if stage == QUAD:
                (came,) = parts
                return (came[0, index].astype(F32) + came[1, index].astype(F32)) + (
                    came[2, index].astype(F32) + came[3, index].astype(F32)
                )
            kept, came = parts
            return kept[index].astype(F32) + came[index].astype(F32)

        if len(targets) == 1:
            targets[0][...] = total_at(0).astype(BF)
        else:
            mine = (meta[OWNER] >> bit) & 1
            for flipped, out in enumerate(targets):
                which = 1 - mine if flipped else mine
                for to in range(out.shape[0]):
                    out[to] = total_at(2 * to + which).astype(BF)


class Piece:
    def __init__(self, keep, sends, over_x):
        self.over_x = over_x
        self.rows = keep.shape[1]
        self.columns = keep.shape[2] // 2 if over_x else keep.shape[2]
        bits = list(range(1, lax.axis_size("batch").bit_length() - 1))
        self.plane, self.bits = (bits[:1], bits[1:]) if over_x else (bits[:2], bits[2:])
        self.stage = CORE_SUM
        self.parts = [keep] + [flip(send, "batch", 1) for send in sends]

    def shapes(self):
        sds = lambda *lead: jax.ShapeDtypeStruct(lead + (self.rows, self.columns), BF)
        if self.stage == CORE_SUM:
            return [sds(4, self.parts[0].shape[0] // 2 ** len(self.plane))]
        count = self.parts[0].shape[-3]
        return [sds(count // 2)] * 2 if count > 1 else [sds()]

    def taken(self, results):
        self.sending = results[-1]
        if self.stage == CORE_SUM:
            owners = lax.axis_size("batch")
            if self.over_x:
                groups = [
                    [2 * (high + 2 * bit + core) + side for bit in range(2) for side in range(2)]
                    for high in range(0, owners, 4)
                    for core in range(2)
                ]
                came = lax.all_to_all(results[0], ("batch", "blk"), 0, 0, axis_index_groups=groups)
            else:
                groups = [
                    [high + 2 * place + core for place in range(4)] for high in range(0, owners, 8) for core in range(2)
                ]
                came = lax.all_to_all(results[0], "batch", 0, 0, axis_index_groups=groups)
            self.parts = [came]
            self.stage = QUAD
        elif len(results) == 2:
            self.parts = [results[0], flip(results[1], "batch", 1 << self.bits.pop(0))]
            self.stage = PAIR
        else:
            self.parts = [results[0], flip(results[0], "blk", 1)]
            self.stage = None

    def finish(self, side):
        own, came = self.parts
        if not self.over_x:
            return own.astype(F32) + came.astype(F32)
        return jnp.concatenate([jnp.where(side == 0, own, came), jnp.where(side == 0, came, own)], axis=1).astype(F32)


def take(meta, pieces, *order_after):
    operands, plan, shapes = [], [], []
    for piece in pieces:
        piece.parts = list(lax.optimization_barrier(tuple(piece.parts) + order_after)[: len(piece.parts)])
        made = piece.shapes()
        bit = piece.bits[0] if piece.bits else 0
        plan.append((piece.stage, piece.over_x, bit, len(piece.parts), len(made)))
        operands += piece.parts
        shapes += made
    vmem = pl.BlockSpec(memory_space=pltpu.VMEM)
    out = pl.pallas_call(
        functools.partial(combine_kernel, plan),
        in_specs=[pl.BlockSpec(memory_space=pltpu.SMEM)] + [vmem] * len(operands),
        out_specs=[vmem] * len(shapes),
        out_shape=shapes,
        compiler_params=params(28),
        cost_estimate=cost(1, 1),
        name="combine",
    )(meta, *operands)
    for piece, (_, _, _, _, count) in zip(pieces, plan):
        piece.taken(out[:count])
        out = out[count:]
    return tuple(part for piece in pieces for part in piece.parts[:1] if piece.stage != QUAD)


def local(
    tokens, cotangent, counts, perms, key_mask, w_qkv, bias_q, bias_v, w_out, bias_out, gain_one, shift_one,
    w_in, bias_in, w_back, bias_back, gain_two, shift_two,
):
    _, _, size, width = tokens.shape
    heads = perms.shape[1]
    pairs = heads // 2
    hidden = w_in.shape[1]
    half_rows = size // 2
    total = size + half_rows
    owners = lax.axis_size("batch")
    side = lax.axis_index("blk").astype(jnp.int32)
    owner = lax.axis_index("batch").astype(jnp.int32)
    whole = lambda *shape: once(shape, lambda *_: (0,) * len(shape))
    sds = jax.ShapeDtypeStruct
    anywhere = pl.BlockSpec(memory_space=pl.ANY)

    tok = tokens[0]
    came = flip(tok, "blk", 1)

    count = counts[0]
    lookup = jnp.where(count == 2, perms[0], perms[1])
    own = jnp.where(side == 0, lookup[:, 0], lookup[:, 1])
    two = jnp.where(count > 2, lookup[:, 2], 2)
    source = jnp.concatenate([own, two])
    place = jnp.where(source == 2, 1, jnp.where(source == side, 0, 2))
    live = jnp.stack([(side < count).astype(jnp.int32), (count > 2).astype(jnp.int32)])
    meta = jnp.concatenate([jnp.stack([side, owner & 1]), live, owner[None], place])
    vec = jnp.concatenate([bias_q, bias_v, bias_out, gain_one, shift_one, bias_back, gain_two, shift_two]).reshape(8, width)
    own_mask = key_mask[0]

    def grid_spec(grid, in_specs, out_specs, scratch=()):
        return pltpu.PrefetchScalarGridSpec(
            num_scalar_prefetch=1, grid=grid, in_specs=in_specs, out_specs=out_specs, scratch_shapes=list(scratch)
        )

    slot = lambda at: once((None, size, width), lambda *_: (at, 0, 0))
    all_rows = whole(total, width)
    vectors = whole(8, width)
    own_q, own_k, own_v, own_mb = pl.pallas_call(
        project_own,
        grid_spec=grid_spec(
            (3,),
            [slot(0), whole(1, size), pl.BlockSpec((width, width), lambda i, m: (0, i)), vectors],
            [whole(width, size), whole(size, width), whole(width, size), whole(size, 128)],
        ),
        out_shape=[sds((width, size), BF), sds((size, width), BF), sds((width, size), BF), sds((size, 128), F32)],
        compiler_params=params(60),
        cost_estimate=cost(1e9, 1),
        name="project_own",
    )(meta, tok, own_mask[0:1], w_qkv, vec)
    other_mask = flip(after(own_mask, own_mb), "blk", 1)
    masks = jnp.stack([jnp.where(side == 0, own_mask[1], other_mask[1]), other_mask[0]])
    cot = cotangent[0]
    cot_came = lax.ppermute(after(cot[1, half_rows:], came), "blk", [(0, 1)])

    pair_q = pl.BlockSpec((128, total), lambda p, m: (p, 0))
    pair_rows = pl.BlockSpec((3, size, 128), lambda p, m: (0, 0, p))
    pair_cols = pl.BlockSpec((3, 128, size), lambda p, m: (0, p, 0))
    pair_probs = pl.BlockSpec((2, size, total), lambda p, m: (p, 0, 0))
    pair_inv = pl.BlockSpec((1, 2, total), lambda p, m: (p, 0, 0))
    probs, att, att_t, inv, q_t, k, v_t, tok_two = pl.pallas_call(
        functools.partial(attention_forward, heads),
        grid_spec=grid_spec(
            (pairs,),
            [whole(2, size), vectors] + [anywhere] * 7,
            [pair_probs, pl.BlockSpec((total, 128), lambda p, m: (0, p)), pair_q, pair_inv] + [anywhere] * 4,
            [
                pltpu.VMEM((width, total), BF), pltpu.VMEM((3, size, width), BF), pltpu.VMEM((3, width, size), BF),
                pltpu.VMEM((3, size, 128), F32), pltpu.VMEM((width, 3 * width), BF), pltpu.VMEM((size, width), BF),
                pltpu.VMEM((size, width), BF), pltpu.SemaphoreType.DMA((9,)), pltpu.SemaphoreType.DMA((4,)),
            ],
        ),
        out_shape=[
            sds((heads, size, total), BF), sds((total, width), BF), sds((width, total), BF),
            sds((pairs, 2, total), F32), sds((width, total), BF), sds((3, size, width), BF), sds((3, width, size), BF),
            sds((size, width), BF),
        ],
        compiler_params=params(60),
        cost_estimate=cost(1e11, 1),
        name="attention_forward",
    )(meta, masks, vec, tok, came, w_qkv, own_q, own_k, own_v, own_mb)

    chunk = 1024
    steps = hidden // chunk
    back_steps = 4
    half = owners // 2
    back_rows = hidden // owners
    back_half = pl.BlockSpec((half // back_steps, back_rows, width), lambda i, m: (jnp.maximum(i - steps, 0), 0, 0))
    flat = lambda dtype, columns=width: sds((total, columns), dtype)
    early = lambda i: jnp.minimum(i, steps - 1)
    side_rows = once((half_rows, width), lambda i, m: (m[SIDE], 0))
    slope, back_keep, back_send, sums_two, first, normed_low, mixed, mixed_two, g_second, back_low = pl.pallas_call(
        functools.partial(rows_forward, steps),
        grid_spec=grid_spec(
            (steps + back_steps,),
            [
                slot(0), side_rows, all_rows, slot(0), once((None, half_rows, width), lambda i, m: (1, 0, 0)),
                whole(half_rows, width), whole(width, width), vectors,
                pl.BlockSpec((width, chunk), lambda i, m: (0, early(i))),
                pl.BlockSpec((1, chunk), lambda i, m: (0, early(i))),
                pl.BlockSpec((chunk, width), lambda i, m: (early(i), 0)),
            ],
            [
                pl.BlockSpec((total, chunk), lambda i, m: (0, early(i))),
                back_half, back_half, whole(8, width),
            ]
            + [anywhere] * 6,
            [
                pltpu.VMEM((total, width), F32), pltpu.VMEM((total, width), BF), pltpu.VMEM((total, width), BF),
                pltpu.VMEM((total, width), F32), pltpu.VMEM((total, width), BF), pltpu.VMEM((total, hidden), BF),
                pltpu.SemaphoreType.DMA((6,)),
            ],
        ),
        out_shape=[
            flat(BF, hidden), sds((half, back_rows, width), BF), sds((half, back_rows, width), BF),
            sds((8, width), F32), flat(F32), flat(BF),
            sds((size, width), BF), sds((half_rows, width), BF), flat(F32), flat(BF),
        ],
        compiler_params=params(60),
        cost_estimate=cost(1e11, 1),
        name="rows_forward",
    )(
        meta, tok, tok_two, att, cot, cot, cot_came, w_out, vec, w_in, bias_in.reshape(1, hidden), w_back,
    )

    back = Piece(back_keep, [back_send], True)
    take(meta, [back])
    back_low = after(back_low, back.sending)
    mixed_came = lax.ppermute(mixed_two, "blk", [(1, 0)])

    own_rows = width // owners
    in_steps = hidden // width
    in_early = lambda i: jnp.minimum(i, in_steps - 1)
    in_half = pl.BlockSpec((half, own_rows, width), lambda i, m: (0, 0, i))
    in_keep, *rest = pl.pallas_call(
        rows_backward,
        grid_spec=grid_spec(
            (in_steps + 1,),
            [
                all_rows, all_rows, pl.BlockSpec((total, width), lambda i, m: (0, in_early(i))),
                pl.BlockSpec((width, width), lambda i, m: (0, in_early(i))),
                pl.BlockSpec((width, width), lambda i, m: (in_early(i), 0)),
                whole(width, width), vectors, anywhere, anywhere, anywhere,
            ],
            [
                in_half, *[whole(half, own_rows, width)] * (in_steps + 1), all_rows, all_rows, whole(width, total),
                pl.BlockSpec((1, width), lambda i, m: (0, in_early(i))), whole(8, width),
            ],
            [
                pltpu.VMEM((total, width), F32), pltpu.VMEM((total, width), F32), pltpu.VMEM((total, width), F32),
                pltpu.VMEM((width, total), BF), pltpu.SemaphoreType.DMA((3,)),
            ],
        ),
        out_shape=[
            sds((half, own_rows, hidden + width), BF), *[sds((half, own_rows, width), BF)] * (in_steps + 1), flat(F32),
            flat(BF),
            sds((width, total), BF), sds((1, hidden), F32), sds((8, width), F32),
        ],
        compiler_params=params(60),
        cost_estimate=cost(1e11, 1),
        name="rows_backward",
    )(meta, back_low, normed_low, slope, w_in, w_back, w_out, vec, first, g_second, att_t)
    in_sends, (g_first, first_low, do_t, g_b_in, sums_one) = rest[:-5], rest[-5:]
    inner = Piece(in_keep, in_sends, False)
    do_t = after(do_t, *take(meta, [back], do_t))
    do_t = after(do_t, *take(meta, [inner], do_t))
    gq_shapes = [
        sds((width, total), BF), sds((3, 2, width, size), BF), sds((1, width), F32), sds((1, width), F32),
    ]

    gq_t, gkv_t, g_bq, g_bv = pl.pallas_call(
        functools.partial(attention_backward, heads),
        grid_spec=grid_spec(
            (pairs,),
            [pair_probs, pair_rows, pair_cols, pair_q, pair_q, pair_q, pair_inv],
            [pair_q, pl.BlockSpec((3, 2, 128, size), lambda p, m: (0, 0, p, 0))]
            + [pl.BlockSpec((1, 128), lambda p, m: (0, p))] * 2,
            [
                pltpu.VMEM((3, 128, size), F32), pltpu.VMEM((3, 128, size), F32), pltpu.VMEM((128, total), F32),
                pltpu.VMEM((3, 128, size), BF), pltpu.VMEM((3, size, 128), BF),
            ],
        ),
        out_shape=gq_shapes,
        compiler_params=params(60),
        cost_estimate=cost(1e11, 1),
        name="attention_backward",
    )(meta, probs, k, v_t, q_t, do_t, att_t, inv)
    gkv_t = gkv_t.reshape(3, 2 * width, size)
    gq_t = after(gq_t, mixed_came, *take(meta, [back], gq_t))

    columns = 3 * width + 128
    vmem = pl.BlockSpec(memory_space=pltpu.VMEM)
    run_weights = pl.pallas_call(
        weight_gradients,
        in_specs=[pl.BlockSpec(memory_space=pltpu.SMEM)] + [anywhere] * 5 + [vmem] * 5,
        out_specs=[anywhere] * 2,
        scratch_shapes=[
            pltpu.VMEM((3, size, width), BF), pltpu.VMEM((width, total), BF), pltpu.VMEM((3, 2 * width, size), BF),
            pltpu.VMEM((width, 3 * size), BF),
            pltpu.VMEM((2, half, own_rows, width), BF), pltpu.VMEM((2, half, own_rows, width), BF),
            pltpu.VMEM((half, own_rows, 128), BF), pltpu.VMEM((half, own_rows, 128), BF),
            pltpu.SemaphoreType.DMA((7,)), pltpu.SemaphoreType.DMA((6,)),
        ],
        out_shape=[sds((half, own_rows, columns), BF)] * 2,
        compiler_params=params(60),
        cost_estimate=cost(4e9, 1),
        name="weight_gradients",
    )
    last_keep, last_send = run_weights(
        meta, tok, tok_two, came, gq_t, gkv_t, sums_two, sums_one, g_bq, g_bv, g_b_in
    )
    last = Piece(last_keep, [last_send], False)
    shown = take(meta, [inner, back], last_keep)
    gq_t = after(gq_t, *shown, inner.sending, back.sending)

    sent, two_own, own_grad = pl.pallas_call(
        tokens_backward,
        grid_spec=grid_spec(
            (3,),
            [
                whole(width, 3 * width), whole(width, total),
                pl.BlockSpec((None, 2 * width, size), lambda i, m: (2 - i, 0, 0)), all_rows,
            ],
            [whole(2, size, width), whole(size, width), whole(size, width)],
            [pltpu.VMEM((width, 2 * width), BF), pltpu.VMEM((width, width), BF)],
        ),
        out_shape=[sds((2, size, width), BF), sds((size, width), F32), sds((size, width), F32)],
        compiler_params=params(60),
        cost_estimate=cost(1e11, 1),
        name="tokens_backward",
    )(meta, w_qkv, gq_t, gkv_t, g_first)
    came_grad = flip(sent, "blk", 1)
    shown = take(meta, [last], own_grad)
    shown = take(meta, [last, inner], last.sending)
    while last.stage is not None:
        shown = take(meta, [piece for piece in (last, inner, back) if piece.stage is not None], *shown)

    out_back = back.finish(side)
    out_in = inner.finish(side)
    out_last = last.finish(side)

    came_grad = after(came_grad, *shown).astype(F32)
    tokens_grad = jnp.stack([own_grad + came_grad[0], jnp.where(side == 0, two_own + came_grad[1], 0.0)]).astype(BF)[None]
    mixed_other = jnp.where(side == 0, jnp.concatenate([mixed_two, mixed_came]), jnp.zeros((), BF))
    mixed_all = jnp.stack([mixed, mixed_other])[None]
    pick = lambda at: out_last[:, 3 * width + at]
    line = min(64, back_rows)
    return (
        mixed_all, tokens_grad,
        out_last[:, : 3 * width], pick(6), pick(7), out_in[:, hidden:], pick(5), pick(3), pick(4),
        out_in[:, :hidden], out_last[: back_rows // line, 3 * width + 64 : 3 * width + 64 + line].reshape(-1), out_back, pick(2), pick(0),
        pick(1),
    )


def solution(mesh):
    split = P("batch", None, "blk", None)
    in_specs = (split, split, P("batch"), P(), P("batch", None, "blk")) + (P(),) * 13
    matrix, vector = P("batch", None), P("batch")
    out_specs = (
        split, split, matrix, vector, vector, matrix, vector, vector, vector, matrix, vector, matrix, vector, vector,
        vector,
    )
    return jax.shard_map(local, mesh=mesh, in_specs=in_specs, out_specs=out_specs, check_vma=False)
```

```python
import functools
import math

import jax
import jax.numpy as jnp
from jax import lax
from jax.experimental import pallas as pl
from jax.experimental.pallas import tpu as pltpu
from jax.sharding import PartitionSpec as P

EPSILON = 1e-05
BF = jnp.bfloat16
F32 = jnp.float32
MIB = 1024 * 1024
NEGATIVE = -1e30

SIDE, CORE, LIVE, OWNER, SOURCE = 0, 1, 2, 4, 5


def dot(a, b, ca=1, cb=0):
    return lax.dot_general(a, b, (((ca,), (cb,)), ((), ())), preferred_element_type=F32)


def params(mebibytes):
    return pltpu.CompilerParams(vmem_limit_bytes=mebibytes * MIB)


def cost(flops, read):
    return pl.CostEstimate(flops=int(flops), bytes_accessed=int(read), transcendentals=0)


def once(shape, index):
    return pl.BlockSpec(shape, index, pipeline_mode=pl.Buffered(1))


def mask_columns(mask_row):
    penalty = jnp.where(mask_row == 0, NEGATIVE, 0.0).astype(F32)
    return jnp.broadcast_to(penalty, (128, penalty.shape[1])).T


def project_own(meta, tok, mask, w, vec, q_t, k, v_t, mb):
    step = pl.program_id(0)
    rows = tok[...]

    @pl.when(step == 0)
    def _():
        queries = (dot(rows, w[...]) + vec[0:1, :]).astype(BF)
        q_t[...] = (queries * 0.125).T
        mb[...] = mask_columns(mask[...])

    @pl.when(step == 1)
    def _():
        k[...] = dot(rows, w[...]).astype(BF)

    @pl.when(step == 2)
    def _():
        v_t[...] = (dot(rows, w[...]) + vec[1:2, :]).astype(BF).T


def pad_pair(part, head):
    zeros = jnp.zeros_like(part)
    return jnp.concatenate([part, zeros] if head % 2 == 0 else [zeros, part], axis=0)


def units(heads, each, size, total, meta):
    first = pl.program_id(0) * each
    out = []
    for head in range(each):
        for slot, queries in enumerate((slice(0, size), slice(size, total))):
            source = meta[SOURCE + slot * heads + first + head]
            out.append((head, slice(64 * head, 64 * head + 64), queries, source))
    return out


def project_others(meta, vec, masks, starts, ins, k, v_t, q_t, mb, w, rows):
    size, width = k.shape[1:]
    half_rows = size // 2
    own_two, partner_two = starts

    @pl.when(meta[SIDE] == 0)
    def _():
        own_two.start()

    @pl.when(meta[SIDE] == 1)
    def _():
        partner_two.start()

    for copy in ins:
        copy.start()
    mb[1] = mask_columns(masks[0:1, :])
    mb[2] = mask_columns(masks[1:2, :])
    own_two.wait()
    for copy in ins[:2]:
        copy.wait()
    keys = dot(rows[...], w[:, width : 2 * width]).astype(BF)
    k[1] = keys[:size]
    k[2] = keys[size:]
    ins[2].wait()
    values = (dot(rows[...], w[:, 2 * width :]) + vec[1:2, :]).astype(BF)
    ins[3].wait()
    mine = rows[pl.ds(pl.multiple_of(meta[SIDE] * half_rows, half_rows), half_rows), :]
    queries = (dot(mine, w[:, :width]) + vec[0:1, :]).astype(BF) * 0.125
    v_t[1] = values[:size].T
    v_t[2] = values[size:].T
    q_t[:, size:] = queries.T
    for copy in ins[4:]:
        copy.wait()


def attention_forward(
    heads, meta, masks, vec, tok_in, came_in, w_in, q_own, k_own, v_own, mb_own,
    probs, att, att_t, inv, q_out, k_out, v_out, two_out,
    q_t, k, v_t, mb, w, rows, sems, out_sems,
):
    size, total = k.shape[1], q_t.shape[1]
    width = k.shape[2]
    step = pl.program_id(0)
    copy = pltpu.make_async_copy
    outs = [
        copy(source, target, out_sems.at[at])
        for at, (source, target) in enumerate(((q_t, q_out), (k, k_out), (v_t, v_out), (rows.at[pl.ds(0, size)], two_out)))
    ]

    @pl.when(step == 0)
    def _():
        columns = [slice(width, 2 * width), slice(2 * width, 3 * width), slice(0, width)]
        two = rows.at[pl.ds(0, size)]
        starts = [copy(tok_in.at[1], two, sems.at[0]), copy(came_in.at[1], two, sems.at[0])]
        ins = [
            copy(w_in.at[:, columns[0]], w.at[:, columns[0]], sems.at[1]),
            copy(came_in.at[0], rows.at[pl.ds(size, size)], sems.at[2]),
            copy(w_in.at[:, columns[1]], w.at[:, columns[1]], sems.at[3]),
            copy(w_in.at[:, columns[2]], w.at[:, columns[2]], sems.at[4]),
            copy(q_own, q_t.at[:, pl.ds(0, size)], sems.at[5]),
            copy(k_own, k.at[0], sems.at[6]),
            copy(v_own, v_t.at[0], sems.at[7]),
            copy(mb_own, mb.at[0], sems.at[8]),
        ]
        project_others(meta, vec, masks, starts, ins, k, v_t, q_t, mb, w, rows)
        for out in outs:
            out.start()

    todo = units(heads, probs.shape[0], size, total, meta)
    each = att_t.shape[0]

    def lanes_of(head):
        return pl.ds(pl.multiple_of(step * each + head // 2 * 128, 128), 128)

    def rows_of(span):
        return pl.ds(pl.multiple_of(step * each + span.start, 64), 64)

    def score(unit):
        half, span, queries, source = unit
        return dot(k[source, :, lanes_of(half)], pad_pair(q_t[rows_of(span), queries], half))

    def soften(unit, scores):
        half, span, queries, source = unit
        scores = scores + jnp.concatenate([mb[source]] * (scores.shape[1] // 128), axis=1)
        weights = jnp.exp(scores - jnp.max(scores, axis=0, keepdims=True))
        inverse = 1.0 / jnp.sum(weights, axis=0, keepdims=True)
        low = weights.astype(BF)
        probs[half, :, queries] = low
        inv[0, half : half + 1, queries] = inverse
        return low, inverse

    def attend(unit, soft):
        half, span, queries, source = unit
        att_t[span, queries] = (dot(v_t[source, rows_of(span), :], soft[0]) * soft[1]).astype(BF)

    scores = {0: score(todo[0])}
    soft = {}
    for at in range(len(todo) + 1):
        if at + 1 < len(todo):
            scores[at + 1] = score(todo[at + 1])
        if at < len(todo):
            soft[at] = soften(todo[at], scores.pop(at))
        if at > 0:
            attend(todo[at - 1], soft.pop(at - 1))
    att[...] = att_t[...].T

    @pl.when(step == pl.num_programs(0) - 1)
    def _():
        for out in outs:
            out.wait()


def lane_sums(block):
    width = block.shape[1]
    part = block[:, :128]
    for at in range(128, width, 128):
        part = part + block[:, at : at + 128]
    return jnp.sum(part.T, axis=0, keepdims=True)


def attention_backward(
    heads, meta, probs, k, v_t, q_t, do_t, att_t, inv, gq_t, gkv_t, bq, bv, sum_k, sum_v, sum_q, k_t, v
):
    size, total = k.shape[1], q_t.shape[1]
    for at in range(3):
        k_t[at] = k[at].T
        v[at] = v_t[at].T
    todo = units(heads, probs.shape[0], size, total, meta)
    sum_k[...] = jnp.zeros_like(sum_k)
    sum_v[...] = jnp.zeros_like(sum_v)

    def begin(unit):
        half, span, queries, source = unit
        scaled = do_t[span, queries].astype(F32) * inv[0, half : half + 1, queries]
        delta = jnp.sum(scaled * att_t[span, queries].astype(F32), axis=0, keepdims=True)
        scaled = scaled.astype(BF)
        return scaled, delta, dot(v[source, :, 128 * (half // 2) : 128 * (half // 2) + 128], pad_pair(scaled, half))

    def middle(unit, begun):
        half, span, queries, source = unit
        scaled, delta, grad_probs = begun
        low = probs[half, :, queries]
        sum_v[source, span, :] += dot(scaled, low, 1, 1)
        return (low.astype(F32) * (grad_probs - delta)).astype(BF)

    def end(unit, grad_scores):
        half, span, queries, source = unit
        sum_k[source, span, :] += dot(q_t[span, queries], grad_scores, 1, 1)
        grad_q = dot(k_t[source, span, :], grad_scores) * 0.125
        sum_q[span, queries] = grad_q
        gq_t[span, queries] = grad_q.astype(BF)

    begun = {0: begin(todo[0])}
    grads = {}
    for at in range(len(todo) + 1):
        if at + 1 < len(todo):
            begun[at + 1] = begin(todo[at + 1])
        if at < len(todo):
            grads[at] = middle(todo[at], begun.pop(at))
        if at > 0:
            end(todo[at - 1], grads.pop(at - 1))
    gkv_t[:, 0] = sum_k[...].astype(BF)
    gkv_t[:, 1] = sum_v[...].astype(BF)
    bq[...] = lane_sums(sum_q[...])
    bv[...] = lane_sums(sum_v[0] + sum_v[1] + sum_v[2])


def normalise(rows):
    centred = rows - jnp.mean(rows, axis=-1, keepdims=True)
    scale = lax.rsqrt(jnp.mean(centred * centred, axis=-1, keepdims=True) + EPSILON)
    return centred * scale, scale


def norm_backward(grad, norm, scale, gain):
    scaled = grad * gain
    mean = jnp.mean(scaled, axis=-1, keepdims=True)
    along = jnp.mean(scaled * norm, axis=-1, keepdims=True)
    return scale * (scaled - mean - norm * along)


def gelu_pair(u):
    below = 0.5 + 0.5 * lax.erf(u * math.sqrt(0.5))
    bell = jnp.exp2((-0.5 * math.log2(math.e)) * (u * u)) * (1.0 / math.sqrt(2.0 * math.pi))
    return u * below, below + u * bell


B_OUT, GAIN_ONE, SHIFT_ONE, B_BACK, GAIN_TWO, SHIFT_TWO = 2, 3, 4, 5, 6, 7


def tiles_of(total, tile):
    return [slice(at, at + tile) for at in range(0, total, tile)]


def split_cores(meta, block, keep, send, groups, rows):
    mine = meta[CORE]
    for at in range(groups):
        low = block[2 * at * rows : (2 * at + 1) * rows]
        high = block[(2 * at + 1) * rows : (2 * at + 2) * rows]
        if keep is not None:
            keep[at] = jnp.where(mine == 0, low, high).astype(BF)
        if send is not None:
            send[at] = jnp.where(mine == 0, high, low).astype(BF)


def rows_forward(
    steps, meta, tok, two_half, att, cot, cot_half, cot_came, w_out, vec, w_in, b_in, w_back,
    slope, keep, send, sums, first_out, normed_out, mixed_out, mixed_two_out, second_out, back_out,
    first, normed_low, mixed, second, back_low, active, sems,
):
    step = pl.program_id(0)
    total = att.shape[0]
    tile = two_half.shape[0]
    size = total - tile
    chunk = w_in.shape[1]
    tiles = tiles_of(total, tile)
    copies = [
        pltpu.make_async_copy(source, target, sems.at[at])
        for at, (source, target) in enumerate(
            (
                (first, first_out), (normed_low, normed_out), (mixed.at[pl.ds(0, size)], mixed_out),
                (mixed.at[pl.ds(size, tile)], mixed_two_out), (second, second_out), (back_low, back_out),
            )
        )
    ]

    @pl.when(step == 0)
    def _():
        for at, span in enumerate(tiles):
            rows = (tok[span, :] if at + 1 < len(tiles) else two_half[...]).astype(F32)
            rows = rows + dot(att[span, :], w_out[...]) + vec[B_OUT : B_OUT + 1, :]
            first[span, :] = rows
            result = normalise(rows)[0] * vec[GAIN_ONE : GAIN_ONE + 1, :] + vec[SHIFT_ONE : SHIFT_ONE + 1, :]
            normed_low[span, :] = result.astype(BF)
            second[span, :] = result + vec[B_BACK : B_BACK + 1, :]
        copies[0].start()
        copies[1].start()

    @pl.when(step < steps)
    def _():
        hidden = dot(normed_low[...], w_in[...]) + b_in[...]
        value, grad = gelu_pair(hidden)
        value = value.astype(BF)
        active[:, pl.ds(pl.multiple_of(step * chunk, chunk), chunk)] = value
        slope[...] = grad.astype(BF)
        second[...] += dot(value, w_back[...])

    @pl.when(step == steps - 1)
    def _():
        sums[...] = jnp.zeros_like(sums)
        gain, shift = vec[GAIN_TWO : GAIN_TWO + 1, :], vec[SHIFT_TWO : SHIFT_TWO + 1, :]
        for at, span in enumerate(tiles):
            last = at + 1 == len(tiles)
            live = meta[LIVE + last].astype(F32)
            norm, scale = normalise(second[span, :])
            mixed[span, :] = ((norm * gain + shift) * live).astype(BF)
            cotangent = jnp.where(meta[SIDE] == 0, cot_half[...], cot_came[...]) if last else cot[span, :]
            grad = cotangent.astype(F32) * live
            sums[0:1, :] += jnp.sum(grad * norm, axis=0, keepdims=True)
            sums[1:2, :] += jnp.sum(grad, axis=0, keepdims=True)
            grad = norm_backward(grad, norm, scale, gain)
            sums[2:3, :] += jnp.sum(grad, axis=0, keepdims=True)
            second[span, :] = grad
            back_low[span, :] = grad.astype(BF)
        for copy in copies[2:]:
            copy.start()

    @pl.when(step >= steps)
    def _():
        groups, rows, _ = keep.shape
        columns = 2 * groups * rows
        part = active[:, pl.ds(pl.multiple_of((step - steps) * columns, columns), columns)]
        split_cores(meta, dot(part, back_low[...], 0, 0), keep, send, groups, rows)

    @pl.when(step == pl.num_programs(0) - 1)
    def _():
        for copy in copies:
            copy.wait()


def rows_backward(
    meta, back_low, normed_low, slope, w_in, w_back, w_out, vec, first_in, second_in, att_in,
    keep, *refs
):
    sends, (g_first, first_low, do_t, b_in, sums, first, g_normed, g_second, att_t, sems) = refs[:-10], refs[-10:]
    step = pl.program_id(0)
    last = pl.num_programs(0) - 1
    total = back_low.shape[0]
    tiles = tiles_of(total, total // 3)
    copies = [
        pltpu.make_async_copy(first_in, first, sems.at[0]),
        pltpu.make_async_copy(second_in, g_second, sems.at[1]),
        pltpu.make_async_copy(att_in, att_t, sems.at[2]),
    ]

    @pl.when(step == 0)
    def _():
        for copy in copies:
            copy.start()
        g_normed[...] = jnp.zeros_like(g_normed)

    @pl.when(step < last)
    def _():
        grad = dot(back_low[...], w_back[...], 1, 1) * slope[...].astype(F32)
        b_in[...] = jnp.sum(grad, axis=0, keepdims=True)
        low = grad.astype(BF)
        g_normed[...] += dot(low, w_in[...], 1, 1)
        block = dot(normed_low[...], low, 0, 0)
        for number, send in enumerate(sends):

            @pl.when(step < 2 if number == 0 else step >= 2)
            def _():
                split_cores(meta, block, None, send, keep.shape[0], keep.shape[1])

        split_cores(meta, block, keep, None, keep.shape[0], keep.shape[1])

    @pl.when(step == last)
    def _():
        for copy in copies:
            copy.wait()
        sums[...] = jnp.zeros_like(sums)
        for span in tiles:
            norm, scale = normalise(first[span, :])
            grad = g_normed[span, :] + g_second[span, :]
            sums[0:1, :] += jnp.sum(grad * norm, axis=0, keepdims=True)
            sums[1:2, :] += jnp.sum(grad, axis=0, keepdims=True)
            grad = norm_backward(grad, norm, scale, vec[GAIN_ONE : GAIN_ONE + 1, :])
            sums[2:3, :] += jnp.sum(grad, axis=0, keepdims=True)
            g_first[span, :] = grad
            first_low[span, :] = grad.astype(BF)
        do_t[...] = dot(w_out[...], first_low[...], 1, 1).astype(BF)
        split_cores(meta, dot(att_t[...], first_low[...]), keep, sends[-1], keep.shape[0], keep.shape[1])


def weight_gradients(
    meta, tok_in, two_in, other_in, gq_in, gkv_in, sums_two, sums_one, g_bq, g_bv, g_b_in,
    keep_out, send_out,
    tok, gq_t, gkv_t, tok_t, keep, send, keep_last, send_last, sems, out_sems,
):
    _, size, width = tok.shape
    half_rows = size // 2
    ins = [
        pltpu.make_async_copy(source, target, sems.at[at])
        for at, (source, target) in enumerate(
            [
                (tok_in.at[0], tok.at[0]), (two_in, tok.at[1]), (gq_in, gq_t), (other_in.at[0], tok.at[2]),
                (gkv_in.at[0], gkv_t.at[0]), (gkv_in.at[1], gkv_t.at[1]), (gkv_in.at[2], gkv_t.at[2]),
            ]
        )
    ]
    for copy in ins:
        copy.start()
    groups, own_rows = keep.shape[1], keep.shape[2]

    def outs(section):
        slot = section % 2
        columns = pl.ds(section * width, width)
        return [
            pltpu.make_async_copy(keep.at[slot], keep_out.at[:, :, columns], out_sems.at[2 * slot]),
            pltpu.make_async_copy(send.at[slot], send_out.at[:, :, columns], out_sems.at[2 * slot + 1]),
        ]

    def finish(section, block):
        slot = section % 2
        if section >= 2:
            for copy in outs(section - 2):
                copy.wait()
        split_cores(meta, block, keep.at[slot], send.at[slot], groups, own_rows)
        for copy in outs(section):
            copy.start()

    def turn(at):
        tok_t[:, at * size : (at + 1) * size] = tok[at].T

    vectors = [sums_two[0:3, :], sums_one[0:3, :], g_bq[...], g_bv[...], jnp.zeros((120, width), F32)]
    vectors = jnp.concatenate(vectors, axis=0).T
    per_owner = g_b_in.shape[1] // (2 * groups)
    line = min(64, per_owner)
    bias_rows = []
    for at in range(2 * groups):
        lines = [
            jnp.concatenate(
                [
                    jnp.zeros((1, 64), F32),
                    g_b_in[:, at * per_owner + to : at * per_owner + to + line],
                    jnp.zeros((1, 64 - line), F32),
                ][: 2 + (line < 64)],
                axis=1,
            )
            for to in range(0, per_owner, line)
        ]
        bias_rows.append(jnp.concatenate(lines + [jnp.zeros((own_rows - len(lines), 128), F32)], axis=0))
    split_cores(meta, vectors + jnp.concatenate(bias_rows, axis=0), keep_last, send_last, groups, own_rows)
    last = [
        pltpu.make_async_copy(keep_last, keep_out.at[:, :, pl.ds(3 * width, 128)], out_sems.at[4]),
        pltpu.make_async_copy(send_last, send_out.at[:, :, pl.ds(3 * width, 128)], out_sems.at[5]),
    ]
    for copy in last:
        copy.start()
    for copy in ins[:3]:
        copy.wait()
    turn(0)
    turn(1)
    half = tok_t[:, pl.ds(pl.multiple_of(size + meta[SIDE] * half_rows, half_rows), half_rows)]
    blocks = [dot(tok_t[:, :size], gq_t[:, :size], 1, 1) + dot(half, gq_t[:, size:], 1, 1)]
    for copy in ins[3:]:
        copy.wait()
    turn(2)

    def pair_block(which):
        span = slice(which * width, (which + 1) * width)
        block = dot(tok_t[:, :size], gkv_t[0, span, :], 1, 1)
        block = block + dot(tok_t[:, size : 2 * size], gkv_t[1, span, :], 1, 1)
        return block + dot(tok_t[:, 2 * size :], gkv_t[2, span, :], 1, 1)

    blocks.append(pair_block(0))
    finish(0, blocks[0])
    blocks.append(pair_block(1))
    finish(1, blocks[1])
    finish(2, blocks[2])
    for copy in outs(1) + outs(2) + last:
        copy.wait()


def started(pairs, sems):
    copies = [pltpu.make_async_copy(source, target, sems.at[at]) for at, (source, target) in enumerate(pairs)]
    for copy in copies:
        copy.start()
    return copies


def tokens_sent(
    meta, w_in, gq_in, gkv_in, first_in, sent_out, two_out, w, gq_t, gkv_t, first, sent, two, sems, out_sems
):
    width = w.shape[0]
    size = two.shape[0]
    half_rows = size // 2
    late, early = pl.ds(width, 2 * width), pl.ds(0, width)
    half = pl.ds(size, half_rows)
    ins = started(
        [
            (gkv_in.at[2], gkv_t.at[1]), (w_in.at[:, late], w.at[:, late]), (gkv_in.at[1], gkv_t.at[0]),
            (gq_in.at[:, half], gq_t), (w_in.at[:, early], w.at[:, early]), (first_in.at[half], first),
        ],
        sems,
    )
    for copy in ins[:3]:
        copy.wait()
    other = dot(w[:, width:], gkv_t[1])
    block_two = dot(w[:, width:], gkv_t[0])
    sent[0] = other.astype(BF).T
    outs = started([(sent.at[0], sent_out.at[0])], out_sems)
    for copy in ins[3:]:
        copy.wait()
    from_queries = dot(w[:, :width], gq_t[...])
    two[...] = block_two.T
    span = pl.ds(pl.multiple_of(meta[SIDE] * half_rows, half_rows), half_rows)
    two[span, :] += from_queries.T + first[...]
    sent[1] = two[...].astype(BF)
    for number, pair in enumerate([(sent.at[1], sent_out.at[1]), (two, two_out)]):
        copy = pltpu.make_async_copy(*pair, out_sems.at[1 + number])
        copy.start()
        outs.append(copy)
    for copy in outs:
        copy.wait()


def tokens_kept(
    meta, w_in, gq_in, gkv_in, first_in, came_in, two_in, grad_out, w, gq_t, gkv_t, own, came, two, grad, sems, out_sems
):
    width = w.shape[0]
    size = own.shape[0]
    late, early = pl.ds(width, 2 * width), pl.ds(0, width)
    ins = started(
        [
            (gkv_in.at[0], gkv_t), (w_in.at[:, late], w.at[:, late]), (gq_in.at[:, pl.ds(0, size)], gq_t),
            (w_in.at[:, early], w.at[:, early]), (came_in, came), (two_in, two), (first_in.at[pl.ds(0, size)], own),
        ],
        sems,
    )
    for copy in ins[:2]:
        copy.wait()
    total = dot(w[:, width:], gkv_t[...])
    for copy in ins[2:4]:
        copy.wait()
    total = (total + dot(w[:, :width], gq_t[...])).T
    for copy in ins[4:6]:
        copy.wait()
    grad[1] = jnp.where(meta[SIDE] == 0, two[...] + came[1].astype(F32), 0.0).astype(BF)
    outs = started([(grad.at[1], grad_out.at[1])], out_sems)
    ins[6].wait()
    grad[0] = (total + own[...] + came[0].astype(F32)).astype(BF)
    out = pltpu.make_async_copy(grad.at[0], grad_out.at[0], out_sems.at[1])
    out.start()
    for copy in outs + [out]:
        copy.wait()


def flip(value, axis, bit):
    count = lax.axis_size(axis)
    return lax.ppermute(value, axis, [(at, at ^ bit) for at in range(count)])


def after(value, *others):
    return lax.optimization_barrier((value,) + others)[0]


CORE_SUM, QUAD, PAIR, CORE_TWO, HOP_TWO, JOIN = range(6)


def two_parts(stage, bits, meta, parts, targets):
    if stage == CORE_TWO:
        kept, pieces = parts[0], parts[1:]
        starts = [sum(piece.shape[2] for piece in pieces[:number]) for number in range(len(pieces))]

    first = 0
    for part in range(2):
        outs = targets if stage == JOIN else targets[2 * part : 2 * part + 2]
        bit, place = bits[part]
        mine = (meta[OWNER] >> bit) & 1
        columns = parts[2 * part].shape[2] if stage == JOIN else outs[0].shape[2]
        for flipped, out in enumerate(outs):
            which = 1 - mine if flipped else mine
            for to in range(out.shape[0]):
                index = (((to >> place) << 1) << place) | (to & ((1 << place) - 1))
                index = index + (which << place) if len(outs) > 1 else to
                if stage != CORE_TWO:
                    total = parts[2 * part][index].astype(F32) + parts[2 * part + 1][index].astype(F32)
                    span = slice(first, first + columns) if stage == JOIN else slice(0, columns)
                    out[to, :, span] = total.astype(BF)
                    continue
                for start, piece in zip(starts, pieces):
                    low, high = max(start, first), min(start + piece.shape[2], first + columns)
                    if low < high:
                        total = kept[index, :, low:high].astype(F32)
                        total = total + piece[index, :, low - start : high - start].astype(F32)
                        out[to, :, low - first : high - first] = total.astype(BF)
        first += columns


def combine_kernel(plan, meta, *refs):
    refs = list(refs)
    ins = [[refs.pop(0) for _ in range(count)] for *_, count, _ in plan]
    outs = [[refs.pop(0) for _ in range(count)] for *_, count in plan]
    for (stage, over_x, plane, bit, _, _), parts, targets in zip(plan, ins, outs):
        places = 2**plane
        if stage in (CORE_TWO, HOP_TWO, JOIN):
            two_parts(stage, bit, meta, parts, targets)
            continue
        if stage == CORE_SUM:
            kept, pieces = parts[0], parts[1:]
            (out,) = targets
            columns = kept.shape[2]
            starts = [sum(piece.shape[2] for piece in pieces[:number]) for number in range(len(pieces))]
            for at in range(kept.shape[0]):
                for number, piece in enumerate(pieces):
                    begin, end = starts[number], starts[number] + piece.shape[2]
                    if not over_x:
                        span = slice(begin, end)
                        total = kept[at, :, span].astype(F32) + piece[at].astype(F32)
                        out[at % places, at // places, :, span] = total.astype(BF)
                        continue
                    for side in range(2):
                        low = max(begin, side * columns // 2)
                        high = min(end, (side + 1) * columns // 2)
                        if low < high:
                            total = kept[at, :, low:high].astype(F32)
                            total = total + piece[at, :, low - begin : high - begin].astype(F32)
                            to = slice(low - side * columns // 2, high - side * columns // 2)
                            out[2 * (at % places) + side, at // places, :, to] = total.astype(BF)
            continue

        def total_at(index):
            if stage == QUAD:
                (came,) = parts
                total = came[0, index].astype(F32)
                for at in range(1, came.shape[0]):
                    total = total + came[at, index].astype(F32)
                return total
            kept, came = parts
            return kept[index].astype(F32) + came[index].astype(F32)

        if len(targets) == 1:
            targets[0][...] = total_at(0).astype(BF)
        else:
            mine = (meta[OWNER] >> bit) & 1
            for flipped, out in enumerate(targets):
                which = 1 - mine if flipped else mine
                for to in range(out.shape[0]):
                    out[to] = total_at(2 * to + which).astype(BF)


class Piece:
    def __init__(self, keep, sends, plane, over_x):
        self.over_x = over_x
        self.rows = keep.shape[1]
        self.columns = keep.shape[2] // 2 if over_x else keep.shape[2]
        bits = list(range(1, lax.axis_size("batch").bit_length() - 1))
        self.plane, self.bits = plane, bits[plane:]
        self.stage = CORE_SUM
        self.parts = [keep] + [flip(send, "batch", 1) for send in sends]

    def shapes(self):
        sds = lambda *lead: jax.ShapeDtypeStruct(lead + (self.rows, self.columns), BF)
        if self.stage == CORE_SUM:
            places = 2**self.plane
            return [sds(places * (1 + self.over_x), self.parts[0].shape[0] // places)]
        count = self.parts[0].shape[-3]
        return [sds(count // 2)] * 2 if count > 1 else [sds()]

    def taken(self, results):
        self.sending = results[-1]
        if self.stage == CORE_SUM:
            places = 2**self.plane
            starts = [
                high + core for high in range(0, lax.axis_size("batch"), 2 * places) for core in range(2)
            ]
            if self.over_x:
                groups = [[2 * (start + 2 * place) + side for place in range(places) for side in range(2)] for start in starts]
                came = lax.all_to_all(results[0], ("batch", "blk"), 0, 0, axis_index_groups=groups)
            else:
                groups = [[start + 2 * place for place in range(places)] for start in starts]
                came = lax.all_to_all(results[0], "batch", 0, 0, axis_index_groups=groups)
            self.parts = [came]
            self.stage = QUAD
        elif len(results) == 2:
            self.parts = [results[0], flip(results[1], "batch", 1 << self.bits.pop(0))]
            self.stage = PAIR
        else:
            self.parts = [results[0], flip(results[0], "blk", 1)]
            self.stage = None

    def finish(self, side):
        own, came = self.parts
        if not self.over_x:
            return own.astype(F32) + came.astype(F32)
        return jnp.concatenate([jnp.where(side == 0, own, came), jnp.where(side == 0, came, own)], axis=1).astype(F32)


class TwoPartPiece(Piece):
    def __init__(self, keep, sends, widths):
        self.over_x, self.plane = False, 2
        self.rows, self.columns, self.widths = keep.shape[1], keep.shape[2], widths
        self.all_bits = list(range(1, lax.axis_size("batch").bit_length() - 1))
        self.bits = self.all_bits[2:]
        self.stage = CORE_TWO
        self.parts = [keep] + [flip(send, "batch", 1) for send in sends]

    def shapes(self):
        sds = jax.ShapeDtypeStruct
        if self.stage in (CORE_TWO, HOP_TWO):
            count = self.parts[0].shape[0] // 2
            return [sds((count, self.rows, width), BF) for width in self.widths for _ in range(2)]
        count = self.parts[0].shape[0]
        if self.stage == JOIN:
            shape = (count // 2, self.rows, self.columns)
            return [sds(shape, BF)] * 2 if count > 1 else [sds((1,) + shape[1:], BF)]
        return super().shapes()

    def turn(self):
        first, second = self.all_bits[:2]
        if self.stage == CORE_TWO:
            return [(first, 0), (second, 1)]
        if self.stage == HOP_TWO:
            return [(second, 0), (first, 0)]
        return [(self.bits[0] if self.bits else 0, 0)] * 2

    def taken(self, results):
        if self.stage in (CORE_TWO, HOP_TWO):
            (bit_a, _), (bit_b, _) = self.turn()
            keep_a, send_a, keep_b, send_b = results
            self.sending = send_b
            self.parts = [keep_a, flip(send_a, "batch", 1 << bit_a), keep_b, flip(send_b, "batch", 1 << bit_b)]
            self.stage = HOP_TWO if self.stage == CORE_TWO else JOIN
        else:
            super().taken(results)


def take(meta, pieces, *order_after):
    operands, plan, shapes = [], [], []
    for piece in pieces:
        piece.parts = list(lax.optimization_barrier(tuple(piece.parts) + order_after)[: len(piece.parts)])
        made = piece.shapes()
        bit = piece.bits[0] if piece.bits else 0
        if piece.stage in (CORE_TWO, HOP_TWO, JOIN):
            bit = piece.turn()
        plan.append((piece.stage, piece.over_x, piece.plane, bit, len(piece.parts), len(made)))
        operands += piece.parts
        shapes += made
    vmem = pl.BlockSpec(memory_space=pltpu.VMEM)
    out = pl.pallas_call(
        functools.partial(combine_kernel, plan),
        in_specs=[pl.BlockSpec(memory_space=pltpu.SMEM)] + [vmem] * len(operands),
        out_specs=[vmem] * len(shapes),
        out_shape=shapes,
        compiler_params=params(28),
        cost_estimate=cost(1, 1),
        name="combine",
    )(meta, *operands)
    for piece, (*_, count) in zip(pieces, plan):
        piece.taken(out[:count])
        out = out[count:]
    return tuple(part for piece in pieces for part in piece.parts[:1] if piece.stage != QUAD)


def local(
    tokens, cotangent, counts, perms, key_mask, w_qkv, bias_q, bias_v, w_out, bias_out, gain_one, shift_one,
    w_in, bias_in, w_back, bias_back, gain_two, shift_two,
):
    _, _, size, width = tokens.shape
    heads = perms.shape[1]
    hidden = w_in.shape[1]
    half_rows = size // 2
    total = size + half_rows
    owners = lax.axis_size("batch")
    side = lax.axis_index("blk").astype(jnp.int32)
    owner = lax.axis_index("batch").astype(jnp.int32)
    whole = lambda *shape: once(shape, lambda *_: (0,) * len(shape))
    sds = jax.ShapeDtypeStruct
    anywhere = pl.BlockSpec(memory_space=pl.ANY)
    smem = pl.BlockSpec(memory_space=pltpu.SMEM)

    tok = tokens[0]
    came = flip(tok, "blk", 1)

    count = counts[0]
    lookup = jnp.where(count == 2, perms[0], perms[1])
    own = jnp.where(side == 0, lookup[:, 0], lookup[:, 1])
    two = jnp.where(count > 2, lookup[:, 2], 2)
    source = jnp.concatenate([own, two])
    place = jnp.where(source == 2, 1, jnp.where(source == side, 0, 2))
    live = jnp.stack([(side < count).astype(jnp.int32), (count > 2).astype(jnp.int32)])
    meta = jnp.concatenate([jnp.stack([side, owner & 1]), live, owner[None], place])
    vec = jnp.concatenate([bias_q, bias_v, bias_out, gain_one, shift_one, bias_back, gain_two, shift_two]).reshape(8, width)
    own_mask = key_mask[0]

    def grid_spec(grid, in_specs, out_specs, scratch=()):
        return pltpu.PrefetchScalarGridSpec(
            num_scalar_prefetch=1, grid=grid, in_specs=in_specs, out_specs=out_specs, scratch_shapes=list(scratch)
        )

    slot = lambda at: once((None, size, width), lambda *_: (at, 0, 0))
    all_rows = whole(total, width)
    vectors = whole(8, width)
    own_q, own_k, own_v, own_mb = pl.pallas_call(
        project_own,
        grid_spec=grid_spec(
            (3,),
            [slot(0), whole(1, size), pl.BlockSpec((width, width), lambda i, m: (0, i)), vectors],
            [whole(width, size), whole(size, width), whole(width, size), whole(size, 128)],
        ),
        out_shape=[sds((width, size), BF), sds((size, width), BF), sds((width, size), BF), sds((size, 128), F32)],
        compiler_params=params(60),
        cost_estimate=cost(1e9, 1),
        name="project_own",
    )(meta, tok, own_mask[0:1], w_qkv, vec)
    other_mask = flip(after(own_mask, own_mb), "blk", 1)
    masks = jnp.stack([jnp.where(side == 0, own_mask[1], other_mask[1]), other_mask[0]])
    cot = cotangent[0]
    cot_came = lax.ppermute(after(cot[1, half_rows:], came), "blk", [(0, 1)])

    each = 4
    span = each * width // heads
    some_q = pl.BlockSpec((span, total), lambda p, m: (p, 0))
    some_rows = pl.BlockSpec((3, size, span), lambda p, m: (0, 0, p))
    some_cols = pl.BlockSpec((3, span, size), lambda p, m: (0, p, 0))
    some_probs = pl.BlockSpec((each, size, total), lambda p, m: (p, 0, 0))
    some_inv = pl.BlockSpec((1, each, total), lambda p, m: (p, 0, 0))
    probs, att, att_t, inv, q_t, k, v_t, tok_two = pl.pallas_call(
        functools.partial(attention_forward, heads),
        grid_spec=grid_spec(
            (heads // each,),
            [whole(2, size), vectors] + [anywhere] * 7,
            [some_probs, pl.BlockSpec((total, span), lambda p, m: (0, p)), some_q, some_inv] + [anywhere] * 4,
            [
                pltpu.VMEM((width, total), BF), pltpu.VMEM((3, size, width), BF), pltpu.VMEM((3, width, size), BF),
                pltpu.VMEM((3, size, 128), F32), pltpu.VMEM((width, 3 * width), BF), pltpu.VMEM((2 * size, width), BF),
                pltpu.SemaphoreType.DMA((9,)), pltpu.SemaphoreType.DMA((4,)),
            ],
        ),
        out_shape=[
            sds((heads, size, total), BF), sds((total, width), BF), sds((width, total), BF),
            sds((heads // each, each, total), F32), sds((width, total), BF), sds((3, size, width), BF), sds((3, width, size), BF),
            sds((size, width), BF),
        ],
        compiler_params=params(60),
        cost_estimate=cost(1e11, 1),
        name="attention_forward",
    )(meta, masks, vec, tok, came, w_qkv, own_q, own_k, own_v, own_mb)

    chunk = 1024
    steps = hidden // chunk
    back_steps = 4
    half = owners // 2
    back_rows = hidden // owners
    back_half = pl.BlockSpec((half // back_steps, back_rows, width), lambda i, m: (jnp.maximum(i - steps, 0), 0, 0))
    flat = lambda dtype, columns=width: sds((total, columns), dtype)
    early = lambda i: jnp.minimum(i, steps - 1)
    side_rows = once((half_rows, width), lambda i, m: (m[SIDE], 0))
    slope, back_keep, back_send, sums_two, first, normed_low, mixed, mixed_two, g_second, back_low = pl.pallas_call(
        functools.partial(rows_forward, steps),
        grid_spec=grid_spec(
            (steps + back_steps,),
            [
                slot(0), side_rows, all_rows, slot(0), once((None, half_rows, width), lambda i, m: (1, 0, 0)),
                whole(half_rows, width), whole(width, width), vectors,
                pl.BlockSpec((width, chunk), lambda i, m: (0, early(i))),
                pl.BlockSpec((1, chunk), lambda i, m: (0, early(i))),
                pl.BlockSpec((chunk, width), lambda i, m: (early(i), 0)),
            ],
            [
                pl.BlockSpec((total, chunk), lambda i, m: (0, early(i))),
                back_half, back_half, whole(8, width),
            ]
            + [anywhere] * 6,
            [
                pltpu.VMEM((total, width), F32), pltpu.VMEM((total, width), BF), pltpu.VMEM((total, width), BF),
                pltpu.VMEM((total, width), F32), pltpu.VMEM((total, width), BF), pltpu.VMEM((total, hidden), BF),
                pltpu.SemaphoreType.DMA((6,)),
            ],
        ),
        out_shape=[
            flat(BF, hidden), sds((half, back_rows, width), BF), sds((half, back_rows, width), BF),
            sds((8, width), F32), flat(F32), flat(BF),
            sds((size, width), BF), sds((half_rows, width), BF), flat(F32), flat(BF),
        ],
        compiler_params=params(60),
        cost_estimate=cost(1e11, 1),
        name="rows_forward",
    )(
        meta, tok, tok_two, att, cot, cot, cot_came, w_out, vec, w_in, bias_in.reshape(1, hidden), w_back,
    )

    back = Piece(back_keep, [back_send], 2, True)
    mixed_came = lax.ppermute(mixed_two, "blk", [(1, 0)])
    take(meta, [back])
    mixed_came, back_low = lax.optimization_barrier((mixed_came, back_low, back.sending))[:2]

    own_rows = width // owners
    in_steps = hidden // width
    in_early = lambda i: jnp.minimum(i, in_steps - 1)
    in_half = pl.BlockSpec((half, own_rows, width), lambda i, m: (0, 0, i))
    in_keep, *rest = pl.pallas_call(
        rows_backward,
        grid_spec=grid_spec(
            (in_steps + 1,),
            [
                all_rows, all_rows, pl.BlockSpec((total, width), lambda i, m: (0, in_early(i))),
                pl.BlockSpec((width, width), lambda i, m: (0, in_early(i))),
                pl.BlockSpec((width, width), lambda i, m: (in_early(i), 0)),
                whole(width, width), vectors, anywhere, anywhere, anywhere,
            ],
            [
                in_half,
                pl.BlockSpec((half, own_rows, width), lambda i, m: (0, 0, jnp.minimum(i, 1))),
                pl.BlockSpec((half, own_rows, width), lambda i, m: (0, 0, jnp.maximum(i - 2, 0))),
                all_rows, all_rows, whole(width, total),
                pl.BlockSpec((1, width), lambda i, m: (0, in_early(i))), whole(8, width),
            ],
            [
                pltpu.VMEM((total, width), F32), pltpu.VMEM((total, width), F32), pltpu.VMEM((total, width), F32),
                pltpu.VMEM((width, total), BF), pltpu.SemaphoreType.DMA((3,)),
            ],
        ),
        out_shape=[
            sds((half, own_rows, hidden + width), BF), sds((half, own_rows, 2 * width), BF),
            sds((half, own_rows, (in_steps - 1) * width), BF), flat(F32),
            flat(BF),
            sds((width, total), BF), sds((1, hidden), F32), sds((8, width), F32),
        ],
        compiler_params=params(60),
        cost_estimate=cost(1e11, 1),
        name="rows_backward",
    )(meta, back_low, normed_low, slope, w_in, w_back, w_out, vec, first, g_second, att_t)
    in_sends, (g_first, first_low, do_t, g_b_in, sums_one) = rest[:-5], rest[-5:]
    inner = Piece(in_keep, in_sends, 2, True)
    take(meta, [inner, back], do_t)
    do_t = after(do_t, inner.sending, back.sending)
    gq_shapes = [
        sds((width, total), BF), sds((3, 2, width, size), BF), sds((1, width), F32), sds((1, width), F32),
    ]

    gq_t, gkv_t, g_bq, g_bv = pl.pallas_call(
        functools.partial(attention_backward, heads),
        grid_spec=grid_spec(
            (heads // each,),
            [some_probs, some_rows, some_cols, some_q, some_q, some_q, some_inv],
            [some_q, pl.BlockSpec((3, 2, span, size), lambda p, m: (0, 0, p, 0))]
            + [pl.BlockSpec((1, span), lambda p, m: (0, p))] * 2,
            [
                pltpu.VMEM((3, span, size), F32), pltpu.VMEM((3, span, size), F32), pltpu.VMEM((span, total), F32),
                pltpu.VMEM((3, span, size), BF), pltpu.VMEM((3, size, span), BF),
            ],
        ),
        out_shape=gq_shapes,
        compiler_params=params(60),
        cost_estimate=cost(1e11, 1),
        name="attention_backward",
    )(meta, probs, k, v_t, q_t, do_t, att_t, inv)
    gkv_t = gkv_t.reshape(3, 2 * width, size)

    own_size, half_size = (width, size), (width, half_rows)
    sent, two_own = pl.pallas_call(
        tokens_sent,
        in_specs=[smem] + [anywhere] * 4,
        out_specs=[anywhere] * 2,
        out_shape=[sds((2, size, width), BF), sds((size, width), F32)],
        scratch_shapes=[
            pltpu.VMEM((width, 3 * width), BF), pltpu.VMEM(half_size, BF), pltpu.VMEM((2, 2 * width, size), BF),
            pltpu.VMEM((half_rows, width), F32), pltpu.VMEM((2, size, width), BF), pltpu.VMEM((size, width), F32),
            pltpu.SemaphoreType.DMA((6,)), pltpu.SemaphoreType.DMA((3,)),
        ],
        compiler_params=params(60),
        cost_estimate=cost(1e9, 1),
        name="tokens_sent",
    )(meta, w_qkv, gq_t, gkv_t, g_first)
    came_grad = flip(sent, "blk", 1)
    gq_t = after(gq_t, sent)

    columns = 3 * width + 128
    vmem = pl.BlockSpec(memory_space=pltpu.VMEM)
    run_weights = pl.pallas_call(
        weight_gradients,
        in_specs=[pl.BlockSpec(memory_space=pltpu.SMEM)] + [anywhere] * 5 + [vmem] * 5,
        out_specs=[anywhere] * 2,
        scratch_shapes=[
            pltpu.VMEM((3, size, width), BF), pltpu.VMEM((width, total), BF), pltpu.VMEM((3, 2 * width, size), BF),
            pltpu.VMEM((width, 3 * size), BF),
            pltpu.VMEM((2, half, own_rows, width), BF), pltpu.VMEM((2, half, own_rows, width), BF),
            pltpu.VMEM((half, own_rows, 128), BF), pltpu.VMEM((half, own_rows, 128), BF),
            pltpu.SemaphoreType.DMA((7,)), pltpu.SemaphoreType.DMA((6,)),
        ],
        out_shape=[sds((half, own_rows, columns), BF)] * 2,
        compiler_params=params(60),
        cost_estimate=cost(1e9, 1),
        name="weight_gradients",
    )
    last_keep, last_send = run_weights(
        meta, tok, tok_two, came, gq_t, gkv_t, sums_two, sums_one, g_bq, g_bv, g_b_in
    )
    last = TwoPartPiece(last_keep, [last_send], [1280, columns - 1280])
    take(meta, [last, inner], last_keep)
    take(meta, [last], inner.sending)
    take(meta, [last, inner, back], last.sending)
    tokens_grad = pl.pallas_call(
        tokens_kept,
        in_specs=[smem] + [anywhere] * 6,
        out_specs=anywhere,
        out_shape=sds((2, size, width), BF),
        scratch_shapes=[
            pltpu.VMEM((width, 3 * width), BF), pltpu.VMEM(own_size, BF), pltpu.VMEM((2 * width, size), BF),
            pltpu.VMEM((size, width), F32), pltpu.VMEM((2, size, width), BF), pltpu.VMEM((size, width), F32),
            pltpu.VMEM((2, size, width), BF), pltpu.SemaphoreType.DMA((7,)), pltpu.SemaphoreType.DMA((2,)),
        ],
        compiler_params=params(60),
        cost_estimate=cost(1e11, 1),
        name="tokens_kept",
    )(meta, w_qkv, after(gq_t, last.sending), gkv_t, g_first, came_grad, two_own)
    take(meta, [last], tokens_grad, back.parts[1], inner.parts[1])
    for piece in (last, inner, back):
        while piece.stage is not None:
            take(meta, [piece])

    out_back = back.finish(side)
    out_in = inner.finish(side)
    own_last, came_last = last.parts
    both = lambda columns: own_last[:, columns].astype(F32) + came_last[:, columns].astype(F32)
    out_qkv, out_vectors = both(slice(0, 3 * width)), both(slice(3 * width, columns))

    mixed_other = jnp.where(side == 0, jnp.concatenate([mixed_two, mixed_came]), jnp.zeros((), BF))
    mixed_all = jnp.stack([mixed, mixed_other])[None]
    pick = lambda at: out_vectors[:, at]
    line = min(64, back_rows)
    return (
        mixed_all, tokens_grad[None],
        out_qkv, pick(6), pick(7), out_in[:, hidden:], pick(5), pick(3), pick(4),
        out_in[:, :hidden], out_vectors[: back_rows // line, 64 : 64 + line].reshape(-1), out_back, pick(2), pick(0),
        pick(1),
    )


def solution(mesh):
    split = P("batch", None, "blk", None)
    in_specs = (split, split, P("batch"), P(), P("batch", None, "blk")) + (P(),) * 13
    matrix, vector = P("batch", None), P("batch")
    out_specs = (
        split, split, matrix, vector, vector, matrix, vector, vector, vector, matrix, vector, matrix, vector, vector,
        vector,
    )
    return jax.shard_map(local, mesh=mesh, in_specs=in_specs, out_specs=out_specs, check_vma=False)
```

```python
import functools
import math

import jax
import jax.numpy as jnp
from jax import lax
from jax.experimental import pallas as pl
from jax.experimental.pallas import tpu as pltpu
from jax.sharding import PartitionSpec as P

EPSILON = 1e-05
BF = jnp.bfloat16
F32 = jnp.float32
MIB = 1024 * 1024
NEGATIVE = -1e30

SIDE, CORE, LIVE, OWNER, SOURCE = 0, 1, 2, 4, 5


def dot(a, b, ca=1, cb=0):
    return lax.dot_general(a, b, (((ca,), (cb,)), ((), ())), preferred_element_type=F32)


def params(mebibytes):
    return pltpu.CompilerParams(vmem_limit_bytes=mebibytes * MIB)


def cost(flops, read):
    return pl.CostEstimate(flops=int(flops), bytes_accessed=int(read), transcendentals=0)


def once(shape, index):
    return pl.BlockSpec(shape, index, pipeline_mode=pl.Buffered(1))


def mask_columns(mask_row):
    penalty = jnp.where(mask_row == 0, NEGATIVE, 0.0).astype(F32)
    return jnp.broadcast_to(penalty, (128, penalty.shape[1])).T


def project_own(meta, tok, mask, w, vec, q_t, k, v_t, mb):
    step = pl.program_id(0)
    rows = tok[...]

    @pl.when(step == 0)
    def _():
        queries = (dot(rows, w[...]) + vec[0:1, :]).astype(BF)
        q_t[...] = (queries * 0.125).T
        mb[...] = mask_columns(mask[...])

    @pl.when(step == 1)
    def _():
        k[...] = dot(rows, w[...]).astype(BF)

    @pl.when(step == 2)
    def _():
        v_t[...] = (dot(rows, w[...]) + vec[1:2, :]).astype(BF).T


def pad_pair(part, head):
    zeros = jnp.zeros_like(part)
    return jnp.concatenate([part, zeros] if head % 2 == 0 else [zeros, part], axis=0)


def units(heads, each, size, total, meta):
    first = pl.program_id(0) * each
    out = []
    for head in range(each):
        for slot, queries in enumerate((slice(0, size), slice(size, total))):
            source = meta[SOURCE + slot * heads + first + head]
            out.append((head, slice(64 * head, 64 * head + 64), queries, source))
    return out


def project_others(meta, vec, masks, starts, ins, k, v_t, q_t, mb, w, rows):
    size, width = k.shape[1:]
    half_rows = size // 2
    own_two, partner_two = starts

    @pl.when(meta[SIDE] == 0)
    def _():
        own_two.start()

    @pl.when(meta[SIDE] == 1)
    def _():
        partner_two.start()

    for copy in ins:
        copy.start()
    mb[1] = mask_columns(masks[0:1, :])
    mb[2] = mask_columns(masks[1:2, :])
    own_two.wait()
    for copy in ins[:2]:
        copy.wait()
    keys = dot(rows[...], w[:, width : 2 * width]).astype(BF)
    k[1] = keys[:size]
    k[2] = keys[size:]
    ins[2].wait()
    values = (dot(rows[...], w[:, 2 * width :]) + vec[1:2, :]).astype(BF)
    ins[3].wait()
    mine = rows[pl.ds(pl.multiple_of(meta[SIDE] * half_rows, half_rows), half_rows), :]
    queries = (dot(mine, w[:, :width]) + vec[0:1, :]).astype(BF) * 0.125
    v_t[1] = values[:size].T
    v_t[2] = values[size:].T
    q_t[:, size:] = queries.T
    for copy in ins[4:]:
        copy.wait()


def attention_forward(
    heads, meta, masks, vec, tok_in, came_in, w_in, q_own, k_own, v_own, mb_own,
    probs, att, att_t, inv, q_out, k_out, v_out, two_out,
    q_t, k, v_t, mb, w, rows, sems, out_sems,
):
    size, total = k.shape[1], q_t.shape[1]
    width = k.shape[2]
    step = pl.program_id(0)
    copy = pltpu.make_async_copy
    outs = [
        copy(source, target, out_sems.at[at])
        for at, (source, target) in enumerate(((q_t, q_out), (k, k_out), (v_t, v_out), (rows.at[pl.ds(0, size)], two_out)))
    ]

    @pl.when(step == 0)
    def _():
        columns = [slice(width, 2 * width), slice(2 * width, 3 * width), slice(0, width)]
        two = rows.at[pl.ds(0, size)]
        starts = [copy(tok_in.at[1], two, sems.at[0]), copy(came_in.at[1], two, sems.at[0])]
        ins = [
            copy(w_in.at[:, columns[0]], w.at[:, columns[0]], sems.at[1]),
            copy(came_in.at[0], rows.at[pl.ds(size, size)], sems.at[2]),
            copy(w_in.at[:, columns[1]], w.at[:, columns[1]], sems.at[3]),
            copy(w_in.at[:, columns[2]], w.at[:, columns[2]], sems.at[4]),
            copy(q_own, q_t.at[:, pl.ds(0, size)], sems.at[5]),
            copy(k_own, k.at[0], sems.at[6]),
            copy(v_own, v_t.at[0], sems.at[7]),
            copy(mb_own, mb.at[0], sems.at[8]),
        ]
        project_others(meta, vec, masks, starts, ins, k, v_t, q_t, mb, w, rows)
        for out in outs:
            out.start()

    todo = units(heads, probs.shape[0], size, total, meta)
    each = att_t.shape[0]

    def lanes_of(head):
        return pl.ds(pl.multiple_of(step * each + head // 2 * 128, 128), 128)

    def rows_of(span):
        return pl.ds(pl.multiple_of(step * each + span.start, 64), 64)

    def score(unit):
        half, span, queries, source = unit
        return dot(k[source, :, lanes_of(half)], pad_pair(q_t[rows_of(span), queries], half))

    def soften(unit, scores):
        half, span, queries, source = unit
        scores = scores + jnp.concatenate([mb[source]] * (scores.shape[1] // 128), axis=1)
        weights = jnp.exp(scores - jnp.max(scores, axis=0, keepdims=True))
        inverse = 1.0 / jnp.sum(weights, axis=0, keepdims=True)
        low = weights.astype(BF)
        probs[half, :, queries] = low
        inv[0, half : half + 1, queries] = inverse
        return low, inverse

    def attend(unit, soft):
        half, span, queries, source = unit
        att_t[span, queries] = (dot(v_t[source, rows_of(span), :], soft[0]) * soft[1]).astype(BF)

    scores = {0: score(todo[0])}
    soft = {}
    for at in range(len(todo) + 1):
        if at + 1 < len(todo):
            scores[at + 1] = score(todo[at + 1])
        if at < len(todo):
            soft[at] = soften(todo[at], scores.pop(at))
        if at > 0:
            attend(todo[at - 1], soft.pop(at - 1))
    att[...] = att_t[...].T

    @pl.when(step == pl.num_programs(0) - 1)
    def _():
        for out in outs:
            out.wait()


def lane_sums(block):
    width = block.shape[1]
    part = block[:, :128]
    for at in range(128, width, 128):
        part = part + block[:, at : at + 128]
    return jnp.sum(part.T, axis=0, keepdims=True)


def attention_backward(
    heads, meta, probs, k, v_t, q_t, do_t, att_t, inv, gq_t, gkv_t, bq, bv, sum_k, sum_v, sum_q, k_t, v
):
    size, total = k.shape[1], q_t.shape[1]
    for at in range(3):
        k_t[at] = k[at].T
        v[at] = v_t[at].T
    todo = units(heads, probs.shape[0], size, total, meta)
    sum_k[...] = jnp.zeros_like(sum_k)
    sum_v[...] = jnp.zeros_like(sum_v)

    def begin(unit):
        half, span, queries, source = unit
        scaled = do_t[span, queries].astype(F32) * inv[0, half : half + 1, queries]
        delta = jnp.sum(scaled * att_t[span, queries].astype(F32), axis=0, keepdims=True)
        scaled = scaled.astype(BF)
        return scaled, delta, dot(v[source, :, 128 * (half // 2) : 128 * (half // 2) + 128], pad_pair(scaled, half))

    def middle(unit, begun):
        half, span, queries, source = unit
        scaled, delta, grad_probs = begun
        low = probs[half, :, queries]
        sum_v[source, span, :] += dot(scaled, low, 1, 1)
        return (low.astype(F32) * (grad_probs - delta)).astype(BF)

    def end(unit, grad_scores):
        half, span, queries, source = unit
        sum_k[source, span, :] += dot(q_t[span, queries], grad_scores, 1, 1)
        grad_q = dot(k_t[source, span, :], grad_scores) * 0.125
        sum_q[span, queries] = grad_q
        gq_t[span, queries] = grad_q.astype(BF)

    begun = {0: begin(todo[0])}
    grads = {}
    for at in range(len(todo) + 1):
        if at + 1 < len(todo):
            begun[at + 1] = begin(todo[at + 1])
        if at < len(todo):
            grads[at] = middle(todo[at], begun.pop(at))
        if at > 0:
            end(todo[at - 1], grads.pop(at - 1))
    gkv_t[:, 0] = sum_k[...].astype(BF)
    gkv_t[:, 1] = sum_v[...].astype(BF)
    bq[...] = lane_sums(sum_q[...])
    bv[...] = lane_sums(sum_v[0] + sum_v[1] + sum_v[2])


def normalise(rows):
    centred = rows - jnp.mean(rows, axis=-1, keepdims=True)
    scale = lax.rsqrt(jnp.mean(centred * centred, axis=-1, keepdims=True) + EPSILON)
    return centred * scale, scale


def norm_backward(grad, norm, scale, gain):
    scaled = grad * gain
    mean = jnp.mean(scaled, axis=-1, keepdims=True)
    along = jnp.mean(scaled * norm, axis=-1, keepdims=True)
    return scale * (scaled - mean - norm * along)


def gelu_pair(u):
    below = 0.5 + 0.5 * lax.erf(u * math.sqrt(0.5))
    bell = jnp.exp2((-0.5 * math.log2(math.e)) * (u * u)) * (1.0 / math.sqrt(2.0 * math.pi))
    return u * below, below + u * bell


B_OUT, GAIN_ONE, SHIFT_ONE, B_BACK, GAIN_TWO, SHIFT_TWO = 2, 3, 4, 5, 6, 7


def tiles_of(total, tile):
    return [slice(at, at + tile) for at in range(0, total, tile)]


def split_cores(meta, block, keep, send, groups, rows):
    mine = meta[CORE]
    for at in range(groups):
        low = block[2 * at * rows : (2 * at + 1) * rows]
        high = block[(2 * at + 1) * rows : (2 * at + 2) * rows]
        if keep is not None:
            keep[at] = jnp.where(mine == 0, low, high).astype(BF)
        if send is not None:
            send[at] = jnp.where(mine == 0, high, low).astype(BF)


def rows_forward(
    steps, meta, tok, two_half, att, cot, cot_half, cot_came, w_out, vec, w_in, b_in, w_back,
    slope, keep, send, sums, first_out, normed_out, mixed_out, mixed_two_out, second_out, back_out,
    first, normed_low, mixed, second, back_low, active, sems,
):
    step = pl.program_id(0)
    total = att.shape[0]
    tile = two_half.shape[0]
    size = total - tile
    chunk = w_in.shape[1]
    tiles = tiles_of(total, tile)
    copies = [
        pltpu.make_async_copy(source, target, sems.at[at])
        for at, (source, target) in enumerate(
            (
                (first, first_out), (normed_low, normed_out), (mixed.at[pl.ds(0, size)], mixed_out),
                (mixed.at[pl.ds(size, tile)], mixed_two_out), (second, second_out), (back_low, back_out),
            )
        )
    ]

    @pl.when(step == 0)
    def _():
        for at, span in enumerate(tiles):
            rows = (tok[span, :] if at + 1 < len(tiles) else two_half[...]).astype(F32)
            rows = rows + dot(att[span, :], w_out[...]) + vec[B_OUT : B_OUT + 1, :]
            first[span, :] = rows
            result = normalise(rows)[0] * vec[GAIN_ONE : GAIN_ONE + 1, :] + vec[SHIFT_ONE : SHIFT_ONE + 1, :]
            normed_low[span, :] = result.astype(BF)
            second[span, :] = result + vec[B_BACK : B_BACK + 1, :]
        copies[0].start()
        copies[1].start()

    @pl.when(step < steps)
    def _():
        hidden = dot(normed_low[...], w_in[...]) + b_in[...]
        value, grad = gelu_pair(hidden)
        value = value.astype(BF)
        active[:, pl.ds(pl.multiple_of(step * chunk, chunk), chunk)] = value
        slope[...] = grad.astype(BF)
        second[...] += dot(value, w_back[...])

    @pl.when(step == steps - 1)
    def _():
        sums[...] = jnp.zeros_like(sums)
        gain, shift = vec[GAIN_TWO : GAIN_TWO + 1, :], vec[SHIFT_TWO : SHIFT_TWO + 1, :]
        for at, span in enumerate(tiles):
            last = at + 1 == len(tiles)
            live = meta[LIVE + last].astype(F32)
            norm, scale = normalise(second[span, :])
            mixed[span, :] = ((norm * gain + shift) * live).astype(BF)
            cotangent = jnp.where(meta[SIDE] == 0, cot_half[...], cot_came[...]) if last else cot[span, :]
            grad = cotangent.astype(F32) * live
            sums[0:1, :] += jnp.sum(grad * norm, axis=0, keepdims=True)
            sums[1:2, :] += jnp.sum(grad, axis=0, keepdims=True)
            grad = norm_backward(grad, norm, scale, gain)
            sums[2:3, :] += jnp.sum(grad, axis=0, keepdims=True)
            second[span, :] = grad
            back_low[span, :] = grad.astype(BF)
        for copy in copies[2:]:
            copy.start()

    @pl.when(step >= steps)
    def _():
        groups, rows, _ = keep.shape
        columns = 2 * groups * rows
        part = active[:, pl.ds(pl.multiple_of((step - steps) * columns, columns), columns)]
        split_cores(meta, dot(part, back_low[...], 0, 0), keep, send, groups, rows)

    @pl.when(step == pl.num_programs(0) - 1)
    def _():
        for copy in copies:
            copy.wait()


def rows_backward(
    meta, back_low, normed_low, slope, w_in, w_back, vec, first_in, second_in, att_in, w_out_in,
    keep, send_a, send_b, b_in, sums, first_out, do_out,
    first, g_normed, g_second, att_t, g_first, first_low, do_t, w_out, sems, out_sems,
):
    sends = (send_a, send_b)
    step = pl.program_id(0)
    last = pl.num_programs(0) - 1
    total = back_low.shape[0]
    tiles = tiles_of(total, total // 3)
    copies = [
        pltpu.make_async_copy(first_in, first, sems.at[0]),
        pltpu.make_async_copy(second_in, g_second, sems.at[1]),
        pltpu.make_async_copy(att_in, att_t, sems.at[2]),
        pltpu.make_async_copy(w_out_in, w_out, sems.at[3]),
    ]

    @pl.when(step == 0)
    def _():
        for copy in copies:
            copy.start()
        g_normed[...] = jnp.zeros_like(g_normed)

    @pl.when(step < last)
    def _():
        grad = dot(back_low[...], w_back[...], 1, 1) * slope[...].astype(F32)
        b_in[...] = jnp.sum(grad, axis=0, keepdims=True)
        low = grad.astype(BF)
        g_normed[...] += dot(low, w_in[...], 1, 1)
        block = dot(normed_low[...], low, 0, 0)
        for number, send in enumerate(sends):

            @pl.when(step < 2 if number == 0 else step >= 2)
            def _():
                split_cores(meta, block, None, send, keep.shape[0], keep.shape[1])

        split_cores(meta, block, keep, None, keep.shape[0], keep.shape[1])

    @pl.when(step == last)
    def _():
        for copy in copies:
            copy.wait()
        sums[...] = jnp.zeros_like(sums)
        for span in tiles:
            norm, scale = normalise(first[span, :])
            grad = g_normed[span, :] + g_second[span, :]
            sums[0:1, :] += jnp.sum(grad * norm, axis=0, keepdims=True)
            sums[1:2, :] += jnp.sum(grad, axis=0, keepdims=True)
            grad = norm_backward(grad, norm, scale, vec[GAIN_ONE : GAIN_ONE + 1, :])
            sums[2:3, :] += jnp.sum(grad, axis=0, keepdims=True)
            g_first[span, :] = grad
            first_low[span, :] = grad.astype(BF)
        outs = [pltpu.make_async_copy(g_first, first_out, out_sems.at[0]), pltpu.make_async_copy(do_t, do_out, out_sems.at[1])]
        outs[0].start()
        do_t[...] = dot(w_out[...], first_low[...], 1, 1).astype(BF)
        outs[1].start()
        split_cores(meta, dot(att_t[...], first_low[...]), keep, sends[-1], keep.shape[0], keep.shape[1])
        for out in outs:
            out.wait()


def weight_gradients(
    meta, tok_in, two_in, other_in, gq_in, gkv_in, sums_two, sums_one, g_bq, g_bv, g_b_in,
    keep_out, send_out,
    tok, gq_t, gkv_t, tok_t, keep, send, keep_last, send_last, sems, out_sems,
):
    _, size, width = tok.shape
    half_rows = size // 2
    ins = [
        pltpu.make_async_copy(source, target, sems.at[at])
        for at, (source, target) in enumerate(
            [
                (tok_in.at[0], tok.at[0]), (two_in, tok.at[1]), (gq_in, gq_t), (other_in.at[0], tok.at[2]),
                (gkv_in.at[0], gkv_t.at[0]), (gkv_in.at[1], gkv_t.at[1]), (gkv_in.at[2], gkv_t.at[2]),
            ]
        )
    ]
    for copy in ins:
        copy.start()
    groups, own_rows = keep.shape[1], keep.shape[2]

    def outs(section):
        slot = section % 2
        columns = pl.ds(section * width, width)
        return [
            pltpu.make_async_copy(keep.at[slot], keep_out.at[:, :, columns], out_sems.at[2 * slot]),
            pltpu.make_async_copy(send.at[slot], send_out.at[:, :, columns], out_sems.at[2 * slot + 1]),
        ]

    def finish(section, block):
        slot = section % 2
        if section >= 2:
            for copy in outs(section - 2):
                copy.wait()
        split_cores(meta, block, keep.at[slot], send.at[slot], groups, own_rows)
        for copy in outs(section):
            copy.start()

    def turn(at):
        tok_t[:, at * size : (at + 1) * size] = tok[at].T

    vectors = [sums_two[0:3, :], sums_one[0:3, :], g_bq[...], g_bv[...], jnp.zeros((120, width), F32)]
    vectors = jnp.concatenate(vectors, axis=0).T
    per_owner = g_b_in.shape[1] // (2 * groups)
    line = min(64, per_owner)
    bias_rows = []
    for at in range(2 * groups):
        lines = [
            jnp.concatenate(
                [
                    jnp.zeros((1, 64), F32),
                    g_b_in[:, at * per_owner + to : at * per_owner + to + line],
                    jnp.zeros((1, 64 - line), F32),
                ][: 2 + (line < 64)],
                axis=1,
            )
            for to in range(0, per_owner, line)
        ]
        bias_rows.append(jnp.concatenate(lines + [jnp.zeros((own_rows - len(lines), 128), F32)], axis=0))
    split_cores(meta, vectors + jnp.concatenate(bias_rows, axis=0), keep_last, send_last, groups, own_rows)
    last = [
        pltpu.make_async_copy(keep_last, keep_out.at[:, :, pl.ds(3 * width, 128)], out_sems.at[4]),
        pltpu.make_async_copy(send_last, send_out.at[:, :, pl.ds(3 * width, 128)], out_sems.at[5]),
    ]
    for copy in last:
        copy.start()
    for copy in ins[:3]:
        copy.wait()
    turn(0)
    turn(1)
    half = tok_t[:, pl.ds(pl.multiple_of(size + meta[SIDE] * half_rows, half_rows), half_rows)]
    blocks = [dot(tok_t[:, :size], gq_t[:, :size], 1, 1) + dot(half, gq_t[:, size:], 1, 1)]
    for copy in ins[3:]:
        copy.wait()
    turn(2)

    def pair_block(which):
        span = slice(which * width, (which + 1) * width)
        block = dot(tok_t[:, :size], gkv_t[0, span, :], 1, 1)
        block = block + dot(tok_t[:, size : 2 * size], gkv_t[1, span, :], 1, 1)
        return block + dot(tok_t[:, 2 * size :], gkv_t[2, span, :], 1, 1)

    blocks.append(pair_block(0))
    finish(0, blocks[0])
    blocks.append(pair_block(1))
    finish(1, blocks[1])
    finish(2, blocks[2])
    for copy in outs(1) + outs(2) + last:
        copy.wait()


def started(pairs, sems):
    copies = [pltpu.make_async_copy(source, target, sems.at[at]) for at, (source, target) in enumerate(pairs)]
    for copy in copies:
        copy.start()
    return copies


def tokens_sent(
    meta, w_in, gq_in, gkv_in, first_in, sent_out, two_out, w, gq_t, gkv_t, first, sent, two, sems, out_sems
):
    width = w.shape[0]
    size = two.shape[0]
    half_rows = size // 2
    late, early = pl.ds(width, 2 * width), pl.ds(0, width)
    half = pl.ds(size, half_rows)
    ins = started(
        [
            (gkv_in.at[2], gkv_t.at[1]), (w_in.at[:, late], w.at[:, late]), (gkv_in.at[1], gkv_t.at[0]),
            (gq_in.at[:, half], gq_t), (w_in.at[:, early], w.at[:, early]), (first_in.at[half], first),
        ],
        sems,
    )
    for copy in ins[:3]:
        copy.wait()
    other = dot(w[:, width:], gkv_t[1])
    block_two = dot(w[:, width:], gkv_t[0])
    sent[0] = other.astype(BF).T
    outs = started([(sent.at[0], sent_out.at[0])], out_sems)
    for copy in ins[3:]:
        copy.wait()
    from_queries = dot(w[:, :width], gq_t[...])
    two[...] = block_two.T
    span = pl.ds(pl.multiple_of(meta[SIDE] * half_rows, half_rows), half_rows)
    two[span, :] += from_queries.T + first[...]
    sent[1] = two[...].astype(BF)
    for number, pair in enumerate([(sent.at[1], sent_out.at[1]), (two, two_out)]):
        copy = pltpu.make_async_copy(*pair, out_sems.at[1 + number])
        copy.start()
        outs.append(copy)
    for copy in outs:
        copy.wait()


def tokens_kept(
    meta, w_in, gq_in, gkv_in, first_in, came_in, two_in, grad_out, w, gq_t, gkv_t, own, came, two, grad, sems, out_sems
):
    width = w.shape[0]
    size = own.shape[0]
    late, early = pl.ds(width, 2 * width), pl.ds(0, width)
    ins = started(
        [
            (gkv_in.at[0], gkv_t), (w_in.at[:, late], w.at[:, late]), (gq_in.at[:, pl.ds(0, size)], gq_t),
            (w_in.at[:, early], w.at[:, early]), (came_in, came), (two_in, two), (first_in.at[pl.ds(0, size)], own),
        ],
        sems,
    )
    for copy in ins[:2]:
        copy.wait()
    total = dot(w[:, width:], gkv_t[...])
    for copy in ins[2:4]:
        copy.wait()
    total = (total + dot(w[:, :width], gq_t[...])).T
    for copy in ins[4:6]:
        copy.wait()
    grad[1] = jnp.where(meta[SIDE] == 0, two[...] + came[1].astype(F32), 0.0).astype(BF)
    outs = started([(grad.at[1], grad_out.at[1])], out_sems)
    ins[6].wait()
    grad[0] = (total + own[...] + came[0].astype(F32)).astype(BF)
    out = pltpu.make_async_copy(grad.at[0], grad_out.at[0], out_sems.at[1])
    out.start()
    for copy in outs + [out]:
        copy.wait()


def flip(value, axis, bit):
    count = lax.axis_size(axis)
    return lax.ppermute(value, axis, [(at, at ^ bit) for at in range(count)])


def after(value, *others):
    return lax.optimization_barrier((value,) + others)[0]


CORE_SUM, QUAD, PAIR, CORE_TWO, HOP_TWO, JOIN = range(6)


def two_parts(stage, bits, meta, parts, targets):
    if stage == CORE_TWO:
        kept, pieces = parts[0], parts[1:]
        starts = [sum(piece.shape[2] for piece in pieces[:number]) for number in range(len(pieces))]

    first = 0
    for part in range(2):
        outs = targets if stage == JOIN else targets[2 * part : 2 * part + 2]
        bit, place = bits[part]
        mine = (meta[OWNER] >> bit) & 1
        columns = parts[2 * part].shape[2] if stage == JOIN else outs[0].shape[2]
        for flipped, out in enumerate(outs):
            which = 1 - mine if flipped else mine
            for to in range(out.shape[0]):
                index = (((to >> place) << 1) << place) | (to & ((1 << place) - 1))
                index = index + (which << place) if len(outs) > 1 else to
                if stage != CORE_TWO:
                    total = parts[2 * part][index].astype(F32) + parts[2 * part + 1][index].astype(F32)
                    span = slice(first, first + columns) if stage == JOIN else slice(0, columns)
                    out[to, :, span] = total.astype(BF)
                    continue
                for start, piece in zip(starts, pieces):
                    low, high = max(start, first), min(start + piece.shape[2], first + columns)
                    if low < high:
                        total = kept[index, :, low:high].astype(F32)
                        total = total + piece[index, :, low - start : high - start].astype(F32)
                        out[to, :, low - first : high - first] = total.astype(BF)
        first += columns


def combine_kernel(plan, meta, *refs):
    refs = list(refs)
    ins = [[refs.pop(0) for _ in range(count)] for *_, count, _ in plan]
    outs = [[refs.pop(0) for _ in range(count)] for *_, count in plan]
    for (stage, over_x, plane, bit, _, _), parts, targets in zip(plan, ins, outs):
        places = 2**plane
        if stage in (CORE_TWO, HOP_TWO, JOIN):
            two_parts(stage, bit, meta, parts, targets)
            continue
        if stage == CORE_SUM:
            kept, pieces = parts[0], parts[1:]
            (out,) = targets
            columns = kept.shape[2]
            starts = [sum(piece.shape[2] for piece in pieces[:number]) for number in range(len(pieces))]
            for at in range(kept.shape[0]):
                for number, piece in enumerate(pieces):
                    begin, end = starts[number], starts[number] + piece.shape[2]
                    if not over_x:
                        span = slice(begin, end)
                        total = kept[at, :, span].astype(F32) + piece[at].astype(F32)
                        out[at % places, at // places, :, span] = total.astype(BF)
                        continue
                    for side in range(2):
                        low = max(begin, side * columns // 2)
                        high = min(end, (side + 1) * columns // 2)
                        if low < high:
                            total = kept[at, :, low:high].astype(F32)
                            total = total + piece[at, :, low - begin : high - begin].astype(F32)
                            to = slice(low - side * columns // 2, high - side * columns // 2)
                            out[2 * (at % places) + side, at // places, :, to] = total.astype(BF)
            continue

        def total_at(index):
            if stage == QUAD:
                (came,) = parts
                total = came[0, index].astype(F32)
                for at in range(1, came.shape[0]):
                    total = total + came[at, index].astype(F32)
                return total
            kept, came = parts
            return kept[index].astype(F32) + came[index].astype(F32)

        if len(targets) == 1:
            targets[0][...] = total_at(0).astype(BF)
        else:
            mine = (meta[OWNER] >> bit) & 1
            for flipped, out in enumerate(targets):
                which = 1 - mine if flipped else mine
                for to in range(out.shape[0]):
                    out[to] = total_at(2 * to + which).astype(BF)


class Piece:
    def __init__(self, keep, sends, plane, over_x):
        self.over_x = over_x
        self.rows = keep.shape[1]
        self.columns = keep.shape[2] // 2 if over_x else keep.shape[2]
        bits = list(range(1, lax.axis_size("batch").bit_length() - 1))
        self.plane, self.bits = plane, bits[plane:]
        self.stage = CORE_SUM
        self.parts = [keep] + [flip(send, "batch", 1) for send in sends]

    def shapes(self):
        sds = lambda *lead: jax.ShapeDtypeStruct(lead + (self.rows, self.columns), BF)
        if self.stage == CORE_SUM:
            places = 2**self.plane
            return [sds(places * (1 + self.over_x), self.parts[0].shape[0] // places)]
        count = self.parts[0].shape[-3]
        return [sds(count // 2)] * 2 if count > 1 else [sds()]

    def taken(self, results):
        self.sending = results[-1]
        if self.stage == CORE_SUM:
            places = 2**self.plane
            starts = [
                high + core for high in range(0, lax.axis_size("batch"), 2 * places) for core in range(2)
            ]
            if self.over_x:
                groups = [[2 * (start + 2 * place) + side for place in range(places) for side in range(2)] for start in starts]
                came = lax.all_to_all(results[0], ("batch", "blk"), 0, 0, axis_index_groups=groups)
            else:
                groups = [[start + 2 * place for place in range(places)] for start in starts]
                came = lax.all_to_all(results[0], "batch", 0, 0, axis_index_groups=groups)
            self.parts = [came]
            self.stage = QUAD
        elif len(results) == 2:
            self.parts = [results[0], flip(results[1], "batch", 1 << self.bits.pop(0))]
            self.stage = PAIR
        else:
            self.parts = [results[0], flip(results[0], "blk", 1)]
            self.stage = None

    def finish(self, side):
        own, came = self.parts
        if not self.over_x:
            return own.astype(F32) + came.astype(F32)
        return jnp.concatenate([jnp.where(side == 0, own, came), jnp.where(side == 0, came, own)], axis=1).astype(F32)


class TwoPartPiece(Piece):
    def __init__(self, keep, sends, widths):
        self.over_x, self.plane = False, 2
        self.rows, self.columns, self.widths = keep.shape[1], keep.shape[2], widths
        self.all_bits = list(range(1, lax.axis_size("batch").bit_length() - 1))
        self.bits = self.all_bits[2:]
        self.stage = CORE_TWO
        self.parts = [keep] + [flip(send, "batch", 1) for send in sends]

    def shapes(self):
        sds = jax.ShapeDtypeStruct
        if self.stage in (CORE_TWO, HOP_TWO):
            count = self.parts[0].shape[0] // 2
            return [sds((count, self.rows, width), BF) for width in self.widths for _ in range(2)]
        count = self.parts[0].shape[0]
        if self.stage == JOIN:
            shape = (count // 2, self.rows, self.columns)
            return [sds(shape, BF)] * 2 if count > 1 else [sds((1,) + shape[1:], BF)]
        return super().shapes()

    def turn(self):
        first, second = self.all_bits[:2]
        if self.stage == CORE_TWO:
            return [(first, 0), (second, 1)]
        if self.stage == HOP_TWO:
            return [(second, 0), (first, 0)]
        return [(self.bits[0] if self.bits else 0, 0)] * 2

    def taken(self, results):
        if self.stage in (CORE_TWO, HOP_TWO):
            (bit_a, _), (bit_b, _) = self.turn()
            keep_a, send_a, keep_b, send_b = results
            self.sending = send_b
            self.parts = [keep_a, flip(send_a, "batch", 1 << bit_a), keep_b, flip(send_b, "batch", 1 << bit_b)]
            self.stage = HOP_TWO if self.stage == CORE_TWO else JOIN
        else:
            super().taken(results)


def take(meta, pieces, *order_after):
    operands, plan, shapes = [], [], []
    for piece in pieces:
        piece.parts = list(lax.optimization_barrier(tuple(piece.parts) + order_after)[: len(piece.parts)])
        made = piece.shapes()
        bit = piece.bits[0] if piece.bits else 0
        if piece.stage in (CORE_TWO, HOP_TWO, JOIN):
            bit = piece.turn()
        plan.append((piece.stage, piece.over_x, piece.plane, bit, len(piece.parts), len(made)))
        operands += piece.parts
        shapes += made
    vmem = pl.BlockSpec(memory_space=pltpu.VMEM)
    out = pl.pallas_call(
        functools.partial(combine_kernel, plan),
        in_specs=[pl.BlockSpec(memory_space=pltpu.SMEM)] + [vmem] * len(operands),
        out_specs=[vmem] * len(shapes),
        out_shape=shapes,
        compiler_params=params(28),
        cost_estimate=cost(1, 1),
        name="combine",
    )(meta, *operands)
    for piece, (*_, count) in zip(pieces, plan):
        piece.taken(out[:count])
        out = out[count:]
    return tuple(part for piece in pieces for part in piece.parts[:1] if piece.stage != QUAD)


def local(
    tokens, cotangent, counts, perms, key_mask, w_qkv, bias_q, bias_v, w_out, bias_out, gain_one, shift_one,
    w_in, bias_in, w_back, bias_back, gain_two, shift_two,
):
    _, _, size, width = tokens.shape
    heads = perms.shape[1]
    hidden = w_in.shape[1]
    half_rows = size // 2
    total = size + half_rows
    owners = lax.axis_size("batch")
    side = lax.axis_index("blk").astype(jnp.int32)
    owner = lax.axis_index("batch").astype(jnp.int32)
    whole = lambda *shape: once(shape, lambda *_: (0,) * len(shape))
    sds = jax.ShapeDtypeStruct
    anywhere = pl.BlockSpec(memory_space=pl.ANY)
    smem = pl.BlockSpec(memory_space=pltpu.SMEM)

    tok = tokens[0]
    came = flip(tok, "blk", 1)

    count = counts[0]
    lookup = jnp.where(count == 2, perms[0], perms[1])
    own = jnp.where(side == 0, lookup[:, 0], lookup[:, 1])
    two = jnp.where(count > 2, lookup[:, 2], 2)
    source = jnp.concatenate([own, two])
    place = jnp.where(source == 2, 1, jnp.where(source == side, 0, 2))
    live = jnp.stack([(side < count).astype(jnp.int32), (count > 2).astype(jnp.int32)])
    meta = jnp.concatenate([jnp.stack([side, owner & 1]), live, owner[None], place])
    vec = jnp.concatenate([bias_q, bias_v, bias_out, gain_one, shift_one, bias_back, gain_two, shift_two]).reshape(8, width)
    own_mask = key_mask[0]

    def grid_spec(grid, in_specs, out_specs, scratch=()):
        return pltpu.PrefetchScalarGridSpec(
            num_scalar_prefetch=1, grid=grid, in_specs=in_specs, out_specs=out_specs, scratch_shapes=list(scratch)
        )

    slot = lambda at: once((None, size, width), lambda *_: (at, 0, 0))
    all_rows = whole(total, width)
    vectors = whole(8, width)
    own_q, own_k, own_v, own_mb = pl.pallas_call(
        project_own,
        grid_spec=grid_spec(
            (3,),
            [slot(0), whole(1, size), pl.BlockSpec((width, width), lambda i, m: (0, i)), vectors],
            [whole(width, size), whole(size, width), whole(width, size), whole(size, 128)],
        ),
        out_shape=[sds((width, size), BF), sds((size, width), BF), sds((width, size), BF), sds((size, 128), F32)],
        compiler_params=params(60),
        cost_estimate=cost(1e9, 1),
        name="project_own",
    )(meta, tok, own_mask[0:1], w_qkv, vec)
    other_mask = flip(after(own_mask, own_mb), "blk", 1)
    masks = jnp.stack([jnp.where(side == 0, own_mask[1], other_mask[1]), other_mask[0]])
    cot = cotangent[0]
    cot_came = lax.ppermute(after(cot[1, half_rows:], came), "blk", [(0, 1)])

    each = 4
    span = each * width // heads
    some_q = pl.BlockSpec((span, total), lambda p, m: (p, 0))
    some_rows = pl.BlockSpec((3, size, span), lambda p, m: (0, 0, p))
    some_cols = pl.BlockSpec((3, span, size), lambda p, m: (0, p, 0))
    some_probs = pl.BlockSpec((each, size, total), lambda p, m: (p, 0, 0))
    some_inv = pl.BlockSpec((1, each, total), lambda p, m: (p, 0, 0))
    probs, att, att_t, inv, q_t, k, v_t, tok_two = pl.pallas_call(
        functools.partial(attention_forward, heads),
        grid_spec=grid_spec(
            (heads // each,),
            [whole(2, size), vectors] + [anywhere] * 7,
            [some_probs, pl.BlockSpec((total, span), lambda p, m: (0, p)), some_q, some_inv] + [anywhere] * 4,
            [
                pltpu.VMEM((width, total), BF), pltpu.VMEM((3, size, width), BF), pltpu.VMEM((3, width, size), BF),
                pltpu.VMEM((3, size, 128), F32), pltpu.VMEM((width, 3 * width), BF), pltpu.VMEM((2 * size, width), BF),
                pltpu.SemaphoreType.DMA((9,)), pltpu.SemaphoreType.DMA((4,)),
            ],
        ),
        out_shape=[
            sds((heads, size, total), BF), sds((total, width), BF), sds((width, total), BF),
            sds((heads // each, each, total), F32), sds((width, total), BF), sds((3, size, width), BF), sds((3, width, size), BF),
            sds((size, width), BF),
        ],
        compiler_params=params(60),
        cost_estimate=cost(1e11, 1),
        name="attention_forward",
    )(meta, masks, vec, tok, came, w_qkv, own_q, own_k, own_v, own_mb)

    chunk = 1024
    steps = hidden // chunk
    back_steps = 4
    half = owners // 2
    back_rows = hidden // owners
    back_half = pl.BlockSpec((half // back_steps, back_rows, width), lambda i, m: (jnp.maximum(i - steps, 0), 0, 0))
    flat = lambda dtype, columns=width: sds((total, columns), dtype)
    early = lambda i: jnp.minimum(i, steps - 1)
    side_rows = once((half_rows, width), lambda i, m: (m[SIDE], 0))
    slope, back_keep, back_send, sums_two, first, normed_low, mixed, mixed_two, g_second, back_low = pl.pallas_call(
        functools.partial(rows_forward, steps),
        grid_spec=grid_spec(
            (steps + back_steps,),
            [
                slot(0), side_rows, all_rows, slot(0), once((None, half_rows, width), lambda i, m: (1, 0, 0)),
                whole(half_rows, width), whole(width, width), vectors,
                pl.BlockSpec((width, chunk), lambda i, m: (0, early(i))),
                pl.BlockSpec((1, chunk), lambda i, m: (0, early(i))),
                pl.BlockSpec((chunk, width), lambda i, m: (early(i), 0)),
            ],
            [
                pl.BlockSpec((total, chunk), lambda i, m: (0, early(i))),
                back_half, back_half, whole(8, width),
            ]
            + [anywhere] * 6,
            [
                pltpu.VMEM((total, width), F32), pltpu.VMEM((total, width), BF), pltpu.VMEM((total, width), BF),
                pltpu.VMEM((total, width), F32), pltpu.VMEM((total, width), BF), pltpu.VMEM((total, hidden), BF),
                pltpu.SemaphoreType.DMA((6,)),
            ],
        ),
        out_shape=[
            flat(BF, hidden), sds((half, back_rows, width), BF), sds((half, back_rows, width), BF),
            sds((8, width), F32), flat(F32), flat(BF),
            sds((size, width), BF), sds((half_rows, width), BF), flat(F32), flat(BF),
        ],
        compiler_params=params(60),
        cost_estimate=cost(1e11, 1),
        name="rows_forward",
    )(
        meta, tok, tok_two, att, cot, cot, cot_came, w_out, vec, w_in, bias_in.reshape(1, hidden), w_back,
    )

    back = Piece(back_keep, [back_send], 2, True)
    mixed_came = lax.ppermute(mixed_two, "blk", [(1, 0)])
    take(meta, [back])
    mixed_came, back_low = lax.optimization_barrier((mixed_came, back_low, back.sending))[:2]

    own_rows = width // owners
    in_steps = hidden // width
    in_early = lambda i: jnp.minimum(i, in_steps - 1)
    in_half = pl.BlockSpec((half, own_rows, width), lambda i, m: (0, 0, i))
    in_keep, in_send_a, in_send_b, g_b_in, sums_one, g_first, do_t = pl.pallas_call(
        rows_backward,
        grid_spec=grid_spec(
            (in_steps + 1,),
            [
                all_rows, all_rows, pl.BlockSpec((total, width), lambda i, m: (0, in_early(i))),
                pl.BlockSpec((width, width), lambda i, m: (0, in_early(i))),
                pl.BlockSpec((width, width), lambda i, m: (in_early(i), 0)),
                vectors, anywhere, anywhere, anywhere, anywhere,
            ],
            [
                in_half,
                pl.BlockSpec((half, own_rows, width), lambda i, m: (0, 0, jnp.minimum(i, 1))),
                pl.BlockSpec((half, own_rows, width), lambda i, m: (0, 0, jnp.maximum(i - 2, 0))),
                pl.BlockSpec((1, width), lambda i, m: (0, in_early(i))), whole(8, width), anywhere, anywhere,
            ],
            [
                pltpu.VMEM((total, width), F32), pltpu.VMEM((total, width), F32), pltpu.VMEM((total, width), F32),
                pltpu.VMEM((width, total), BF), pltpu.VMEM((total, width), F32), pltpu.VMEM((total, width), BF),
                pltpu.VMEM((width, total), BF), pltpu.VMEM((width, width), BF), pltpu.SemaphoreType.DMA((4,)),
                pltpu.SemaphoreType.DMA((2,)),
            ],
        ),
        out_shape=[
            sds((half, own_rows, hidden + width), BF), sds((half, own_rows, 2 * width), BF),
            sds((half, own_rows, (in_steps - 1) * width), BF), sds((1, hidden), F32), sds((8, width), F32), flat(F32),
            sds((width, total), BF),
        ],
        compiler_params=params(60),
        cost_estimate=cost(1e11, 1),
        name="rows_backward",
    )(meta, back_low, normed_low, slope, w_in, w_back, vec, first, g_second, att_t, w_out)
    in_sends = [in_send_a, in_send_b]
    inner = Piece(in_keep, in_sends, 2, True)
    take(meta, [inner], do_t)
    do_t = after(do_t, inner.sending)
    gq_shapes = [
        sds((width, total), BF), sds((3, 2, width, size), BF), sds((1, width), F32), sds((1, width), F32),
    ]

    gq_t, gkv_t, g_bq, g_bv = pl.pallas_call(
        functools.partial(attention_backward, heads),
        grid_spec=grid_spec(
            (heads // each,),
            [some_probs, some_rows, some_cols, some_q, some_q, some_q, some_inv],
            [some_q, pl.BlockSpec((3, 2, span, size), lambda p, m: (0, 0, p, 0))]
            + [pl.BlockSpec((1, span), lambda p, m: (0, p))] * 2,
            [
                pltpu.VMEM((3, span, size), F32), pltpu.VMEM((3, span, size), F32), pltpu.VMEM((span, total), F32),
                pltpu.VMEM((3, span, size), BF), pltpu.VMEM((3, size, span), BF),
            ],
        ),
        out_shape=gq_shapes,
        compiler_params=params(60),
        cost_estimate=cost(1e11, 1),
        name="attention_backward",
    )(meta, probs, k, v_t, q_t, do_t, att_t, inv)
    gkv_t = gkv_t.reshape(3, 2 * width, size)

    columns = 3 * width + 128
    vmem = pl.BlockSpec(memory_space=pltpu.VMEM)
    run_weights = pl.pallas_call(
        weight_gradients,
        in_specs=[pl.BlockSpec(memory_space=pltpu.SMEM)] + [anywhere] * 5 + [vmem] * 5,
        out_specs=[anywhere] * 2,
        scratch_shapes=[
            pltpu.VMEM((3, size, width), BF), pltpu.VMEM((width, total), BF), pltpu.VMEM((3, 2 * width, size), BF),
            pltpu.VMEM((width, 3 * size), BF),
            pltpu.VMEM((2, half, own_rows, width), BF), pltpu.VMEM((2, half, own_rows, width), BF),
            pltpu.VMEM((half, own_rows, 128), BF), pltpu.VMEM((half, own_rows, 128), BF),
            pltpu.SemaphoreType.DMA((7,)), pltpu.SemaphoreType.DMA((6,)),
        ],
        out_shape=[sds((half, own_rows, columns), BF)] * 2,
        compiler_params=params(60),
        cost_estimate=cost(1e9, 1),
        name="weight_gradients",
    )
    last_keep, last_send = run_weights(
        meta, tok, tok_two, came, gq_t, gkv_t, sums_two, sums_one, g_bq, g_bv, g_b_in
    )
    last = TwoPartPiece(last_keep, [last_send], [1280, columns - 1280])
    own_size, half_size = (width, size), (width, half_rows)
    sent, two_own = pl.pallas_call(
        tokens_sent,
        in_specs=[smem] + [anywhere] * 4,
        out_specs=[anywhere] * 2,
        out_shape=[sds((2, size, width), BF), sds((size, width), F32)],
        scratch_shapes=[
            pltpu.VMEM((width, 3 * width), BF), pltpu.VMEM(half_size, BF), pltpu.VMEM((2, 2 * width, size), BF),
            pltpu.VMEM((half_rows, width), F32), pltpu.VMEM((2, size, width), BF), pltpu.VMEM((size, width), F32),
            pltpu.SemaphoreType.DMA((6,)), pltpu.SemaphoreType.DMA((3,)),
        ],
        compiler_params=params(60),
        cost_estimate=cost(11.5e9, 1),
        name="tokens_sent",
    )(meta, w_qkv, after(gq_t, last_keep), gkv_t, g_first)
    came_grad = flip(sent, "blk", 1)

    take(meta, [last], sent)
    take(meta, [inner, back], last.sending)
    take(meta, [last], inner.sending)
    take(meta, [last, inner, back], last.sending)
    tokens_grad = pl.pallas_call(
        tokens_kept,
        in_specs=[smem] + [anywhere] * 6,
        out_specs=anywhere,
        out_shape=sds((2, size, width), BF),
        scratch_shapes=[
            pltpu.VMEM((width, 3 * width), BF), pltpu.VMEM(own_size, BF), pltpu.VMEM((2 * width, size), BF),
            pltpu.VMEM((size, width), F32), pltpu.VMEM((2, size, width), BF), pltpu.VMEM((size, width), F32),
            pltpu.VMEM((2, size, width), BF), pltpu.SemaphoreType.DMA((7,)), pltpu.SemaphoreType.DMA((2,)),
        ],
        compiler_params=params(60),
        cost_estimate=cost(1e11, 1),
        name="tokens_kept",
    )(meta, w_qkv, after(gq_t, last.sending), gkv_t, g_first, came_grad, two_own)
    take(meta, [last], tokens_grad, back.parts[1], inner.parts[1])
    for piece in (last, inner, back):
        while piece.stage is not None:
            take(meta, [piece])

    out_back = back.finish(side)
    out_in = inner.finish(side)
    own_last, came_last = last.parts
    both = lambda columns: own_last[:, columns].astype(F32) + came_last[:, columns].astype(F32)
    out_qkv, out_vectors = both(slice(0, 3 * width)), both(slice(3 * width, columns))

    mixed_other = jnp.where(side == 0, jnp.concatenate([mixed_two, mixed_came]), jnp.zeros((), BF))
    mixed_all = jnp.stack([mixed, mixed_other])[None]
    pick = lambda at: out_vectors[:, at]
    line = min(64, back_rows)
    return (
        mixed_all, tokens_grad[None],
        out_qkv, pick(6), pick(7), out_in[:, hidden:], pick(5), pick(3), pick(4),
        out_in[:, :hidden], out_vectors[: back_rows // line, 64 : 64 + line].reshape(-1), out_back, pick(2), pick(0),
        pick(1),
    )


def solution(mesh):
    split = P("batch", None, "blk", None)
    in_specs = (split, split, P("batch"), P(), P("batch", None, "blk")) + (P(),) * 13
    matrix, vector = P("batch", None), P("batch")
    out_specs = (
        split, split, matrix, vector, vector, matrix, vector, vector, vector, matrix, vector, matrix, vector, vector,
        vector,
    )
    return jax.shard_map(local, mesh=mesh, in_specs=in_specs, out_specs=out_specs, check_vma=False)
```

```python
import functools
import math

import jax
import jax.numpy as jnp
from jax import lax
from jax.experimental import pallas as pl
from jax.experimental.pallas import tpu as pltpu
from jax.sharding import PartitionSpec as P

EPSILON = 1e-05
BF = jnp.bfloat16
F32 = jnp.float32
MIB = 1024 * 1024
NEGATIVE = -1e30

SIDE, CORE, LIVE, OWNER, SOURCE = 0, 1, 2, 4, 5


def dot(a, b, ca=1, cb=0):
    return lax.dot_general(a, b, (((ca,), (cb,)), ((), ())), preferred_element_type=F32)


def params(mebibytes):
    return pltpu.CompilerParams(vmem_limit_bytes=mebibytes * MIB)


def cost(flops, read):
    return pl.CostEstimate(flops=int(flops), bytes_accessed=int(read), transcendentals=0)


def once(shape, index):
    return pl.BlockSpec(shape, index, pipeline_mode=pl.Buffered(1))


def mask_columns(mask_row):
    penalty = jnp.where(mask_row == 0, NEGATIVE, 0.0).astype(F32)
    return jnp.broadcast_to(penalty, (128, penalty.shape[1])).T


def project_own(meta, tok, mask, w, vec, q_t, k, v_t, mb):
    step = pl.program_id(0)
    rows = tok[...]

    @pl.when(step == 0)
    def _():
        queries = (dot(rows, w[...]) + vec[0:1, :]).astype(BF)
        q_t[...] = (queries * 0.125).T
        mb[...] = mask_columns(mask[...])

    @pl.when(step == 1)
    def _():
        k[...] = dot(rows, w[...]).astype(BF)

    @pl.when(step == 2)
    def _():
        v_t[...] = (dot(rows, w[...]) + vec[1:2, :]).astype(BF).T


def pad_pair(part, head):
    zeros = jnp.zeros_like(part)
    return jnp.concatenate([part, zeros] if head % 2 == 0 else [zeros, part], axis=0)


def units(heads, each, size, total, meta):
    first = pl.program_id(0) * each
    out = []
    for head in range(each):
        for slot, queries in enumerate((slice(0, size), slice(size, total))):
            source = meta[SOURCE + slot * heads + first + head]
            out.append((head, slice(64 * head, 64 * head + 64), queries, source))
    return out


def project_others(meta, vec, masks, starts, ins, k, v_t, q_t, mb, w, rows):
    size, width = k.shape[1:]
    half_rows = size // 2
    own_two, partner_two = starts

    @pl.when(meta[SIDE] == 0)
    def _():
        own_two.start()

    @pl.when(meta[SIDE] == 1)
    def _():
        partner_two.start()

    for copy in ins:
        copy.start()
    mb[1] = mask_columns(masks[0])
    mb[2] = mask_columns(masks[1])
    own_two.wait()
    for copy in ins[:2]:
        copy.wait()
    keys = dot(rows[...], w[:, width : 2 * width]).astype(BF)
    k[1] = keys[:size]
    k[2] = keys[size:]
    ins[2].wait()
    values = (dot(rows[...], w[:, 2 * width :]) + vec[1:2, :]).astype(BF)
    ins[3].wait()
    mine = rows[pl.ds(pl.multiple_of(meta[SIDE] * half_rows, half_rows), half_rows), :]
    queries = (dot(mine, w[:, :width]) + vec[0:1, :]).astype(BF) * 0.125
    v_t[1] = values[:size].T
    v_t[2] = values[size:].T
    q_t[:, size:] = queries.T
    for copy in ins[4:]:
        copy.wait()


def attention_forward(
    heads, meta, own_mask, other_mask, vec, tok_in, came_in, w_in, q_own, k_own, v_own, mb_own,
    probs, att, att_t, inv, q_out, k_out, v_out, two_out,
    q_t, k, v_t, mb, w, rows, sems, out_sems,
):
    size, total = k.shape[1], q_t.shape[1]
    width = k.shape[2]
    step = pl.program_id(0)
    copy = pltpu.make_async_copy
    outs = [
        copy(source, target, out_sems.at[at])
        for at, (source, target) in enumerate(((q_t, q_out), (k, k_out), (v_t, v_out), (rows.at[pl.ds(0, size)], two_out)))
    ]

    @pl.when(step == 0)
    def _():
        columns = [slice(width, 2 * width), slice(2 * width, 3 * width), slice(0, width)]
        two = rows.at[pl.ds(0, size)]
        starts = [copy(tok_in.at[1], two, sems.at[0]), copy(came_in.at[1], two, sems.at[0])]
        ins = [
            copy(w_in.at[:, columns[0]], w.at[:, columns[0]], sems.at[1]),
            copy(came_in.at[0], rows.at[pl.ds(size, size)], sems.at[2]),
            copy(w_in.at[:, columns[1]], w.at[:, columns[1]], sems.at[3]),
            copy(w_in.at[:, columns[2]], w.at[:, columns[2]], sems.at[4]),
            copy(q_own, q_t.at[:, pl.ds(0, size)], sems.at[5]),
            copy(k_own, k.at[0], sems.at[6]),
            copy(v_own, v_t.at[0], sems.at[7]),
            copy(mb_own, mb.at[0], sems.at[8]),
        ]
        masks = (jnp.where(meta[SIDE] == 0, own_mask[1:2, :], other_mask[1:2, :]), other_mask[0:1, :])
        project_others(meta, vec, masks, starts, ins, k, v_t, q_t, mb, w, rows)
        for out in outs:
            out.start()

    todo = units(heads, probs.shape[0], size, total, meta)
    each = att_t.shape[0]

    def lanes_of(head):
        return pl.ds(pl.multiple_of(step * each + head // 2 * 128, 128), 128)

    def rows_of(span):
        return pl.ds(pl.multiple_of(step * each + span.start, 64), 64)

    def score(unit):
        half, span, queries, source = unit
        return dot(k[source, :, lanes_of(half)], pad_pair(q_t[rows_of(span), queries], half))

    def soften(unit, scores):
        half, span, queries, source = unit
        scores = scores + jnp.concatenate([mb[source]] * (scores.shape[1] // 128), axis=1)
        weights = jnp.exp(scores - jnp.max(scores, axis=0, keepdims=True))
        inverse = 1.0 / jnp.sum(weights, axis=0, keepdims=True)
        low = weights.astype(BF)
        probs[half, :, queries] = low
        inv[0, half : half + 1, queries] = inverse
        return low, inverse

    def attend(unit, soft):
        half, span, queries, source = unit
        att_t[span, queries] = (dot(v_t[source, rows_of(span), :], soft[0]) * soft[1]).astype(BF)

    scores = {0: score(todo[0])}
    soft = {}
    for at in range(len(todo) + 1):
        if at + 1 < len(todo):
            scores[at + 1] = score(todo[at + 1])
        if at < len(todo):
            soft[at] = soften(todo[at], scores.pop(at))
        if at > 0:
            attend(todo[at - 1], soft.pop(at - 1))
    att[...] = att_t[...].T

    @pl.when(step == pl.num_programs(0) - 1)
    def _():
        for out in outs:
            out.wait()


def lane_sums(block):
    width = block.shape[1]
    part = block[:, :128]
    for at in range(128, width, 128):
        part = part + block[:, at : at + 128]
    return jnp.sum(part.T, axis=0, keepdims=True)


def attention_backward(
    heads, meta, probs, k, v_t, q_t, do_t, att_t, inv, gq_t, gkv_t, bq, bv, sum_k, sum_v, sum_q, k_t, v
):
    size, total = k.shape[1], q_t.shape[1]
    for at in range(3):
        k_t[at] = k[at].T
        v[at] = v_t[at].T
    todo = units(heads, probs.shape[0], size, total, meta)
    sum_k[...] = jnp.zeros_like(sum_k)
    sum_v[...] = jnp.zeros_like(sum_v)

    def begin(unit):
        half, span, queries, source = unit
        scaled = do_t[span, queries].astype(F32) * inv[0, half : half + 1, queries]
        delta = jnp.sum(scaled * att_t[span, queries].astype(F32), axis=0, keepdims=True)
        scaled = scaled.astype(BF)
        return scaled, delta, dot(v[source, :, 128 * (half // 2) : 128 * (half // 2) + 128], pad_pair(scaled, half))

    def middle(unit, begun):
        half, span, queries, source = unit
        scaled, delta, grad_probs = begun
        low = probs[half, :, queries]
        sum_v[source, span, :] += dot(scaled, low, 1, 1)
        return (low.astype(F32) * (grad_probs - delta)).astype(BF)

    def end(unit, grad_scores):
        half, span, queries, source = unit
        sum_k[source, span, :] += dot(q_t[span, queries], grad_scores, 1, 1)
        grad_q = dot(k_t[source, span, :], grad_scores) * 0.125
        sum_q[span, queries] = grad_q
        gq_t[span, queries] = grad_q.astype(BF)

    begun = {0: begin(todo[0])}
    grads = {}
    for at in range(len(todo) + 1):
        if at + 1 < len(todo):
            begun[at + 1] = begin(todo[at + 1])
        if at < len(todo):
            grads[at] = middle(todo[at], begun.pop(at))
        if at > 0:
            end(todo[at - 1], grads.pop(at - 1))
    gkv_t[:, 0] = sum_k[...].astype(BF)
    gkv_t[:, 1] = sum_v[...].astype(BF)
    bq[...] = lane_sums(sum_q[...])
    bv[...] = lane_sums(sum_v[0] + sum_v[1] + sum_v[2])


def normalise(rows):
    centred = rows - jnp.mean(rows, axis=-1, keepdims=True)
    scale = lax.rsqrt(jnp.mean(centred * centred, axis=-1, keepdims=True) + EPSILON)
    return centred * scale, scale


def norm_backward(grad, norm, scale, gain):
    scaled = grad * gain
    mean = jnp.mean(scaled, axis=-1, keepdims=True)
    along = jnp.mean(scaled * norm, axis=-1, keepdims=True)
    return scale * (scaled - mean - norm * along)


def gelu_pair(u):
    below = 0.5 + 0.5 * lax.erf(u * math.sqrt(0.5))
    bell = jnp.exp2((-0.5 * math.log2(math.e)) * (u * u)) * (1.0 / math.sqrt(2.0 * math.pi))
    return u * below, below + u * bell


B_OUT, GAIN_ONE, SHIFT_ONE, B_BACK, GAIN_TWO, SHIFT_TWO = 2, 3, 4, 5, 6, 7


def tiles_of(total, tile):
    return [slice(at, at + tile) for at in range(0, total, tile)]


def split_cores(meta, block, keep, send, groups, rows):
    mine = meta[CORE]
    for at in range(groups):
        low = block[2 * at * rows : (2 * at + 1) * rows].astype(BF)
        high = block[(2 * at + 1) * rows : (2 * at + 2) * rows].astype(BF)
        if keep is not None:
            keep[at] = jnp.where(mine == 0, low, high)
        if send is not None:
            send[at] = jnp.where(mine == 0, high, low)


def rows_forward(
    steps, meta, tok, two_half, att, cot, cot_half, cot_came, w_out, vec, w_in, b_in, w_back,
    slope, keep, send, sums, first_out, normed_out, mixed_out, mixed_two_out, second_out, back_out,
    first, normed_low, mixed, second, back_low, active, sems,
):
    step = pl.program_id(0)
    total = att.shape[0]
    tile = two_half.shape[0]
    size = total - tile
    chunk = w_in.shape[1]
    tiles = tiles_of(total, tile)
    copies = [
        pltpu.make_async_copy(source, target, sems.at[at])
        for at, (source, target) in enumerate(
            (
                (first, first_out), (normed_low, normed_out), (mixed.at[pl.ds(0, size)], mixed_out),
                (mixed.at[pl.ds(size, tile)], mixed_two_out), (second, second_out), (back_low, back_out),
            )
        )
    ]

    @pl.when(step == 0)
    def _():
        for at, span in enumerate(tiles):
            rows = (tok[span, :] if at + 1 < len(tiles) else two_half[...]).astype(F32)
            rows = rows + dot(att[span, :], w_out[...]) + vec[B_OUT : B_OUT + 1, :]
            first[span, :] = rows
            result = normalise(rows)[0] * vec[GAIN_ONE : GAIN_ONE + 1, :] + vec[SHIFT_ONE : SHIFT_ONE + 1, :]
            normed_low[span, :] = result.astype(BF)
            second[span, :] = result + vec[B_BACK : B_BACK + 1, :]
        copies[0].start()
        copies[1].start()

    @pl.when(step < steps)
    def _():
        hidden = dot(normed_low[...], w_in[...]) + b_in[...]
        value, grad = gelu_pair(hidden)
        value = value.astype(BF)
        active[:, pl.ds(pl.multiple_of(step * chunk, chunk), chunk)] = value
        slope[...] = grad.astype(BF)
        second[...] += dot(value, w_back[...])

    @pl.when(step == steps - 1)
    def _():
        sums[...] = jnp.zeros_like(sums)
        gain, shift = vec[GAIN_TWO : GAIN_TWO + 1, :], vec[SHIFT_TWO : SHIFT_TWO + 1, :]
        for at, span in enumerate(tiles):
            last = at + 1 == len(tiles)
            live = meta[LIVE + last].astype(F32)
            norm, scale = normalise(second[span, :])
            mixed[span, :] = ((norm * gain + shift) * live).astype(BF)
            cotangent = jnp.where(meta[SIDE] == 0, cot_half[...], cot_came[...]) if last else cot[span, :]
            grad = cotangent.astype(F32) * live
            sums[0:1, :] += jnp.sum(grad * norm, axis=0, keepdims=True)
            sums[1:2, :] += jnp.sum(grad, axis=0, keepdims=True)
            grad = norm_backward(grad, norm, scale, gain)
            sums[2:3, :] += jnp.sum(grad, axis=0, keepdims=True)
            second[span, :] = grad
            back_low[span, :] = grad.astype(BF)
        for copy in copies[2:]:
            copy.start()

    @pl.when(step >= steps)
    def _():
        groups, rows, _ = keep.shape
        columns = 2 * groups * rows
        part = active[:, pl.ds(pl.multiple_of((step - steps) * columns, columns), columns)]
        split_cores(meta, dot(part, back_low[...], 0, 0), keep, send, groups, rows)

    @pl.when(step == pl.num_programs(0) - 1)
    def _():
        for copy in copies:
            copy.wait()


def rows_backward(
    meta, back_low, normed_low, slope, w_in, w_back, vec, first_in, second_in, att_in, w_out_in,
    keep, send, b_in, sums, first_out, do_out,
    first, g_normed, g_second, att_t, g_first, first_low, do_t, w_out, sems, out_sems,
):
    step = pl.program_id(0)
    last = pl.num_programs(0) - 1
    total = back_low.shape[0]
    tiles = tiles_of(total, total // 3)
    copies = [
        pltpu.make_async_copy(first_in, first, sems.at[0]),
        pltpu.make_async_copy(second_in, g_second, sems.at[1]),
        pltpu.make_async_copy(att_in, att_t, sems.at[2]),
        pltpu.make_async_copy(w_out_in, w_out, sems.at[3]),
    ]

    @pl.when(step == 0)
    def _():
        for copy in copies:
            copy.start()
        g_normed[...] = jnp.zeros_like(g_normed)

    @pl.when(step < last)
    def _():
        grad = dot(back_low[...], w_back[...], 1, 1) * slope[...].astype(F32)
        b_in[...] = jnp.sum(grad, axis=0, keepdims=True)
        low = grad.astype(BF)
        g_normed[...] += dot(low, w_in[...], 1, 1)
        block = dot(normed_low[...], low, 0, 0)
        split_cores(meta, block, keep, send, keep.shape[0], keep.shape[1])

    @pl.when(step == last)
    def _():
        for copy in copies:
            copy.wait()
        sums[...] = jnp.zeros_like(sums)
        for span in tiles:
            norm, scale = normalise(first[span, :])
            grad = g_normed[span, :] + g_second[span, :]
            sums[0:1, :] += jnp.sum(grad * norm, axis=0, keepdims=True)
            sums[1:2, :] += jnp.sum(grad, axis=0, keepdims=True)
            grad = norm_backward(grad, norm, scale, vec[GAIN_ONE : GAIN_ONE + 1, :])
            sums[2:3, :] += jnp.sum(grad, axis=0, keepdims=True)
            g_first[span, :] = grad
            first_low[span, :] = grad.astype(BF)
        outs = [pltpu.make_async_copy(g_first, first_out, out_sems.at[0]), pltpu.make_async_copy(do_t, do_out, out_sems.at[1])]
        outs[0].start()
        do_t[...] = dot(w_out[...], first_low[...], 1, 1).astype(BF)
        outs[1].start()
        split_cores(meta, dot(att_t[...], first_low[...]), keep, send, keep.shape[0], keep.shape[1])
        for out in outs:
            out.wait()


def weight_gradients(
    meta, tok_in, two_in, other_in, gq_in, gkv_in, sums_two, sums_one, g_bq, g_bv, g_b_in,
    keep_out, send_out,
    tok, gq_t, gkv_t, tok_t, keep, send, keep_last, send_last, sems, out_sems,
):
    _, size, width = tok.shape
    half_rows = size // 2
    ins = [
        pltpu.make_async_copy(source, target, sems.at[at])
        for at, (source, target) in enumerate(
            [
                (tok_in.at[0], tok.at[0]), (two_in, tok.at[1]), (gq_in, gq_t), (other_in.at[0], tok.at[2]),
                (gkv_in.at[0], gkv_t.at[0]), (gkv_in.at[1], gkv_t.at[1]), (gkv_in.at[2], gkv_t.at[2]),
            ]
        )
    ]
    for copy in ins:
        copy.start()
    groups, own_rows = keep.shape[1], keep.shape[2]

    def outs(section):
        slot = section % 2
        columns = pl.ds(section * width, width)
        return [
            pltpu.make_async_copy(keep.at[slot], keep_out.at[:, :, columns], out_sems.at[2 * slot]),
            pltpu.make_async_copy(send.at[slot], send_out.at[:, :, columns], out_sems.at[2 * slot + 1]),
        ]

    def finish(section, block):
        slot = section % 2
        if section >= 2:
            for copy in outs(section - 2):
                copy.wait()
        split_cores(meta, block, keep.at[slot], send.at[slot], groups, own_rows)
        for copy in outs(section):
            copy.start()

    def turn(at):
        tok_t[:, at * size : (at + 1) * size] = tok[at].T

    vectors = [sums_two[0:3, :], sums_one[0:3, :], g_bq[...], g_bv[...], jnp.zeros((120, width), F32)]
    vectors = jnp.concatenate(vectors, axis=0).T
    per_owner = g_b_in.shape[1] // (2 * groups)
    line = min(64, per_owner)
    bias_rows = []
    for at in range(2 * groups):
        lines = [
            jnp.concatenate(
                [
                    jnp.zeros((1, 64), F32),
                    g_b_in[:, at * per_owner + to : at * per_owner + to + line],
                    jnp.zeros((1, 64 - line), F32),
                ][: 2 + (line < 64)],
                axis=1,
            )
            for to in range(0, per_owner, line)
        ]
        bias_rows.append(jnp.concatenate(lines + [jnp.zeros((own_rows - len(lines), 128), F32)], axis=0))
    split_cores(meta, vectors + jnp.concatenate(bias_rows, axis=0), keep_last, send_last, groups, own_rows)
    last = [
        pltpu.make_async_copy(keep_last, keep_out.at[:, :, pl.ds(3 * width, 128)], out_sems.at[4]),
        pltpu.make_async_copy(send_last, send_out.at[:, :, pl.ds(3 * width, 128)], out_sems.at[5]),
    ]
    for copy in last:
        copy.start()
    for copy in ins[:3]:
        copy.wait()
    turn(0)
    turn(1)
    half = tok_t[:, pl.ds(pl.multiple_of(size + meta[SIDE] * half_rows, half_rows), half_rows)]
    blocks = [dot(tok_t[:, :size], gq_t[:, :size], 1, 1) + dot(half, gq_t[:, size:], 1, 1)]
    for copy in ins[3:]:
        copy.wait()
    turn(2)

    def pair_block(which):
        span = slice(which * width, (which + 1) * width)
        block = dot(tok_t[:, :size], gkv_t[0, span, :], 1, 1)
        block = block + dot(tok_t[:, size : 2 * size], gkv_t[1, span, :], 1, 1)
        return block + dot(tok_t[:, 2 * size :], gkv_t[2, span, :], 1, 1)

    blocks.append(pair_block(0))
    finish(0, blocks[0])
    blocks.append(pair_block(1))
    finish(1, blocks[1])
    finish(2, blocks[2])
    for copy in outs(1) + outs(2) + last:
        copy.wait()


def started(pairs, sems):
    copies = [pltpu.make_async_copy(source, target, sems.at[at]) for at, (source, target) in enumerate(pairs)]
    for copy in copies:
        copy.start()
    return copies


def tokens_sent(
    meta, w_in, gq_in, gkv_in, first_in, sent_out, two_out, w, gq_t, gkv_t, first, sent, two, sems, out_sems
):
    width = w.shape[0]
    size = two.shape[0]
    half_rows = size // 2
    late, early = pl.ds(width, 2 * width), pl.ds(0, width)
    half = pl.ds(size, half_rows)
    ins = started(
        [
            (gkv_in.at[2], gkv_t.at[1]), (w_in.at[:, late], w.at[:, late]), (gkv_in.at[1], gkv_t.at[0]),
            (gq_in.at[:, half], gq_t), (w_in.at[:, early], w.at[:, early]), (first_in.at[half], first),
        ],
        sems,
    )
    for copy in ins[:3]:
        copy.wait()
    sent[0] = dot(gkv_t[1], w[:, width:], 0, 1).astype(BF)
    outs = started([(sent.at[0], sent_out.at[0])], out_sems)
    for copy in ins[3:]:
        copy.wait()
    two[...] = dot(gkv_t[0], w[:, width:], 0, 1)
    span = pl.ds(pl.multiple_of(meta[SIDE] * half_rows, half_rows), half_rows)
    two[span, :] += dot(gq_t[...], w[:, :width], 0, 1) + first[...]
    sent[1] = two[...].astype(BF)
    for number, pair in enumerate([(sent.at[1], sent_out.at[1]), (two, two_out)]):
        copy = pltpu.make_async_copy(*pair, out_sems.at[1 + number])
        copy.start()
        outs.append(copy)
    for copy in outs:
        copy.wait()


def tokens_kept(
    meta, w_in, gq_in, gkv_in, first_in, came_in, two_in, grad_out, w, gq_t, gkv_t, own, came, two, grad, sems, out_sems
):
    width = w.shape[0]
    size = own.shape[0]
    late, early = pl.ds(width, 2 * width), pl.ds(0, width)
    ins = started(
        [
            (gkv_in.at[0], gkv_t), (w_in.at[:, late], w.at[:, late]), (gq_in.at[:, pl.ds(0, size)], gq_t),
            (w_in.at[:, early], w.at[:, early]), (came_in, came), (two_in, two), (first_in.at[pl.ds(0, size)], own),
        ],
        sems,
    )
    for copy in ins[:2]:
        copy.wait()
    total = dot(gkv_t[...], w[:, width:], 0, 1)
    for copy in ins[2:4]:
        copy.wait()
    total = total + dot(gq_t[...], w[:, :width], 0, 1)
    for copy in ins[4:6]:
        copy.wait()
    grad[1] = jnp.where(meta[SIDE] == 0, two[...] + came[1].astype(F32), 0.0).astype(BF)
    outs = started([(grad.at[1], grad_out.at[1])], out_sems)
    ins[6].wait()
    grad[0] = (total + own[...] + came[0].astype(F32)).astype(BF)
    out = pltpu.make_async_copy(grad.at[0], grad_out.at[0], out_sems.at[1])
    out.start()
    for copy in outs + [out]:
        copy.wait()


def flip(value, axis, bit):
    count = lax.axis_size(axis)
    return lax.ppermute(value, axis, [(at, at ^ bit) for at in range(count)])


def after(value, *others):
    return lax.optimization_barrier((value,) + others)[0]


CORE_SUM, QUAD, PAIR, CORE_TWO, HOP_TWO, JOIN = range(6)


def two_parts(stage, bits, meta, parts, targets):
    if stage == CORE_TWO:
        kept, pieces = parts[0], parts[1:]
        starts = [sum(piece.shape[2] for piece in pieces[:number]) for number in range(len(pieces))]

    first = 0
    for part in range(2):
        outs = targets if stage == JOIN else targets[2 * part : 2 * part + 2]
        bit, place = bits[part]
        mine = (meta[OWNER] >> bit) & 1
        columns = parts[2 * part].shape[2] if stage == JOIN else outs[0].shape[2]
        for flipped, out in enumerate(outs):
            which = 1 - mine if flipped else mine
            for to in range(out.shape[0]):
                index = (((to >> place) << 1) << place) | (to & ((1 << place) - 1))
                index = index + (which << place) if len(outs) > 1 else to
                if stage != CORE_TWO:
                    total = parts[2 * part][index] + parts[2 * part + 1][index]
                    span = slice(first, first + columns) if stage == JOIN else slice(0, columns)
                    out[to, :, span] = total.astype(BF)
                    continue
                for start, piece in zip(starts, pieces):
                    low, high = max(start, first), min(start + piece.shape[2], first + columns)
                    if low < high:
                        total = kept[index, :, low:high] + piece[index, :, low - start : high - start]
                        out[to, :, low - first : high - first] = total.astype(BF)
        first += columns


def combine_kernel(plan, meta, *refs):
    refs = list(refs)
    ins = [[refs.pop(0) for _ in range(count)] for *_, count, _ in plan]
    outs = [[refs.pop(0) for _ in range(count)] for *_, count in plan]
    for (stage, over_x, plane, bit, _, _), parts, targets in zip(plan, ins, outs):
        places = 2**plane
        if stage in (CORE_TWO, HOP_TWO, JOIN):
            two_parts(stage, bit, meta, parts, targets)
            continue
        if stage == CORE_SUM:
            kept, pieces = parts[0], parts[1:]
            (out,) = targets
            columns = kept.shape[2]
            starts = [sum(piece.shape[2] for piece in pieces[:number]) for number in range(len(pieces))]
            for at in range(kept.shape[0]):
                for number, piece in enumerate(pieces):
                    begin, end = starts[number], starts[number] + piece.shape[2]
                    if not over_x:
                        span = slice(begin, end)
                        total = kept[at, :, span].astype(F32) + piece[at].astype(F32)
                        out[at % places, at // places, :, span] = total.astype(BF)
                        continue
                    for side in range(2):
                        low = max(begin, side * columns // 2)
                        high = min(end, (side + 1) * columns // 2)
                        if low < high:
                            total = kept[at, :, low:high] + piece[at, :, low - begin : high - begin]
                            to = slice(low - side * columns // 2, high - side * columns // 2)
                            out[2 * (at % places) + side, at // places, :, to] = total.astype(BF)
            continue

        def total_at(index):
            if stage == QUAD:
                (came,) = parts
                total = came[0, index].astype(F32)
                for at in range(1, came.shape[0]):
                    total = total + came[at, index].astype(F32)
                return total
            kept, came = parts
            return kept[index] + came[index]

        if len(targets) == 1:
            targets[0][...] = total_at(0).astype(BF)
        else:
            mine = (meta[OWNER] >> bit) & 1
            for flipped, out in enumerate(targets):
                which = 1 - mine if flipped else mine
                for to in range(out.shape[0]):
                    out[to] = total_at(2 * to + which).astype(BF)


class Piece:
    def __init__(self, keep, sends, plane, over_x):
        self.over_x = over_x
        self.rows = keep.shape[1]
        self.columns = keep.shape[2] // 2 if over_x else keep.shape[2]
        bits = list(range(1, lax.axis_size("batch").bit_length() - 1))
        self.plane, self.bits = plane, bits[plane:]
        self.stage = CORE_SUM
        self.parts = [keep] + [flip(send, "batch", 1) for send in sends]

    def shapes(self):
        sds = lambda *lead: jax.ShapeDtypeStruct(lead + (self.rows, self.columns), BF)
        if self.stage == CORE_SUM:
            places = 2**self.plane
            return [sds(places * (1 + self.over_x), self.parts[0].shape[0] // places)]
        count = self.parts[0].shape[-3]
        return [sds(count // 2)] * 2 if count > 1 else [sds()]

    def taken(self, results):
        self.sending = results[-1]
        if self.stage == CORE_SUM:
            places = 2**self.plane
            starts = [
                high + core for high in range(0, lax.axis_size("batch"), 2 * places) for core in range(2)
            ]
            if self.over_x:
                groups = [[2 * (start + 2 * place) + side for place in range(places) for side in range(2)] for start in starts]
                came = lax.all_to_all(results[0], ("batch", "blk"), 0, 0, axis_index_groups=groups)
            else:
                groups = [[start + 2 * place for place in range(places)] for start in starts]
                came = lax.all_to_all(results[0], "batch", 0, 0, axis_index_groups=groups)
            self.parts = [came]
            self.stage = QUAD
        elif len(results) == 2:
            self.parts = [results[0], flip(results[1], "batch", 1 << self.bits.pop(0))]
            self.stage = PAIR
        else:
            self.parts = [results[0], flip(results[0], "blk", 1)]
            self.stage = None

    def finish(self, side):
        own, came = self.parts
        if not self.over_x:
            return own.astype(F32) + came.astype(F32)
        return jnp.concatenate([jnp.where(side == 0, own, came), jnp.where(side == 0, came, own)], axis=1).astype(F32)


class TwoPartPiece(Piece):
    def __init__(self, keep, sends, widths):
        self.over_x, self.plane = False, 2
        self.rows, self.columns, self.widths = keep.shape[1], keep.shape[2], widths
        self.all_bits = list(range(1, lax.axis_size("batch").bit_length() - 1))
        self.bits = self.all_bits[2:]
        self.stage = CORE_TWO
        self.parts = [keep] + [flip(send, "batch", 1) for send in sends]

    def shapes(self):
        sds = jax.ShapeDtypeStruct
        if self.stage in (CORE_TWO, HOP_TWO):
            count = self.parts[0].shape[0] // 2
            return [sds((count, self.rows, width), BF) for width in self.widths for _ in range(2)]
        count = self.parts[0].shape[0]
        if self.stage == JOIN:
            shape = (count // 2, self.rows, self.columns)
            return [sds(shape, BF)] * 2 if count > 1 else [sds((1,) + shape[1:], BF)]
        return super().shapes()

    def turn(self):
        first, second = self.all_bits[:2]
        if self.stage == CORE_TWO:
            return [(first, 0), (second, 1)]
        if self.stage == HOP_TWO:
            return [(second, 0), (first, 0)]
        return [(self.bits[0] if self.bits else 0, 0)] * 2

    def taken(self, results):
        if self.stage in (CORE_TWO, HOP_TWO):
            (bit_a, _), (bit_b, _) = self.turn()
            keep_a, send_a, keep_b, send_b = results
            self.sending = send_b
            self.parts = [keep_a, flip(send_a, "batch", 1 << bit_a), keep_b, flip(send_b, "batch", 1 << bit_b)]
            self.stage = HOP_TWO if self.stage == CORE_TWO else JOIN
        else:
            super().taken(results)


def take(meta, pieces, *order_after):
    operands, plan, shapes = [], [], []
    for piece in pieces:
        piece.parts = list(lax.optimization_barrier(tuple(piece.parts) + order_after)[: len(piece.parts)])
        made = piece.shapes()
        bit = piece.bits[0] if piece.bits else 0
        if piece.stage in (CORE_TWO, HOP_TWO, JOIN):
            bit = piece.turn()
        plan.append((piece.stage, piece.over_x, piece.plane, bit, len(piece.parts), len(made)))
        operands += piece.parts
        shapes += made
    vmem = pl.BlockSpec(memory_space=pltpu.VMEM)
    out = pl.pallas_call(
        functools.partial(combine_kernel, plan),
        in_specs=[pl.BlockSpec(memory_space=pltpu.SMEM)] + [vmem] * len(operands),
        out_specs=[vmem] * len(shapes),
        out_shape=shapes,
        compiler_params=params(28),
        cost_estimate=cost(1, 1),
        name="combine",
    )(meta, *operands)
    for piece, (*_, count) in zip(pieces, plan):
        piece.taken(out[:count])
        out = out[count:]
    return tuple(part for piece in pieces for part in piece.parts[:1] if piece.stage != QUAD)


def local(
    tokens, cotangent, counts, perms, key_mask, w_qkv, bias_q, bias_v, w_out, bias_out, gain_one, shift_one,
    w_in, bias_in, w_back, bias_back, gain_two, shift_two,
):
    _, _, size, width = tokens.shape
    heads = perms.shape[1]
    hidden = w_in.shape[1]
    half_rows = size // 2
    total = size + half_rows
    owners = lax.axis_size("batch")
    side = lax.axis_index("blk").astype(jnp.int32)
    owner = lax.axis_index("batch").astype(jnp.int32)
    whole = lambda *shape: once(shape, lambda *_: (0,) * len(shape))
    sds = jax.ShapeDtypeStruct
    anywhere = pl.BlockSpec(memory_space=pl.ANY)
    smem = pl.BlockSpec(memory_space=pltpu.SMEM)

    tok = tokens[0]
    came = flip(tok, "blk", 1)

    count = counts[0]
    lookup = jnp.where(count == 2, perms[0], perms[1])
    own = jnp.where(side == 0, lookup[:, 0], lookup[:, 1])
    two = jnp.where(count > 2, lookup[:, 2], 2)
    source = jnp.concatenate([own, two])
    place = jnp.where(source == 2, 1, jnp.where(source == side, 0, 2))
    live = jnp.stack([(side < count).astype(jnp.int32), (count > 2).astype(jnp.int32)])
    meta = jnp.concatenate([jnp.stack([side, owner & 1]), live, owner[None], place])
    vec = jnp.concatenate([bias_q, bias_v, bias_out, gain_one, shift_one, bias_back, gain_two, shift_two]).reshape(8, width)
    own_mask = key_mask[0]

    def grid_spec(grid, in_specs, out_specs, scratch=()):
        return pltpu.PrefetchScalarGridSpec(
            num_scalar_prefetch=1, grid=grid, in_specs=in_specs, out_specs=out_specs, scratch_shapes=list(scratch)
        )

    slot = lambda at: once((None, size, width), lambda *_: (at, 0, 0))
    all_rows = whole(total, width)
    vectors = whole(8, width)
    own_q, own_k, own_v, own_mb = pl.pallas_call(
        project_own,
        grid_spec=grid_spec(
            (3,),
            [slot(0), whole(1, size), pl.BlockSpec((width, width), lambda i, m: (0, i)), vectors],
            [whole(width, size), whole(size, width), whole(width, size), whole(size, 128)],
        ),
        out_shape=[sds((width, size), BF), sds((size, width), BF), sds((width, size), BF), sds((size, 128), F32)],
        compiler_params=params(60),
        cost_estimate=cost(1e9, 1),
        name="project_own",
    )(meta, tok, own_mask[0:1], w_qkv, vec)
    other_mask = flip(after(own_mask, own_mb), "blk", 1)
    masks = (own_mask, other_mask)
    cot = cotangent[0]
    cot_came = lax.ppermute(after(cot[1, half_rows:], came), "blk", [(0, 1)])

    each = 4
    span = each * width // heads
    some_q = pl.BlockSpec((span, total), lambda p, m: (p, 0))
    some_rows = pl.BlockSpec((3, size, span), lambda p, m: (0, 0, p))
    some_cols = pl.BlockSpec((3, span, size), lambda p, m: (0, p, 0))
    some_probs = pl.BlockSpec((each, size, total), lambda p, m: (p, 0, 0))
    some_inv = pl.BlockSpec((1, each, total), lambda p, m: (p, 0, 0))
    probs, att, att_t, inv, q_t, k, v_t, tok_two = pl.pallas_call(
        functools.partial(attention_forward, heads),
        grid_spec=grid_spec(
            (heads // each,),
            [whole(2, size), whole(2, size), vectors] + [anywhere] * 7,
            [some_probs, pl.BlockSpec((total, span), lambda p, m: (0, p)), some_q, some_inv] + [anywhere] * 4,
            [
                pltpu.VMEM((width, total), BF), pltpu.VMEM((3, size, width), BF), pltpu.VMEM((3, width, size), BF),
                pltpu.VMEM((3, size, 128), F32), pltpu.VMEM((width, 3 * width), BF), pltpu.VMEM((2 * size, width), BF),
                pltpu.SemaphoreType.DMA((9,)), pltpu.SemaphoreType.DMA((4,)),
            ],
        ),
        out_shape=[
            sds((heads, size, total), BF), sds((total, width), BF), sds((width, total), BF),
            sds((heads // each, each, total), F32), sds((width, total), BF), sds((3, size, width), BF), sds((3, width, size), BF),
            sds((size, width), BF),
        ],
        compiler_params=params(60),
        cost_estimate=cost(1e11, 1),
        name="attention_forward",
    )(meta, *masks, vec, tok, came, w_qkv, own_q, own_k, own_v, own_mb)

    chunk = 1024
    steps = hidden // chunk
    back_steps = 4
    half = owners // 2
    back_rows = hidden // owners
    back_half = pl.BlockSpec((half // back_steps, back_rows, width), lambda i, m: (jnp.maximum(i - steps, 0), 0, 0))
    flat = lambda dtype, columns=width: sds((total, columns), dtype)
    early = lambda i: jnp.minimum(i, steps - 1)
    side_rows = once((half_rows, width), lambda i, m: (m[SIDE], 0))
    slope, back_keep, back_send, sums_two, first, normed_low, mixed, mixed_two, g_second, back_low = pl.pallas_call(
        functools.partial(rows_forward, steps),
        grid_spec=grid_spec(
            (steps + back_steps,),
            [
                slot(0), side_rows, all_rows, slot(0), once((None, half_rows, width), lambda i, m: (1, 0, 0)),
                whole(half_rows, width), whole(width, width), vectors,
                pl.BlockSpec((width, chunk), lambda i, m: (0, early(i))),
                pl.BlockSpec((1, chunk), lambda i, m: (0, early(i))),
                pl.BlockSpec((chunk, width), lambda i, m: (early(i), 0)),
            ],
            [
                pl.BlockSpec((total, chunk), lambda i, m: (0, early(i))),
                back_half, back_half, whole(8, width),
            ]
            + [anywhere] * 6,
            [
                pltpu.VMEM((total, width), F32), pltpu.VMEM((total, width), BF), pltpu.VMEM((total, width), BF),
                pltpu.VMEM((total, width), F32), pltpu.VMEM((total, width), BF), pltpu.VMEM((total, hidden), BF),
                pltpu.SemaphoreType.DMA((6,)),
            ],
        ),
        out_shape=[
            flat(BF, hidden), sds((half, back_rows, width), BF), sds((half, back_rows, width), BF),
            sds((8, width), F32), flat(F32), flat(BF),
            sds((size, width), BF), sds((half_rows, width), BF), flat(F32), flat(BF),
        ],
        compiler_params=params(60),
        cost_estimate=cost(1e11, 1),
        name="rows_forward",
    )(
        meta, tok, tok_two, att, cot, cot, cot_came, w_out, vec, w_in, bias_in.reshape(1, hidden), w_back,
    )

    back = Piece(back_keep, [back_send], 2, True)
    mixed_came = lax.ppermute(mixed_two, "blk", [(1, 0)])
    take(meta, [back])
    mixed_came, back_low = lax.optimization_barrier((mixed_came, back_low, back.sending))[:2]

    own_rows = width // owners
    in_steps = hidden // width
    in_early = lambda i: jnp.minimum(i, in_steps - 1)
    in_half = pl.BlockSpec((half, own_rows, width), lambda i, m: (0, 0, i))
    in_keep, in_send, g_b_in, sums_one, g_first, do_t = pl.pallas_call(
        rows_backward,
        grid_spec=grid_spec(
            (in_steps + 1,),
            [
                all_rows, all_rows, pl.BlockSpec((total, width), lambda i, m: (0, in_early(i))),
                pl.BlockSpec((width, width), lambda i, m: (0, in_early(i))),
                pl.BlockSpec((width, width), lambda i, m: (in_early(i), 0)),
                vectors, anywhere, anywhere, anywhere, anywhere,
            ],
            [
                in_half, in_half,
                pl.BlockSpec((1, width), lambda i, m: (0, in_early(i))), whole(8, width), anywhere, anywhere,
            ],
            [
                pltpu.VMEM((total, width), F32), pltpu.VMEM((total, width), F32), pltpu.VMEM((total, width), F32),
                pltpu.VMEM((width, total), BF), pltpu.VMEM((total, width), F32), pltpu.VMEM((total, width), BF),
                pltpu.VMEM((width, total), BF), pltpu.VMEM((width, width), BF), pltpu.SemaphoreType.DMA((4,)),
                pltpu.SemaphoreType.DMA((2,)),
            ],
        ),
        out_shape=[
            sds((half, own_rows, hidden + width), BF), sds((half, own_rows, hidden + width), BF), sds((1, hidden), F32), sds((8, width), F32), flat(F32),
            sds((width, total), BF),
        ],
        compiler_params=params(60),
        cost_estimate=cost(1e11, 1),
        name="rows_backward",
    )(meta, back_low, normed_low, slope, w_in, w_back, vec, first, g_second, att_t, w_out)
    in_sends = [in_send]
    inner = Piece(in_keep, in_sends, 2, True)
    take(meta, [inner], do_t)
    do_t = after(do_t, inner.sending)
    gq_shapes = [
        sds((width, total), BF), sds((3, 2, width, size), BF), sds((1, width), F32), sds((1, width), F32),
    ]

    gq_t, gkv_t, g_bq, g_bv = pl.pallas_call(
        functools.partial(attention_backward, heads),
        grid_spec=grid_spec(
            (heads // each,),
            [some_probs, some_rows, some_cols, some_q, some_q, some_q, some_inv],
            [some_q, pl.BlockSpec((3, 2, span, size), lambda p, m: (0, 0, p, 0))]
            + [pl.BlockSpec((1, span), lambda p, m: (0, p))] * 2,
            [
                pltpu.VMEM((3, span, size), F32), pltpu.VMEM((3, span, size), F32), pltpu.VMEM((span, total), F32),
                pltpu.VMEM((3, span, size), BF), pltpu.VMEM((3, size, span), BF),
            ],
        ),
        out_shape=gq_shapes,
        compiler_params=params(60),
        cost_estimate=cost(1e11, 1),
        name="attention_backward",
    )(meta, probs, k, v_t, q_t, do_t, att_t, inv)
    gkv_t = gkv_t.reshape(3, 2 * width, size)

    columns = 3 * width + 128
    vmem = pl.BlockSpec(memory_space=pltpu.VMEM)
    run_weights = pl.pallas_call(
        weight_gradients,
        in_specs=[pl.BlockSpec(memory_space=pltpu.SMEM)] + [anywhere] * 5 + [vmem] * 5,
        out_specs=[anywhere] * 2,
        scratch_shapes=[
            pltpu.VMEM((3, size, width), BF), pltpu.VMEM((width, total), BF), pltpu.VMEM((3, 2 * width, size), BF),
            pltpu.VMEM((width, 3 * size), BF),
            pltpu.VMEM((2, half, own_rows, width), BF), pltpu.VMEM((2, half, own_rows, width), BF),
            pltpu.VMEM((half, own_rows, 128), BF), pltpu.VMEM((half, own_rows, 128), BF),
            pltpu.SemaphoreType.DMA((7,)), pltpu.SemaphoreType.DMA((6,)),
        ],
        out_shape=[sds((half, own_rows, columns), BF)] * 2,
        compiler_params=params(60),
        cost_estimate=cost(1e9, 1),
        name="weight_gradients",
    )
    last_keep, last_send = run_weights(
        meta, tok, tok_two, came, gq_t, gkv_t, sums_two, sums_one, g_bq, g_bv, g_b_in
    )
    last = TwoPartPiece(last_keep, [last_send], [1280, columns - 1280])
    own_size, half_size = (width, size), (width, half_rows)
    sent, two_own = pl.pallas_call(
        tokens_sent,
        in_specs=[smem] + [anywhere] * 4,
        out_specs=[anywhere] * 2,
        out_shape=[sds((2, size, width), BF), sds((size, width), F32)],
        scratch_shapes=[
            pltpu.VMEM((width, 3 * width), BF), pltpu.VMEM(half_size, BF), pltpu.VMEM((2, 2 * width, size), BF),
            pltpu.VMEM((half_rows, width), F32), pltpu.VMEM((2, size, width), BF), pltpu.VMEM((size, width), F32),
            pltpu.SemaphoreType.DMA((6,)), pltpu.SemaphoreType.DMA((3,)),
        ],
        compiler_params=params(60),
        cost_estimate=cost(11.5e9, 1),
        name="tokens_sent",
    )(meta, w_qkv, after(gq_t, last_keep), gkv_t, g_first)
    came_grad = flip(sent, "blk", 1)

    take(meta, [last], sent)
    take(meta, [inner, back], last.sending)
    take(meta, [last], inner.sending)
    take(meta, [last, inner, back], last.sending)
    tokens_grad = pl.pallas_call(
        tokens_kept,
        in_specs=[smem] + [anywhere] * 6,
        out_specs=anywhere,
        out_shape=sds((2, size, width), BF),
        scratch_shapes=[
            pltpu.VMEM((width, 3 * width), BF), pltpu.VMEM(own_size, BF), pltpu.VMEM((2 * width, size), BF),
            pltpu.VMEM((size, width), F32), pltpu.VMEM((2, size, width), BF), pltpu.VMEM((size, width), F32),
            pltpu.VMEM((2, size, width), BF), pltpu.SemaphoreType.DMA((7,)), pltpu.SemaphoreType.DMA((2,)),
        ],
        compiler_params=params(60),
        cost_estimate=cost(1e11, 1),
        name="tokens_kept",
    )(meta, w_qkv, after(gq_t, last.sending), gkv_t, g_first, came_grad, two_own)
    take(meta, [last], tokens_grad, back.parts[1], inner.parts[1])
    for piece in (last, inner, back):
        while piece.stage is not None:
            take(meta, [piece])

    out_back = back.finish(side)
    out_in = inner.finish(side)
    own_last, came_last = last.parts
    both = lambda columns: own_last[:, columns].astype(F32) + came_last[:, columns].astype(F32)
    out_qkv, out_vectors = both(slice(0, 3 * width)), both(slice(3 * width, columns))

    mixed_other = jnp.where(side == 0, jnp.concatenate([mixed_two, mixed_came]), jnp.zeros((), BF))
    mixed_all = jnp.stack([mixed, mixed_other])[None]
    pick = lambda at: out_vectors[:, at]
    line = min(64, back_rows)
    return (
        mixed_all, tokens_grad[None],
        out_qkv, pick(6), pick(7), out_in[:, hidden:], pick(5), pick(3), pick(4),
        out_in[:, :hidden], out_vectors[: back_rows // line, 64 : 64 + line].reshape(-1), out_back, pick(2), pick(0),
        pick(1),
    )


def solution(mesh):
    split = P("batch", None, "blk", None)
    in_specs = (split, split, P("batch"), P(), P("batch", None, "blk")) + (P(),) * 13
    matrix, vector = P("batch", None), P("batch")
    out_specs = (
        split, split, matrix, vector, vector, matrix, vector, vector, vector, matrix, vector, matrix, vector, vector,
        vector,
    )
    return jax.shard_map(local, mesh=mesh, in_specs=in_specs, out_specs=out_specs, check_vma=False)
```

```python
import functools
import math

import jax
import jax.numpy as jnp
from jax import lax
from jax.experimental import pallas as pl
from jax.experimental.pallas import tpu as pltpu
from jax.sharding import PartitionSpec as P

EPSILON = 1e-05
BF = jnp.bfloat16
F32 = jnp.float32
MIB = 1024 * 1024
NEGATIVE = -1e30

SIDE, CORE, LIVE, OWNER, SOURCE = 0, 1, 2, 4, 5


def dot(a, b, ca=1, cb=0):
    return lax.dot_general(a, b, (((ca,), (cb,)), ((), ())), preferred_element_type=F32)


def params(mebibytes):
    return pltpu.CompilerParams(vmem_limit_bytes=mebibytes * MIB)


def cost(flops, read):
    return pl.CostEstimate(flops=int(flops), bytes_accessed=int(read), transcendentals=0)


def once(shape, index):
    return pl.BlockSpec(shape, index, pipeline_mode=pl.Buffered(1))


def mask_columns(mask_row):
    penalty = jnp.where(mask_row == 0, NEGATIVE, 0.0).astype(F32)
    return jnp.broadcast_to(penalty, (128, penalty.shape[1])).T


def project_own(meta, tok, mask, w, vec, q_t, k, v_t, mb):
    step = pl.program_id(0)
    rows = tok[...]

    @pl.when(step == 0)
    def _():
        queries = (dot(rows, w[...]) + vec[0:1, :]).astype(BF)
        q_t[...] = (queries * 0.125).T
        mb[...] = mask_columns(mask[...])

    @pl.when(step == 1)
    def _():
        k[...] = dot(rows, w[...]).astype(BF)

    @pl.when(step == 2)
    def _():
        v_t[...] = (dot(rows, w[...]) + vec[1:2, :]).astype(BF).T


def pad_pair(part, head):
    zeros = jnp.zeros_like(part)
    return jnp.concatenate([part, zeros] if head % 2 == 0 else [zeros, part], axis=0)


def units(heads, each, size, total, meta):
    first = pl.program_id(0) * each
    out = []
    for head in range(each):
        for slot, queries in enumerate((slice(0, size), slice(size, total))):
            source = meta[SOURCE + slot * heads + first + head]
            out.append((head, slice(64 * head, 64 * head + 64), queries, source))
    return out


def project_others(meta, vec, masks, starts, ins, k, v_t, q_t, mb, w, rows):
    size, width = k.shape[1:]
    half_rows = size // 2
    own_two, partner_two = starts

    @pl.when(meta[SIDE] == 0)
    def _():
        own_two.start()

    @pl.when(meta[SIDE] == 1)
    def _():
        partner_two.start()

    for copy in ins:
        copy.start()
    mb[1] = mask_columns(masks[0])
    mb[2] = mask_columns(masks[1])
    own_two.wait()
    for copy in ins[:2]:
        copy.wait()
    keys = dot(rows[...], w[:, width : 2 * width]).astype(BF)
    k[1] = keys[:size]
    k[2] = keys[size:]
    ins[2].wait()
    values = (dot(rows[...], w[:, 2 * width :]) + vec[1:2, :]).astype(BF)
    ins[3].wait()
    mine = rows[pl.ds(pl.multiple_of(meta[SIDE] * half_rows, half_rows), half_rows), :]
    queries = (dot(mine, w[:, :width]) + vec[0:1, :]).astype(BF) * 0.125
    v_t[1] = values[:size].T
    v_t[2] = values[size:].T
    q_t[:, size:] = queries.T
    for copy in ins[4:]:
        copy.wait()


def attention_forward(
    heads, meta, own_mask, other_mask, vec, tok_in, came_in, w_in, q_own, k_own, v_own, mb_own,
    probs, att, att_t, inv, q_out, k_out, v_out, two_out,
    q_t, k, v_t, mb, w, rows, sems, out_sems,
):
    size, total = k.shape[1], q_t.shape[1]
    width = k.shape[2]
    step = pl.program_id(0)
    copy = pltpu.make_async_copy
    outs = [
        copy(source, target, out_sems.at[at])
        for at, (source, target) in enumerate(((q_t, q_out), (k, k_out), (v_t, v_out), (rows.at[pl.ds(0, size)], two_out)))
    ]

    @pl.when(step == 0)
    def _():
        columns = [slice(width, 2 * width), slice(2 * width, 3 * width), slice(0, width)]
        two = rows.at[pl.ds(0, size)]
        starts = [copy(tok_in.at[1], two, sems.at[0]), copy(came_in.at[1], two, sems.at[0])]
        ins = [
            copy(w_in.at[:, columns[0]], w.at[:, columns[0]], sems.at[1]),
            copy(came_in.at[0], rows.at[pl.ds(size, size)], sems.at[2]),
            copy(w_in.at[:, columns[1]], w.at[:, columns[1]], sems.at[3]),
            copy(w_in.at[:, columns[2]], w.at[:, columns[2]], sems.at[4]),
            copy(q_own, q_t.at[:, pl.ds(0, size)], sems.at[5]),
            copy(k_own, k.at[0], sems.at[6]),
            copy(v_own, v_t.at[0], sems.at[7]),
            copy(mb_own, mb.at[0], sems.at[8]),
        ]
        masks = (jnp.where(meta[SIDE] == 0, own_mask[1:2, :], other_mask[1:2, :]), other_mask[0:1, :])
        project_others(meta, vec, masks, starts, ins, k, v_t, q_t, mb, w, rows)
        for out in outs:
            out.start()

    todo = units(heads, probs.shape[0], size, total, meta)
    each = att_t.shape[0]

    def lanes_of(head):
        return pl.ds(pl.multiple_of(step * each + head // 2 * 128, 128), 128)

    def rows_of(span):
        return pl.ds(pl.multiple_of(step * each + span.start, 64), 64)

    def score(unit):
        half, span, queries, source = unit
        return dot(k[source, :, lanes_of(half)], pad_pair(q_t[rows_of(span), queries], half))

    def soften(unit, scores):
        half, span, queries, source = unit
        scores = scores + jnp.concatenate([mb[source]] * (scores.shape[1] // 128), axis=1)
        weights = jnp.exp(scores - jnp.max(scores, axis=0, keepdims=True))
        inverse = 1.0 / jnp.sum(weights, axis=0, keepdims=True)
        low = weights.astype(BF)
        probs[half, :, queries] = low
        inv[0, half : half + 1, queries] = inverse
        return low, inverse

    def attend(unit, soft):
        half, span, queries, source = unit
        att_t[span, queries] = (dot(v_t[source, rows_of(span), :], soft[0]) * soft[1]).astype(BF)

    scores = {0: score(todo[0])}
    soft = {}
    for at in range(len(todo) + 1):
        if at + 1 < len(todo):
            scores[at + 1] = score(todo[at + 1])
        if at < len(todo):
            soft[at] = soften(todo[at], scores.pop(at))
        if at > 0:
            attend(todo[at - 1], soft.pop(at - 1))
    att[...] = att_t[...].T

    @pl.when(step == pl.num_programs(0) - 1)
    def _():
        for out in outs:
            out.wait()


def lane_sums(block):
    width = block.shape[1]
    part = block[:, :128]
    for at in range(128, width, 128):
        part = part + block[:, at : at + 128]
    return jnp.sum(part.T, axis=0, keepdims=True)


def attention_backward(
    heads, meta, probs, k, v_t, q_t, do_t, att_t, inv, gq_t, gkv_t, bq, bv, sum_k, sum_v, sum_q, k_t, v
):
    size, total = k.shape[1], q_t.shape[1]
    for at in range(3):
        k_t[at] = k[at].T
        v[at] = v_t[at].T
    todo = units(heads, probs.shape[0], size, total, meta)
    sum_k[...] = jnp.zeros_like(sum_k)
    sum_v[...] = jnp.zeros_like(sum_v)

    def begin(unit):
        half, span, queries, source = unit
        scaled = do_t[span, queries].astype(F32) * inv[0, half : half + 1, queries]
        delta = jnp.sum(scaled * att_t[span, queries].astype(F32), axis=0, keepdims=True)
        scaled = scaled.astype(BF)
        return scaled, delta, dot(v[source, :, 128 * (half // 2) : 128 * (half // 2) + 128], pad_pair(scaled, half))

    def middle(unit, begun):
        half, span, queries, source = unit
        scaled, delta, grad_probs = begun
        low = probs[half, :, queries]
        sum_v[source, span, :] += dot(scaled, low, 1, 1)
        return (low.astype(F32) * (grad_probs - delta)).astype(BF)

    def end(unit, grad_scores):
        half, span, queries, source = unit
        sum_k[source, span, :] += dot(q_t[span, queries], grad_scores, 1, 1)
        grad_q = dot(k_t[source, span, :], grad_scores) * 0.125
        sum_q[span, queries] = grad_q
        gq_t[span, queries] = grad_q.astype(BF)

    begun = {0: begin(todo[0])}
    grads = {}
    for at in range(len(todo) + 1):
        if at + 1 < len(todo):
            begun[at + 1] = begin(todo[at + 1])
        if at < len(todo):
            grads[at] = middle(todo[at], begun.pop(at))
        if at > 0:
            end(todo[at - 1], grads.pop(at - 1))
    gkv_t[:, 0] = sum_k[...].astype(BF)
    gkv_t[:, 1] = sum_v[...].astype(BF)
    bq[...] = lane_sums(sum_q[...])
    bv[...] = lane_sums(sum_v[0] + sum_v[1] + sum_v[2])


def normalise(rows):
    centred = rows - jnp.mean(rows, axis=-1, keepdims=True)
    scale = lax.rsqrt(jnp.mean(centred * centred, axis=-1, keepdims=True) + EPSILON)
    return centred * scale, scale


def norm_backward(grad, norm, scale, gain):
    scaled = grad * gain
    mean = jnp.mean(scaled, axis=-1, keepdims=True)
    along = jnp.mean(scaled * norm, axis=-1, keepdims=True)
    return scale * (scaled - mean - norm * along)


def gelu_pair(u):
    below = 0.5 + 0.5 * lax.erf(u * math.sqrt(0.5))
    bell = jnp.exp2((-0.5 * math.log2(math.e)) * (u * u)) * (1.0 / math.sqrt(2.0 * math.pi))
    return u * below, below + u * bell


B_OUT, GAIN_ONE, SHIFT_ONE, B_BACK, GAIN_TWO, SHIFT_TWO = 2, 3, 4, 5, 6, 7


def tiles_of(total, tile):
    return [slice(at, at + tile) for at in range(0, total, tile)]


def split_cores(meta, block, keep, send, groups, rows):
    mine = meta[CORE]
    for at in range(groups):
        low = block[2 * at * rows : (2 * at + 1) * rows].astype(BF)
        high = block[(2 * at + 1) * rows : (2 * at + 2) * rows].astype(BF)
        if keep is not None:
            keep[at] = jnp.where(mine == 0, low, high)
        if send is not None:
            send[at] = jnp.where(mine == 0, high, low)


def rows_forward(
    steps, meta, tok, two_half, att, cot, cot_half, cot_came, w_out, vec, w_in, b_in, w_back,
    slope, keep, send, sums, first_out, normed_out, mixed_out, mixed_two_out, second_out, back_out,
    first, normed_low, mixed, second, back_low, active, sems,
):
    step = pl.program_id(0)
    total = att.shape[0]
    tile = two_half.shape[0]
    size = total - tile
    chunk = w_in.shape[1]
    tiles = tiles_of(total, tile)
    copies = [
        pltpu.make_async_copy(source, target, sems.at[at])
        for at, (source, target) in enumerate(
            (
                (first, first_out), (normed_low, normed_out), (mixed.at[pl.ds(0, size)], mixed_out),
                (mixed.at[pl.ds(size, tile)], mixed_two_out), (second, second_out), (back_low, back_out),
            )
        )
    ]

    @pl.when(step == 0)
    def _():
        for at, span in enumerate(tiles):
            rows = (tok[span, :] if at + 1 < len(tiles) else two_half[...]).astype(F32)
            rows = rows + dot(att[span, :], w_out[...]) + vec[B_OUT : B_OUT + 1, :]
            first[span, :] = rows
            result = normalise(rows)[0] * vec[GAIN_ONE : GAIN_ONE + 1, :] + vec[SHIFT_ONE : SHIFT_ONE + 1, :]
            normed_low[span, :] = result.astype(BF)
            second[span, :] = result + vec[B_BACK : B_BACK + 1, :]
        copies[0].start()
        copies[1].start()

    @pl.when(step < steps)
    def _():
        hidden = dot(normed_low[...], w_in[...]) + b_in[...]
        value, grad = gelu_pair(hidden)
        value = value.astype(BF)
        active[:, pl.ds(pl.multiple_of(step * chunk, chunk), chunk)] = value
        slope[...] = grad.astype(BF)
        second[...] += dot(value, w_back[...])

    @pl.when(step == steps - 1)
    def _():
        sums[...] = jnp.zeros_like(sums)
        gain, shift = vec[GAIN_TWO : GAIN_TWO + 1, :], vec[SHIFT_TWO : SHIFT_TWO + 1, :]
        for at, span in enumerate(tiles):
            last = at + 1 == len(tiles)
            live = meta[LIVE + last].astype(F32)
            norm, scale = normalise(second[span, :])
            mixed[span, :] = ((norm * gain + shift) * live).astype(BF)
            cotangent = jnp.where(meta[SIDE] == 0, cot_half[...], cot_came[...]) if last else cot[span, :]
            grad = cotangent.astype(F32) * live
            sums[0:1, :] += jnp.sum(grad * norm, axis=0, keepdims=True)
            sums[1:2, :] += jnp.sum(grad, axis=0, keepdims=True)
            grad = norm_backward(grad, norm, scale, gain)
            sums[2:3, :] += jnp.sum(grad, axis=0, keepdims=True)
            second[span, :] = grad
            back_low[span, :] = grad.astype(BF)
        for copy in copies[2:]:
            copy.start()

    @pl.when(step >= steps)
    def _():
        groups, rows, _ = keep.shape
        columns = 2 * groups * rows
        part = active[:, pl.ds(pl.multiple_of((step - steps) * columns, columns), columns)]
        split_cores(meta, dot(part, back_low[...], 0, 0), keep, send, groups, rows)

    @pl.when(step == pl.num_programs(0) - 1)
    def _():
        for copy in copies:
            copy.wait()


def rows_backward(
    meta, back_low, normed_low, slope, w_in, w_back, vec, first_in, second_in, att_in, w_out_in,
    keep, send, b_in, sums, first_out, do_out,
    first, g_normed, g_second, att_t, g_first, first_low, do_t, w_out, sems, out_sems,
):
    step = pl.program_id(0)
    last = pl.num_programs(0) - 1
    total = back_low.shape[0]
    tiles = tiles_of(total, total // 3)
    copies = [
        pltpu.make_async_copy(first_in, first, sems.at[0]),
        pltpu.make_async_copy(second_in, g_second, sems.at[1]),
        pltpu.make_async_copy(att_in, att_t, sems.at[2]),
        pltpu.make_async_copy(w_out_in, w_out, sems.at[3]),
    ]

    @pl.when(step == 0)
    def _():
        for copy in copies:
            copy.start()
        g_normed[...] = jnp.zeros_like(g_normed)

    @pl.when(step < last)
    def _():
        grad = dot(back_low[...], w_back[...], 1, 1) * slope[...].astype(F32)
        b_in[...] = jnp.sum(grad, axis=0, keepdims=True)
        low = grad.astype(BF)
        g_normed[...] += dot(low, w_in[...], 1, 1)
        block = dot(normed_low[...], low, 0, 0)
        split_cores(meta, block, keep, send, keep.shape[0], keep.shape[1])

    @pl.when(step == last)
    def _():
        for copy in copies:
            copy.wait()
        sums[...] = jnp.zeros_like(sums)
        for span in tiles:
            norm, scale = normalise(first[span, :])
            grad = g_normed[span, :] + g_second[span, :]
            sums[0:1, :] += jnp.sum(grad * norm, axis=0, keepdims=True)
            sums[1:2, :] += jnp.sum(grad, axis=0, keepdims=True)
            grad = norm_backward(grad, norm, scale, vec[GAIN_ONE : GAIN_ONE + 1, :])
            sums[2:3, :] += jnp.sum(grad, axis=0, keepdims=True)
            g_first[span, :] = grad
            first_low[span, :] = grad.astype(BF)
        outs = [pltpu.make_async_copy(g_first, first_out, out_sems.at[0]), pltpu.make_async_copy(do_t, do_out, out_sems.at[1])]
        outs[0].start()
        do_t[...] = dot(w_out[...], first_low[...], 1, 1).astype(BF)
        outs[1].start()
        split_cores(meta, dot(att_t[...], first_low[...]), keep, send, keep.shape[0], keep.shape[1])
        for out in outs:
            out.wait()


def weight_gradients(
    meta, tok_in, two_in, other_in, gq_in, gkv_in, sums_two, sums_one, g_bq, g_bv, g_b_in,
    keep_out, send_out,
    tok, gq_t, gkv_t, tok_t, keep, send, keep_last, send_last, sems, out_sems,
):
    _, size, width = tok.shape
    half_rows = size // 2
    ins = [
        pltpu.make_async_copy(source, target, sems.at[at])
        for at, (source, target) in enumerate(
            [
                (tok_in.at[0], tok.at[0]), (two_in, tok.at[1]), (gq_in, gq_t), (other_in.at[0], tok.at[2]),
                (gkv_in.at[0], gkv_t.at[0]), (gkv_in.at[1], gkv_t.at[1]), (gkv_in.at[2], gkv_t.at[2]),
            ]
        )
    ]
    for copy in ins:
        copy.start()
    groups, own_rows = keep.shape[1], keep.shape[2]

    def outs(section):
        slot = section % 2
        columns = pl.ds(section * width, width)
        return [
            pltpu.make_async_copy(keep.at[slot], keep_out.at[:, :, columns], out_sems.at[2 * slot]),
            pltpu.make_async_copy(send.at[slot], send_out.at[:, :, columns], out_sems.at[2 * slot + 1]),
        ]

    def finish(section, block):
        slot = section % 2
        if section >= 2:
            for copy in outs(section - 2):
                copy.wait()
        split_cores(meta, block, keep.at[slot], send.at[slot], groups, own_rows)
        for copy in outs(section):
            copy.start()

    def turn(at):
        tok_t[:, at * size : (at + 1) * size] = tok[at].T

    vectors = [sums_two[0:3, :], sums_one[0:3, :], g_bq[...], g_bv[...], jnp.zeros((120, width), F32)]
    vectors = jnp.concatenate(vectors, axis=0).T
    per_owner = g_b_in.shape[1] // (2 * groups)
    line = min(64, per_owner)
    bias_rows = []
    for at in range(2 * groups):
        lines = [
            jnp.concatenate(
                [
                    jnp.zeros((1, 64), F32),
                    g_b_in[:, at * per_owner + to : at * per_owner + to + line],
                    jnp.zeros((1, 64 - line), F32),
                ][: 2 + (line < 64)],
                axis=1,
            )
            for to in range(0, per_owner, line)
        ]
        bias_rows.append(jnp.concatenate(lines + [jnp.zeros((own_rows - len(lines), 128), F32)], axis=0))
    split_cores(meta, vectors + jnp.concatenate(bias_rows, axis=0), keep_last, send_last, groups, own_rows)
    last = [
        pltpu.make_async_copy(keep_last, keep_out.at[:, :, pl.ds(3 * width, 128)], out_sems.at[4]),
        pltpu.make_async_copy(send_last, send_out.at[:, :, pl.ds(3 * width, 128)], out_sems.at[5]),
    ]
    for copy in last:
        copy.start()
    for copy in ins[:3]:
        copy.wait()
    turn(0)
    turn(1)
    half = tok_t[:, pl.ds(pl.multiple_of(size + meta[SIDE] * half_rows, half_rows), half_rows)]
    blocks = [dot(tok_t[:, :size], gq_t[:, :size], 1, 1) + dot(half, gq_t[:, size:], 1, 1)]
    for copy in ins[3:]:
        copy.wait()
    turn(2)

    def pair_block(which):
        span = slice(which * width, (which + 1) * width)
        block = dot(tok_t[:, :size], gkv_t[0, span, :], 1, 1)
        block = block + dot(tok_t[:, size : 2 * size], gkv_t[1, span, :], 1, 1)
        return block + dot(tok_t[:, 2 * size :], gkv_t[2, span, :], 1, 1)

    blocks.append(pair_block(0))
    finish(0, blocks[0])
    blocks.append(pair_block(1))
    finish(1, blocks[1])
    finish(2, blocks[2])
    for copy in outs(1) + outs(2) + last:
        copy.wait()


def started(pairs, sems):
    copies = [pltpu.make_async_copy(source, target, sems.at[at]) for at, (source, target) in enumerate(pairs)]
    for copy in copies:
        copy.start()
    return copies


def tokens_sent(
    meta, w_in, gq_in, gkv_in, first_in, sent_out, two_out, w, gq_t, gkv_t, first, sent, two, sems, out_sems
):
    width = w.shape[0]
    size = two.shape[0]
    half_rows = size // 2
    late, early = pl.ds(width, 2 * width), pl.ds(0, width)
    half = pl.ds(size, half_rows)
    ins = started(
        [
            (gkv_in.at[2], gkv_t.at[1]), (w_in.at[:, late], w.at[:, late]), (gkv_in.at[1], gkv_t.at[0]),
            (gq_in.at[:, half], gq_t), (w_in.at[:, early], w.at[:, early]), (first_in.at[half], first),
        ],
        sems,
    )
    for copy in ins[:3]:
        copy.wait()
    sent[0] = dot(gkv_t[1], w[:, width:], 0, 1).astype(BF)
    outs = started([(sent.at[0], sent_out.at[0])], out_sems)
    for copy in ins[3:]:
        copy.wait()
    two[...] = dot(gkv_t[0], w[:, width:], 0, 1)
    span = pl.ds(pl.multiple_of(meta[SIDE] * half_rows, half_rows), half_rows)
    two[span, :] += dot(gq_t[...], w[:, :width], 0, 1) + first[...]
    sent[1] = two[...].astype(BF)
    for number, pair in enumerate([(sent.at[1], sent_out.at[1]), (two, two_out)]):
        copy = pltpu.make_async_copy(*pair, out_sems.at[1 + number])
        copy.start()
        outs.append(copy)
    for copy in outs:
        copy.wait()


def tokens_kept(
    meta, w_in, gq_in, gkv_in, first_in, came_in, two_in, grad_out, w, gq_t, gkv_t, own, came, two, grad, sems, out_sems
):
    width = w.shape[0]
    size = own.shape[0]
    late, early = pl.ds(width, 2 * width), pl.ds(0, width)
    ins = started(
        [
            (gkv_in.at[0], gkv_t), (w_in.at[:, late], w.at[:, late]), (gq_in.at[:, pl.ds(0, size)], gq_t),
            (w_in.at[:, early], w.at[:, early]), (came_in, came), (two_in, two), (first_in.at[pl.ds(0, size)], own),
        ],
        sems,
    )
    for copy in ins[:2]:
        copy.wait()
    total = dot(gkv_t[...], w[:, width:], 0, 1)
    for copy in ins[2:4]:
        copy.wait()
    total = total + dot(gq_t[...], w[:, :width], 0, 1)
    for copy in ins[4:6]:
        copy.wait()
    grad[1] = jnp.where(meta[SIDE] == 0, two[...] + came[1].astype(F32), 0.0).astype(BF)
    outs = started([(grad.at[1], grad_out.at[1])], out_sems)
    ins[6].wait()
    grad[0] = (total + own[...] + came[0].astype(F32)).astype(BF)
    out = pltpu.make_async_copy(grad.at[0], grad_out.at[0], out_sems.at[1])
    out.start()
    for copy in outs + [out]:
        copy.wait()


def flip(value, axis, bit):
    count = lax.axis_size(axis)
    return lax.ppermute(value, axis, [(at, at ^ bit) for at in range(count)])


def after(value, *others):
    return lax.optimization_barrier((value,) + others)[0]


CORE_SUM, QUAD, PAIR, CORE_TWO, HOP_TWO, JOIN = range(6)


def two_parts(stage, bits, meta, parts, targets):
    if stage == CORE_TWO:
        kept, pieces = parts[0], parts[1:]
        starts = [sum(piece.shape[2] for piece in pieces[:number]) for number in range(len(pieces))]

    first = 0
    for part in range(2):
        outs = targets if stage == JOIN else targets[2 * part : 2 * part + 2]
        bit, place = bits[part]
        mine = (meta[OWNER] >> bit) & 1
        columns = parts[2 * part].shape[2] if stage == JOIN else outs[0].shape[2]
        for flipped, out in enumerate(outs):
            which = 1 - mine if flipped else mine
            for to in range(out.shape[0]):
                index = (((to >> place) << 1) << place) | (to & ((1 << place) - 1))
                index = index + (which << place) if len(outs) > 1 else to
                if stage != CORE_TWO:
                    total = parts[2 * part][index] + parts[2 * part + 1][index]
                    span = slice(first, first + columns) if stage == JOIN else slice(0, columns)
                    out[to, :, span] = total.astype(BF)
                    continue
                for start, piece in zip(starts, pieces):
                    low, high = max(start, first), min(start + piece.shape[2], first + columns)
                    if low < high:
                        total = kept[index, :, low:high] + piece[index, :, low - start : high - start]
                        out[to, :, low - first : high - first] = total.astype(BF)
        first += columns


def combine_kernel(plan, meta, *refs):
    refs = list(refs)
    ins = [[refs.pop(0) for _ in range(count)] for *_, count, _ in plan]
    outs = [[refs.pop(0) for _ in range(count)] for *_, count in plan]
    for (stage, over_x, plane, bit, _, _), parts, targets in zip(plan, ins, outs):
        places = 2**plane
        if stage in (CORE_TWO, HOP_TWO, JOIN):
            two_parts(stage, bit, meta, parts, targets)
            continue
        if stage == CORE_SUM:
            kept, pieces = parts[0], parts[1:]
            (out,) = targets
            columns = kept.shape[2]
            starts = [sum(piece.shape[2] for piece in pieces[:number]) for number in range(len(pieces))]
            for at in range(kept.shape[0]):
                for number, piece in enumerate(pieces):
                    begin, end = starts[number], starts[number] + piece.shape[2]
                    if not over_x:
                        span = slice(begin, end)
                        total = kept[at, :, span].astype(F32) + piece[at].astype(F32)
                        out[at % places, at // places, :, span] = total.astype(BF)
                        continue
                    for side in range(2):
                        low = max(begin, side * columns // 2)
                        high = min(end, (side + 1) * columns // 2)
                        if low < high:
                            total = kept[at, :, low:high] + piece[at, :, low - begin : high - begin]
                            to = slice(low - side * columns // 2, high - side * columns // 2)
                            out[2 * (at % places) + side, at // places, :, to] = total.astype(BF)
            continue

        def total_at(index):
            if stage == QUAD:
                (came,) = parts
                total = came[0, index].astype(F32)
                for at in range(1, came.shape[0]):
                    total = total + came[at, index].astype(F32)
                return total
            kept, came = parts
            return kept[index] + came[index]

        if len(targets) == 1:
            targets[0][...] = total_at(0).astype(BF)
        else:
            mine = (meta[OWNER] >> bit) & 1
            for flipped, out in enumerate(targets):
                which = 1 - mine if flipped else mine
                for to in range(out.shape[0]):
                    out[to] = total_at(2 * to + which).astype(BF)


class Piece:
    def __init__(self, keep, sends, plane, over_x):
        self.over_x = over_x
        self.rows = keep.shape[1]
        self.columns = keep.shape[2] // 2 if over_x else keep.shape[2]
        bits = list(range(1, lax.axis_size("batch").bit_length() - 1))
        self.plane, self.bits = plane, bits[plane:]
        self.stage = CORE_SUM
        self.parts = [keep] + [flip(send, "batch", 1) for send in sends]

    def shapes(self):
        sds = lambda *lead: jax.ShapeDtypeStruct(lead + (self.rows, self.columns), BF)
        if self.stage == CORE_SUM:
            places = 2**self.plane
            return [sds(places * (1 + self.over_x), self.parts[0].shape[0] // places)]
        count = self.parts[0].shape[-3]
        return [sds(count // 2)] * 2 if count > 1 else [sds()]

    def taken(self, results):
        self.sending = results[-1]
        if self.stage == CORE_SUM:
            places = 2**self.plane
            starts = [
                high + core for high in range(0, lax.axis_size("batch"), 2 * places) for core in range(2)
            ]
            if self.over_x:
                groups = [[2 * (start + 2 * place) + side for place in range(places) for side in range(2)] for start in starts]
                came = lax.all_to_all(results[0], ("batch", "blk"), 0, 0, axis_index_groups=groups)
            else:
                groups = [[start + 2 * place for place in range(places)] for start in starts]
                came = lax.all_to_all(results[0], "batch", 0, 0, axis_index_groups=groups)
            self.parts = [came]
            self.stage = QUAD
        elif len(results) == 2:
            self.parts = [results[0], flip(results[1], "batch", 1 << self.bits.pop(0))]
            self.stage = PAIR
        else:
            self.parts = [results[0], flip(results[0], "blk", 1)]
            self.stage = None

    def finish(self, side):
        own, came = self.parts
        if not self.over_x:
            return own.astype(F32) + came.astype(F32)
        return jnp.concatenate([jnp.where(side == 0, own, came), jnp.where(side == 0, came, own)], axis=1).astype(F32)


class TwoPartPiece(Piece):
    def __init__(self, keep, sends, widths):
        self.over_x, self.plane = False, 2
        self.rows, self.columns, self.widths = keep.shape[1], keep.shape[2], widths
        self.all_bits = list(range(1, lax.axis_size("batch").bit_length() - 1))
        self.bits = self.all_bits[2:]
        self.stage = CORE_TWO
        self.parts = [keep] + [flip(send, "batch", 1) for send in sends]

    def shapes(self):
        sds = jax.ShapeDtypeStruct
        if self.stage in (CORE_TWO, HOP_TWO):
            count = self.parts[0].shape[0] // 2
            return [sds((count, self.rows, width), BF) for width in self.widths for _ in range(2)]
        count = self.parts[0].shape[0]
        if self.stage == JOIN:
            shape = (count // 2, self.rows, self.columns)
            return [sds(shape, BF)] * 2 if count > 1 else [sds((1,) + shape[1:], BF)]
        return super().shapes()

    def turn(self):
        first, second = self.all_bits[:2]
        if self.stage == CORE_TWO:
            return [(first, 0), (second, 1)]
        if self.stage == HOP_TWO:
            return [(second, 0), (first, 0)]
        return [(self.bits[0] if self.bits else 0, 0)] * 2

    def taken(self, results):
        if self.stage in (CORE_TWO, HOP_TWO):
            (bit_a, _), (bit_b, _) = self.turn()
            keep_a, send_a, keep_b, send_b = results
            self.sending = send_b
            self.parts = [keep_a, flip(send_a, "batch", 1 << bit_a), keep_b, flip(send_b, "batch", 1 << bit_b)]
            self.stage = HOP_TWO if self.stage == CORE_TWO else JOIN
        else:
            super().taken(results)


def take(meta, pieces, *order_after):
    operands, plan, shapes = [], [], []
    for piece in pieces:
        piece.parts = list(lax.optimization_barrier(tuple(piece.parts) + order_after)[: len(piece.parts)])
        made = piece.shapes()
        bit = piece.bits[0] if piece.bits else 0
        if piece.stage in (CORE_TWO, HOP_TWO, JOIN):
            bit = piece.turn()
        plan.append((piece.stage, piece.over_x, piece.plane, bit, len(piece.parts), len(made)))
        operands += piece.parts
        shapes += made
    vmem = pl.BlockSpec(memory_space=pltpu.VMEM)
    out = pl.pallas_call(
        functools.partial(combine_kernel, plan),
        in_specs=[pl.BlockSpec(memory_space=pltpu.SMEM)] + [vmem] * len(operands),
        out_specs=[vmem] * len(shapes),
        out_shape=shapes,
        compiler_params=params(28),
        cost_estimate=cost(1, 1),
        name="combine",
    )(meta, *operands)
    for piece, (*_, count) in zip(pieces, plan):
        piece.taken(out[:count])
        out = out[count:]
    return tuple(part for piece in pieces for part in piece.parts[:1] if piece.stage != QUAD)


def local(
    tokens, cotangent, counts, perms, key_mask, w_qkv, bias_q, bias_v, w_out, bias_out, gain_one, shift_one,
    w_in, bias_in, w_back, bias_back, gain_two, shift_two,
):
    _, _, size, width = tokens.shape
    heads = perms.shape[1]
    hidden = w_in.shape[1]
    half_rows = size // 2
    total = size + half_rows
    owners = lax.axis_size("batch")
    side = lax.axis_index("blk").astype(jnp.int32)
    owner = lax.axis_index("batch").astype(jnp.int32)
    whole = lambda *shape: once(shape, lambda *_: (0,) * len(shape))
    sds = jax.ShapeDtypeStruct
    anywhere = pl.BlockSpec(memory_space=pl.ANY)
    smem = pl.BlockSpec(memory_space=pltpu.SMEM)

    tok = tokens[0]
    came = flip(tok, "blk", 1)

    count = counts[0]
    lookup = jnp.where(count == 2, perms[0], perms[1])
    own = jnp.where(side == 0, lookup[:, 0], lookup[:, 1])
    two = jnp.where(count > 2, lookup[:, 2], 2)
    source = jnp.concatenate([own, two])
    place = jnp.where(source == 2, 1, jnp.where(source == side, 0, 2))
    live = jnp.stack([(side < count).astype(jnp.int32), (count > 2).astype(jnp.int32)])
    meta = jnp.concatenate([jnp.stack([side, owner & 1]), live, owner[None], place])
    vec = jnp.concatenate([bias_q, bias_v, bias_out, gain_one, shift_one, bias_back, gain_two, shift_two]).reshape(8, width)
    own_mask = key_mask[0]

    def grid_spec(grid, in_specs, out_specs, scratch=()):
        return pltpu.PrefetchScalarGridSpec(
            num_scalar_prefetch=1, grid=grid, in_specs=in_specs, out_specs=out_specs, scratch_shapes=list(scratch)
        )

    slot = lambda at: once((None, size, width), lambda *_: (at, 0, 0))
    all_rows = whole(total, width)
    vectors = whole(8, width)
    own_q, own_k, own_v, own_mb = pl.pallas_call(
        project_own,
        grid_spec=grid_spec(
            (3,),
            [slot(0), whole(1, size), pl.BlockSpec((width, width), lambda i, m: (0, i)), vectors],
            [whole(width, size), whole(size, width), whole(width, size), whole(size, 128)],
        ),
        out_shape=[sds((width, size), BF), sds((size, width), BF), sds((width, size), BF), sds((size, 128), F32)],
        compiler_params=params(60),
        cost_estimate=cost(1e9, 1),
        name="project_own",
    )(meta, tok, own_mask[0:1], w_qkv, vec)
    other_mask = flip(after(own_mask, own_mb), "blk", 1)
    masks = (own_mask, other_mask)
    cot = cotangent[0]
    cot_came = lax.ppermute(after(cot[1, half_rows:], came), "blk", [(0, 1)])

    each = 4
    span = each * width // heads
    some_q = pl.BlockSpec((span, total), lambda p, m: (p, 0))
    some_rows = pl.BlockSpec((3, size, span), lambda p, m: (0, 0, p))
    some_cols = pl.BlockSpec((3, span, size), lambda p, m: (0, p, 0))
    some_probs = pl.BlockSpec((each, size, total), lambda p, m: (p, 0, 0))
    some_inv = pl.BlockSpec((1, each, total), lambda p, m: (p, 0, 0))
    probs, att, att_t, inv, q_t, k, v_t, tok_two = pl.pallas_call(
        functools.partial(attention_forward, heads),
        grid_spec=grid_spec(
            (heads // each,),
            [whole(2, size), whole(2, size), vectors] + [anywhere] * 7,
            [some_probs, pl.BlockSpec((total, span), lambda p, m: (0, p)), some_q, some_inv] + [anywhere] * 4,
            [
                pltpu.VMEM((width, total), BF), pltpu.VMEM((3, size, width), BF), pltpu.VMEM((3, width, size), BF),
                pltpu.VMEM((3, size, 128), F32), pltpu.VMEM((width, 3 * width), BF), pltpu.VMEM((2 * size, width), BF),
                pltpu.SemaphoreType.DMA((9,)), pltpu.SemaphoreType.DMA((4,)),
            ],
        ),
        out_shape=[
            sds((heads, size, total), BF), sds((total, width), BF), sds((width, total), BF),
            sds((heads // each, each, total), F32), sds((width, total), BF), sds((3, size, width), BF), sds((3, width, size), BF),
            sds((size, width), BF),
        ],
        compiler_params=params(60),
        cost_estimate=cost(1e11, 1),
        name="attention_forward",
    )(meta, *masks, vec, tok, came, w_qkv, own_q, own_k, own_v, own_mb)

    chunk = 1024
    steps = hidden // chunk
    back_steps = 2
    half = owners // 2
    back_rows = hidden // owners
    back_half = pl.BlockSpec((half // back_steps, back_rows, width), lambda i, m: (jnp.maximum(i - steps, 0), 0, 0))
    flat = lambda dtype, columns=width: sds((total, columns), dtype)
    early = lambda i: jnp.minimum(i, steps - 1)
    side_rows = once((half_rows, width), lambda i, m: (m[SIDE], 0))
    slope, back_keep, back_send, sums_two, first, normed_low, mixed, mixed_two, g_second, back_low = pl.pallas_call(
        functools.partial(rows_forward, steps),
        grid_spec=grid_spec(
            (steps + back_steps,),
            [
                slot(0), side_rows, all_rows, slot(0), once((None, half_rows, width), lambda i, m: (1, 0, 0)),
                whole(half_rows, width), whole(width, width), vectors,
                pl.BlockSpec((width, chunk), lambda i, m: (0, early(i))),
                pl.BlockSpec((1, chunk), lambda i, m: (0, early(i))),
                pl.BlockSpec((chunk, width), lambda i, m: (early(i), 0)),
            ],
            [
                pl.BlockSpec((total, chunk), lambda i, m: (0, early(i))),
                back_half, back_half, whole(8, width),
            ]
            + [anywhere] * 6,
            [
                pltpu.VMEM((total, width), F32), pltpu.VMEM((total, width), BF), pltpu.VMEM((total, width), BF),
                pltpu.VMEM((total, width), F32), pltpu.VMEM((total, width), BF), pltpu.VMEM((total, hidden), BF),
                pltpu.SemaphoreType.DMA((6,)),
            ],
        ),
        out_shape=[
            flat(BF, hidden), sds((half, back_rows, width), BF), sds((half, back_rows, width), BF),
            sds((8, width), F32), flat(F32), flat(BF),
            sds((size, width), BF), sds((half_rows, width), BF), flat(F32), flat(BF),
        ],
        compiler_params=params(60),
        cost_estimate=cost(1e11, 1),
        name="rows_forward",
    )(
        meta, tok, tok_two, att, cot, cot, cot_came, w_out, vec, w_in, bias_in.reshape(1, hidden), w_back,
    )

    back = Piece(back_keep, [back_send], 2, True)
    mixed_came = lax.ppermute(mixed_two, "blk", [(1, 0)])
    take(meta, [back])
    mixed_came, back_low = lax.optimization_barrier((mixed_came, back_low, back.sending))[:2]

    own_rows = width // owners
    in_steps = hidden // width
    in_early = lambda i: jnp.minimum(i, in_steps - 1)
    in_half = pl.BlockSpec((half, own_rows, width), lambda i, m: (0, 0, i))
    in_keep, in_send, g_b_in, sums_one, g_first, do_t = pl.pallas_call(
        rows_backward,
        grid_spec=grid_spec(
            (in_steps + 1,),
            [
                all_rows, all_rows, pl.BlockSpec((total, width), lambda i, m: (0, in_early(i))),
                pl.BlockSpec((width, width), lambda i, m: (0, in_early(i))),
                pl.BlockSpec((width, width), lambda i, m: (in_early(i), 0)),
                vectors, anywhere, anywhere, anywhere, anywhere,
            ],
            [
                in_half, in_half,
                pl.BlockSpec((1, width), lambda i, m: (0, in_early(i))), whole(8, width), anywhere, anywhere,
            ],
            [
                pltpu.VMEM((total, width), F32), pltpu.VMEM((total, width), F32), pltpu.VMEM((total, width), F32),
                pltpu.VMEM((width, total), BF), pltpu.VMEM((total, width), F32), pltpu.VMEM((total, width), BF),
                pltpu.VMEM((width, total), BF), pltpu.VMEM((width, width), BF), pltpu.SemaphoreType.DMA((4,)),
                pltpu.SemaphoreType.DMA((2,)),
            ],
        ),
        out_shape=[
            sds((half, own_rows, hidden + width), BF), sds((half, own_rows, hidden + width), BF), sds((1, hidden), F32), sds((8, width), F32), flat(F32),
            sds((width, total), BF),
        ],
        compiler_params=params(60),
        cost_estimate=cost(1e11, 1),
        name="rows_backward",
    )(meta, back_low, normed_low, slope, w_in, w_back, vec, first, g_second, att_t, w_out)
    in_sends = [in_send]
    inner = Piece(in_keep, in_sends, 2, True)
    take(meta, [inner], do_t)
    do_t = after(do_t, inner.sending)
    gq_shapes = [
        sds((width, total), BF), sds((3, 2, width, size), BF), sds((1, width), F32), sds((1, width), F32),
    ]

    gq_t, gkv_t, g_bq, g_bv = pl.pallas_call(
        functools.partial(attention_backward, heads),
        grid_spec=grid_spec(
            (heads // each,),
            [some_probs, some_rows, some_cols, some_q, some_q, some_q, some_inv],
            [some_q, pl.BlockSpec((3, 2, span, size), lambda p, m: (0, 0, p, 0))]
            + [pl.BlockSpec((1, span), lambda p, m: (0, p))] * 2,
            [
                pltpu.VMEM((3, span, size), F32), pltpu.VMEM((3, span, size), F32), pltpu.VMEM((span, total), F32),
                pltpu.VMEM((3, span, size), BF), pltpu.VMEM((3, size, span), BF),
            ],
        ),
        out_shape=gq_shapes,
        compiler_params=params(60),
        cost_estimate=cost(1e11, 1),
        name="attention_backward",
    )(meta, probs, k, v_t, q_t, do_t, att_t, inv)
    gkv_t = gkv_t.reshape(3, 2 * width, size)

    columns = 3 * width + 128
    vmem = pl.BlockSpec(memory_space=pltpu.VMEM)
    run_weights = pl.pallas_call(
        weight_gradients,
        in_specs=[pl.BlockSpec(memory_space=pltpu.SMEM)] + [anywhere] * 5 + [vmem] * 5,
        out_specs=[anywhere] * 2,
        scratch_shapes=[
            pltpu.VMEM((3, size, width), BF), pltpu.VMEM((width, total), BF), pltpu.VMEM((3, 2 * width, size), BF),
            pltpu.VMEM((width, 3 * size), BF),
            pltpu.VMEM((2, half, own_rows, width), BF), pltpu.VMEM((2, half, own_rows, width), BF),
            pltpu.VMEM((half, own_rows, 128), BF), pltpu.VMEM((half, own_rows, 128), BF),
            pltpu.SemaphoreType.DMA((7,)), pltpu.SemaphoreType.DMA((6,)),
        ],
        out_shape=[sds((half, own_rows, columns), BF)] * 2,
        compiler_params=params(60),
        cost_estimate=cost(1e9, 1),
        name="weight_gradients",
    )
    last_keep, last_send = run_weights(
        meta, tok, tok_two, came, gq_t, gkv_t, sums_two, sums_one, g_bq, g_bv, g_b_in
    )
    last = TwoPartPiece(last_keep, [last_send], [1408, columns - 1408])
    own_size, half_size = (width, size), (width, half_rows)
    sent, two_own = pl.pallas_call(
        tokens_sent,
        in_specs=[smem] + [anywhere] * 4,
        out_specs=[anywhere] * 2,
        out_shape=[sds((2, size, width), BF), sds((size, width), F32)],
        scratch_shapes=[
            pltpu.VMEM((width, 3 * width), BF), pltpu.VMEM(half_size, BF), pltpu.VMEM((2, 2 * width, size), BF),
            pltpu.VMEM((half_rows, width), F32), pltpu.VMEM((2, size, width), BF), pltpu.VMEM((size, width), F32),
            pltpu.SemaphoreType.DMA((6,)), pltpu.SemaphoreType.DMA((3,)),
        ],
        compiler_params=params(60),
        cost_estimate=cost(11.5e9, 1),
        name="tokens_sent",
    )(meta, w_qkv, after(gq_t, last_keep), gkv_t, g_first)
    came_grad = flip(sent, "blk", 1)

    take(meta, [last], sent)
    take(meta, [inner, back], last.sending)
    take(meta, [last], inner.sending)
    take(meta, [last, inner, back], last.sending)
    tokens_grad = pl.pallas_call(
        tokens_kept,
        in_specs=[smem] + [anywhere] * 6,
        out_specs=anywhere,
        out_shape=sds((2, size, width), BF),
        scratch_shapes=[
            pltpu.VMEM((width, 3 * width), BF), pltpu.VMEM(own_size, BF), pltpu.VMEM((2 * width, size), BF),
            pltpu.VMEM((size, width), F32), pltpu.VMEM((2, size, width), BF), pltpu.VMEM((size, width), F32),
            pltpu.VMEM((2, size, width), BF), pltpu.SemaphoreType.DMA((7,)), pltpu.SemaphoreType.DMA((2,)),
        ],
        compiler_params=params(60),
        cost_estimate=cost(1e11, 1),
        name="tokens_kept",
    )(meta, w_qkv, after(gq_t, last.sending), gkv_t, g_first, came_grad, two_own)
    take(meta, [last], tokens_grad, back.parts[1], inner.parts[1])
    for piece in (last, inner, back):
        while piece.stage is not None:
            take(meta, [piece])

    out_back = back.finish(side)
    out_in = inner.finish(side)
    own_last, came_last = last.parts
    both = lambda columns: own_last[:, columns].astype(F32) + came_last[:, columns].astype(F32)
    out_qkv, out_vectors = both(slice(0, 3 * width)), both(slice(3 * width, columns))

    mixed_other = jnp.where(side == 0, jnp.concatenate([mixed_two, mixed_came]), jnp.zeros((), BF))
    mixed_all = jnp.stack([mixed, mixed_other])[None]
    pick = lambda at: out_vectors[:, at]
    line = min(64, back_rows)
    return (
        mixed_all, tokens_grad[None],
        out_qkv, pick(6), pick(7), out_in[:, hidden:], pick(5), pick(3), pick(4),
        out_in[:, :hidden], out_vectors[: back_rows // line, 64 : 64 + line].reshape(-1), out_back, pick(2), pick(0),
        pick(1),
    )


def solution(mesh):
    split = P("batch", None, "blk", None)
    in_specs = (split, split, P("batch"), P(), P("batch", None, "blk")) + (P(),) * 13
    matrix, vector = P("batch", None), P("batch")
    out_specs = (
        split, split, matrix, vector, vector, matrix, vector, vector, vector, matrix, vector, matrix, vector, vector,
        vector,
    )
    return jax.shard_map(local, mesh=mesh, in_specs=in_specs, out_specs=out_specs, check_vma=False)
```
